32 devices in a mesh: dp: 16 (over z, x, core), mp: 2 (over y).
Axes of the slice: x: 2, y: 2, z: 4, core: 2. Of those that a mesh axis runs over, the one named last changes fastest.
Arguments:
- tokens: bfloat16 [8192, 768], P('dp'), may hold values from -6 to 6
- segment_ids: int32 [16, 512], P('dp'), may hold values from 0 to 5, never falling along the last dimension, each value on 1 to 256 neighbouring positions
- pad_flags: int32 [16, 512], P('dp'), may hold values 0 or 1
- query_weight: bfloat16 [768, 768], P(None, 'mp'), may hold values from -0.21875 to 0.21875
- query_bias: bfloat16 [768], P('mp'), may hold values from -1.5 to 1.5
- key_weight: bfloat16 [768, 768], P(None, 'mp'), may hold values from -0.21875 to 0.21875
- value_weight: bfloat16 [768, 768], P(None, 'mp'), may hold values from -0.21875 to 0.21875
- value_bias: bfloat16 [768], P('mp'), may hold values from -1.5 to 1.5
- output_weight: bfloat16 [768, 768], P('mp'), may hold values from -0.625 to 0.625
- output_bias: bfloat16 [768], replicated, may hold values from -1.5 to 1.5
- first_gain: bfloat16 [768], replicated, may hold values from 0.5 to 1.5
- first_shift: bfloat16 [768], replicated, may hold values from -1.5 to 1.5
- up_weight: bfloat16 [768, 3072], P(None, 'mp'), may hold values from -0.21875 to 0.21875
- up_bias: bfloat16 [3072], P('mp'), may hold values from -1.5 to 1.5
- down_weight: bfloat16 [3072, 768], P('mp'), may hold values from -0.21875 to 0.21875
- down_bias: bfloat16 [768], replicated, may hold values from -1.5 to 1.5
- second_gain: bfloat16 [768], replicated, may hold values from 0.5 to 1.5
- second_shift: bfloat16 [768], replicated, may hold values from -1.5 to 1.5
- term_weight: bfloat16 [768], replicated, may hold values from -0.21875 to 0.21875
- term_bias: bfloat16 [1], replicated, may hold values from -2.5 to 2.5
- hidden_cot: float32 [8192, 768], P('dp'), may hold values from -18 to 18
- term_cot: float32 [8192], P('dp'), may hold values from -6 to 6
Outputs:
- hidden: bfloat16 [8192, 768], P('dp')
- term_weights: float32 [8192], P('dp')
- tokens_grad: float32 [8192, 768], P('dp')
- queryweight_grad: float32 [768, 768], P(None, 'mp')
- querybias_grad: float32 [768], P('mp')
- keyweight_grad: float32 [768, 768], P(None, 'mp')
- valueweight_grad: float32 [768, 768], P(None, 'mp')
- valuebias_grad: float32 [768], P('mp')
- outputweight_grad: float32 [768, 768], P('mp')
- outputbias_grad: float32 [768], replicated
- firstgain_grad: float32 [768], replicated
- firstshift_grad: float32 [768], replicated
- upweight_grad: float32 [768, 3072], P(None, 'mp')
- upbias_grad: float32 [3072], P('mp')
- downweight_grad: float32 [3072, 768], P('mp')
- downbias_grad: float32 [768], replicated
- secondgain_grad: float32 [768], replicated
- secondshift_grad: float32 [768], replicated
- termweight_grad: float32 [768], replicated
- termbias_grad: float32 [1], replicated
The draws below stay inside these ranges and needn't reach their ends.
All inputs are finite; a program needn't handle non-finite values. No bound on the sum of `pad_flags` on one device may be relied on, other than what follows from the above.
Results may differ from the reference program's by a relative error of at most 0.015.
Values sent between devices are 32-bit elements; how exact they have to be, the bound alone decides.
A program may use at most 128 MiB of HBM per device.

```python
import math
import jax
import jax.numpy as jnp
import numpy as np
from jax import lax

D = 768
HEADS = 12
HEAD_DIM = 64
FF = 3072
SEQ = 512
ROWS = 16
TOKENS = 8192


def draw_hidden_cot(key, part):
    ramp = jnp.arange(TOKENS, dtype=jnp.float32)[:, None] / TOKENS
    base = jnp.clip(jax.random.normal(key, (TOKENS, D), jnp.float32), -6.0, 6.0)
    return base * jnp.exp(1.09 * ramp)


def with_ends(entries, stream_key, smallest, largest):
    extent = entries.shape
    spot = [jax.random.randint(jax.random.fold_in(stream_key, axis), (), 0, extent[axis]) for axis in range(len(extent))]
    entries = entries.at[tuple(spot)].set(smallest)
    longest = extent.index(max(extent))
    spot[longest] = (spot[longest] + 1) % extent[longest]
    return entries.at[tuple(spot)].set(largest)


def steps_of(rng, shape, split, low, largest):
    level, own = 1.0, jax.random.fold_in(rng, 6)
    for dim, shards_of in split:
        steps = jnp.exp(jax.random.uniform(jax.random.fold_in(own, dim), (shards_of,), jnp.float32, low / len(split), largest / len(split)))
        level = level * jnp.repeat(steps, shape[dim] // shards_of).reshape([-1 if axis == dim else 1 for axis in range(len(shape))])
    return level


def length_profile(amount, total, bound, lean):
    weights = [(1 << 20) // math.isqrt(rank ** lean) + 1 for rank in range(2, amount + 1)]
    surplus, given = total - bound - (amount - 1), [1] * (amount - 1)
    while surplus > 0:
        free = [i for i in range(amount - 1) if given[i] < bound]
        whole, left = sum([weights[i] for i in free]), surplus
        for i in free:
            more = min(bound - given[i], max(1, left * weights[i] // whole), surplus)
            given[i] = given[i] + more
            surplus = surplus - more
    return np.array([bound] + given)


def ragged_sizes(key, amount, total, bound, skew):
    if amount == 2:
        one = jax.random.randint(key, (), max(1, total - bound), min(bound, total - 1) + 1)
        return jnp.stack([one, total - one])
    lengths = jnp.asarray(length_profile(amount, total, bound, skew), jnp.int32)
    couples = (amount - 1) // 2
    donor, sink = lengths[1:1 + 2 * couples:2], lengths[2:2 + 2 * couples:2]
    margin = jnp.minimum(donor - 1, bound - sink)
    passed = jax.random.randint(jax.random.fold_in(key, 1), (couples,), 0, 1 << 20) % (margin + 1)
    lengths = lengths.at[1:1 + 2 * couples:2].set(donor - passed).at[2:2 + 2 * couples:2].set(sink + passed)
    return lengths[jax.random.permutation(jax.random.fold_in(key, 2), amount)]


def centred(key, extent, scale, most, split=(), held_as=jnp.bfloat16):
    entries = jax.random.normal(key, extent, jnp.float32) * scale
    if len(split) > 0:
        entries = steps_of(key, extent, split, -0.22, 0.18) * entries
    return jnp.clip(entries, min=-most, max=most).astype(held_as)


def setup_inputs(seed: int = 0) -> dict:
    key_list = jax.random.split(jax.random.key(seed), 23)
    tokens = centred(key_list[0], (TOKENS, D), 1.0, 6.0, ((0, 16),))
    segment_ids = jax.vmap(lambda own: jnp.searchsorted(jnp.cumsum(ragged_sizes(own, 6, SEQ, SEQ // 2, 0)), jnp.arange(SEQ), side="right"))(jax.random.split(key_list[1], ROWS)).reshape((ROWS, SEQ)).astype(jnp.int32)
    pad_flags = with_ends((jax.random.randint(key_list[2], (ROWS, SEQ), 0, 8) < 1).astype(jnp.int32), jax.random.fold_in(key_list[2], 1), 0, 1)
    query_weight = centred(key_list[3], (D, D), D ** -0.5, 0.21875, ((1, 2),))
    query_bias = centred(key_list[4], (D,), 0.3, 1.5, ((0, 2),))
    key_weight = centred(key_list[5], (D, D), D ** -0.5, 0.21875, ((1, 2),))
    value_weight = centred(key_list[6], (D, D), D ** -0.5, 0.21875, ((1, 2),))
    value_bias = centred(key_list[7], (D,), 0.3, 1.5, ((0, 2),))
    output_weight = centred(key_list[8], (D, D), (D // 8) ** -0.5, 0.625, ((0, 2),))
    output_bias = centred(key_list[9], (D,), 0.3, 1.5)
    first_gain = jnp.clip(1.0 + 0.1 * jax.random.normal(key_list[10], (D,), jnp.float32), 0.5, 1.5).astype(jnp.bfloat16)
    first_shift = centred(key_list[11], (D,), 0.3, 1.5)
    up_weight = centred(key_list[12], (D, FF), D ** -0.5, 0.21875, ((1, 2),))
    up_bias = centred(key_list[13], (FF,), 0.3, 1.5, ((0, 2),))
    down_weight = centred(key_list[14], (FF, D), (FF // 4) ** -0.5, 0.21875, ((0, 2),))
    down_bias = centred(key_list[15], (D,), 0.3, 1.5)
    second_gain = jnp.clip(1.0 + 0.1 * jax.random.normal(key_list[16], (D,), jnp.float32), 0.5, 1.5).astype(jnp.bfloat16)
    second_shift = centred(key_list[17], (D,), 0.3, 1.5)
    term_weight = centred(key_list[18], (D,), D ** -0.5, 0.21875)
    term_bias = centred(key_list[19], (1,), 0.5, 2.5)
    hidden_cot = draw_hidden_cot(jax.random.fold_in(key_list[22], 71), 0)
    term_cot = centred(key_list[21], (TOKENS,), 1.0, 6.0, ((0, 16),), jnp.float32)
    return dict(tokens=tokens, segment_ids=segment_ids, pad_flags=pad_flags, query_weight=query_weight, query_bias=query_bias, key_weight=key_weight, value_weight=value_weight, value_bias=value_bias, output_weight=output_weight, output_bias=output_bias, first_gain=first_gain, first_shift=first_shift, up_weight=up_weight, up_bias=up_bias, down_weight=down_weight, down_bias=down_bias, second_gain=second_gain, second_shift=second_shift, term_weight=term_weight, term_bias=term_bias, hidden_cot=hidden_cot, term_cot=term_cot)


EPS = 1e-06

@jax.custom_vjp
def low(v):
    return lax.optimization_barrier(v.astype(jnp.bfloat16)).astype(jnp.float32)

@jax.custom_vjp
def low_back(v):
    return v

def low_keep(v):
    return (low(v), None)

def low_pass(kept, grad):
    return (grad,)

def back_keep(v):
    return (v, None)

def back_low(kept, grad):
    return (low(grad),)
low.defvjp(low_keep, low_pass)
low_back.defvjp(back_keep, back_low)

def matmul(left, right):
    return jnp.dot(left, right, precision=lax.Precision.HIGHEST)

def layer_norm(resid, gain, shift):
    center = resid - lax.optimization_barrier(jnp.mean(resid, axis=-1, keepdims=True))
    spread = lax.optimization_barrier(jnp.mean(center * center, axis=-1, keepdims=True))
    return center * lax.rsqrt(spread + EPS) * gain + shift

def attend_row(items):
    queries, key_rows, values, segment, padding = items
    length = segment.shape[0]
    same = segment[:, None] == segment[None, :]
    diagonal = lax.broadcasted_iota(jnp.int32, (length, length), 0) == lax.broadcasted_iota(jnp.int32, (length, length), 1)
    allowed = same & ((padding[None, :] == 0) | diagonal)
    scores = low_back(jnp.einsum('qhd,khd->hqk', queries, key_rows, precision=lax.Precision.HIGHEST) * HEAD_DIM ** (-0.5))
    scores = jnp.where(allowed[None], scores, -1000000000.0)
    maxima = lax.optimization_barrier(jnp.max(scores, axis=-1, keepdims=True))
    expo = jnp.exp(scores - maxima)
    probs = expo / lax.optimization_barrier(jnp.sum(expo, axis=-1, keepdims=True))
    return jnp.einsum('hqk,khd->qhd', low(probs), values, precision=lax.Precision.HIGHEST)

def forward(params, inputs, segment, padding):
    query_weight, query_bias, key_weight, value_weight, value_bias, output_weight, output_bias, first_gain, first_shift, up_weight, up_bias, down_weight, down_bias, second_gain, second_shift, term_weight, term_bias = params
    count = segment.shape[0]
    queries = low_back(low(matmul(inputs, query_weight) + query_bias)).reshape(count, SEQ, HEADS, HEAD_DIM)
    key_rows = low_back(low(matmul(inputs, key_weight))).reshape(count, SEQ, HEADS, HEAD_DIM)
    values = low_back(low(matmul(inputs, value_weight) + value_bias)).reshape(count, SEQ, HEADS, HEAD_DIM)
    context = lax.map(jax.checkpoint(attend_row), (queries, key_rows, values, segment, padding))
    context = low_back(low(context.reshape(count * SEQ, D)))
    attn = low_back(matmul(context, output_weight) + output_bias)
    first = layer_norm(inputs + attn, first_gain, first_shift)
    upper = low_back(matmul(low(first), up_weight) + up_bias)
    active = low(jax.nn.gelu(upper, approximate=False))
    branch = low_back(matmul(active, down_weight) + down_bias)
    second = layer_norm(first + branch, second_gain, second_shift)
    keep = 1.0 - padding.reshape(count * SEQ).astype(jnp.float32)
    term = jax.nn.softplus(lax.optimization_barrier(jnp.sum(second * term_weight, axis=-1)) + term_bias[0]) * keep
    return (second, term)

def reference(tokens, segment_ids, pad_flags, query_weight, query_bias, key_weight, value_weight, value_bias, output_weight, output_bias, first_gain, first_shift, up_weight, up_bias, down_weight, down_bias, second_gain, second_shift, term_weight, term_bias, hidden_cot, term_cot):
    params = tuple((weight.astype(jnp.float32) for weight in (query_weight, query_bias, key_weight, value_weight, value_bias, output_weight, output_bias, first_gain, first_shift, up_weight, up_bias, down_weight, down_bias, second_gain, second_shift, term_weight, term_bias)))
    per_group = math.gcd(ROWS, max(1, 4096 // SEQ))
    groups = ROWS // per_group
    inputs = tokens.astype(jnp.float32).reshape(groups, per_group * SEQ, D)
    segment = segment_ids.reshape(groups, per_group, SEQ)
    padding = pad_flags.reshape(groups, per_group, SEQ)
    cot_rows = hidden_cot.astype(jnp.float32).reshape(groups, per_group * SEQ, D)
    cot_terms = term_cot.astype(jnp.float32).reshape(groups, per_group * SEQ)

    def one_group(carry, items):
        group_in, group_seg, group_pad, group_cot, group_tcot = items

        def local_forward(weights, values_in):
            return forward(weights, values_in, group_seg, group_pad)
        (second, term), backward = jax.vjp(local_forward, params, group_in)
        weight_grads, input_grad = backward((group_cot, group_tcot))
        carry = jax.tree.map(lambda total, extra: total + extra, carry, weight_grads)
        return (carry, (second, term, input_grad))
    zeros = tuple((jnp.zeros_like(weight) for weight in params))
    totals, (second, term, input_grad) = lax.scan(one_group, zeros, (inputs, segment, padding, cot_rows, cot_terms))
    return (second.reshape(TOKENS, D).astype(jnp.bfloat16), term.reshape(TOKENS), input_grad.reshape(TOKENS, D), totals[0], totals[1], totals[2], totals[3], totals[4], totals[5], totals[6], totals[7], totals[8], totals[9], totals[10], totals[11], totals[12], totals[13], totals[14], totals[15], totals[16])
```

```python
from functools import partial

import jax
import jax.numpy as jnp
from jax import lax
from jax.experimental import pallas as pl
from jax.experimental.pallas import tpu as pltpu
from jax.sharding import PartitionSpec as P

HEAD_DIM = 64
EPS = 1e-06
GROUP = 16
RING = 8
BATCHES = 6
MESH = pl.DeviceIdType.MESH
bf16, f32 = jnp.bfloat16, jnp.float32

V_QV, V_OB, V_G1, V_S1, V_DB, V_G2, V_S2, V_TW, V_TB = range(9)
G_QV, G_OB, G_G1, G_S1, G_UB0, G_UB1, G_DB, G_G2, G_S2, G_TW, G_TB = range(11)


def nn(a, b):
    return jnp.dot(a, b, preferred_element_type=f32)


def nt(a, b):
    return lax.dot_general(a, b, (((1,), (1,)), ((), ())), preferred_element_type=f32)


def tn(a, b):
    return lax.dot_general(a, b, (((0,), (0,)), ((), ())), preferred_element_type=f32)


def colsum(v):
    return jnp.sum(v, axis=0, keepdims=True)


def rowmean(v):
    return jnp.mean(v, axis=-1, keepdims=True)


def kernel(
    tokens, seg, pad, tcot, vec, ubv, wq, wk, wv, wo, wu, wd, hcot,
    o_hid, o_term, o_tok, o_wq, o_wk, o_wv, o_wo, o_wu, o_wd, o_sm,
    tok_v, wq_v, wk_v, wv_v, wo_v, woo_v, wu_v, wd_v, hc,
    kn, vn, kT, vT, qz, qTz, pm, ctxT, xh, rs, fl, gp, act, bs, br, fr, db, du,
    dcz, dcTz, dsb, dqT, dq, dk, dv, hid, col, trm, sm, smr, G, S, R,
    ld_sem, out_sem, y_s, y_r, wx_s, wx_r, ws_s, ws_r, sm_s, sm_r,
    sib_s, sib_r, rs_s, rs_r, ag_s, ag_r, fw_s, fw_r, free_sib, free_ring,
):
    T, D = tokens.shape
    L, F = wq.shape[1], wu.shape[1]
    NP = L // 128
    CH, PC, FB = T // 2, T // 4, 512
    NPC = T // PC
    SUB = G.shape[0] // BATCHES
    HALF, CK = SUB // 2, SUB // 2 // RING

    me, mp = lax.axis_index("dp"), lax.axis_index("mp")
    base, rank = me // GROUP * GROUP, me % GROUP
    core, chip = rank % 2, rank // 2
    x, z = chip % 2, chip // 2
    pos = jnp.where(x == 0, z, RING - 1 - z)
    vp = jnp.where(core == 0, pos, (RING - pos) % RING)
    vps = (RING - vp) % RING

    def at_vp(v):
        p = jnp.where(core == 0, v, (RING - v) % RING)
        c = jnp.where(p < RING // 2, 2 * p, 2 * (RING - 1 - p) + 1)
        return (base + 2 * c + core, mp)

    def at_xz(ax, az):
        return (base + 2 * (2 * az + ax) + core, mp)

    YN = (me, 1 - mp)
    SIB = (base + 2 * chip + 1 - core, mp)
    NXT, PRV = at_vp((vp + 1) % RING), at_vp((vp + RING - 1) % RING)
    XN = at_xz(1 - x, z)
    Z1 = at_xz(x, z // 2 * 2 + 1 - z % 2)
    Z2 = at_xz(x, (z + 2) % 4)

    def rc(src, dst, ss, rr, dev):
        return pltpu.make_async_remote_copy(
            src_ref=src, dst_ref=dst, send_sem=ss, recv_sem=rr, device_id=dev, device_id_type=MESH
        )

    pairs = [
        (tokens, tok_v), (wq, wq_v), (wk, wk_v), (wv, wv_v), (wo, wo_v), (wu, wu_v), (wd, wd_v), (hcot, hc),
    ]
    loads = [pltpu.make_async_copy(a, b, ld_sem.at[i]) for i, (a, b) in enumerate(pairs)]
    for c in loads:
        c.start()
    L_TOK, L_WQ, L_WK, L_WV, L_WO, L_WU, L_WD, L_HC = loads

    peers = (YN, SIB, NXT, PRV, XN, Z1, Z2)
    bar = pltpu.get_barrier_semaphore()
    for d in peers:
        pl.semaphore_signal(bar, inc=1, device_id=d, device_id_type=MESH)
    pl.semaphore_wait(bar, len(peers))

    r_first = 1 * F
    r_wor = r_first + T
    r_wos = r_wor + L
    r_bias = 2 * F
    r_cs = r_bias + T
    r_cr = r_cs + L
    SH = L // 4

    L_WO.wait()
    share = pl.multiple_of((2 * x + core) * SH, SH)
    share_x = pl.multiple_of((2 * (1 - x) + core) * SH, SH)
    share_s = pl.multiple_of((2 * x + 1 - core) * SH, SH)
    share_sx = pl.multiple_of((2 * (1 - x) + 1 - core) * SH, SH)
    G[r_wos : r_wos + SH, :] = wo_v[pl.ds(share, SH), :].astype(f32)

    def wor(s):
        return G.at[pl.ds(pl.multiple_of(r_wor + s, 32), SH)]

    wo_y = rc(G.at[pl.ds(r_wos, SH)], wor(share), y_s.at[0], y_r.at[0], YN)
    wo_y.start()
    wo_x = rc(wor(share), wor(share), wx_s.at[0], wx_r.at[0], XN)
    wo_x_in = rc(wor(share_x), wor(share_x), wx_s.at[0], wx_r.at[0], XN)
    wo_f = [
        rc(wor(share), wor(share), ws_s.at[0], ws_r.at[0], SIB),
        rc(wor(share_x), wor(share_x), ws_s.at[1], ws_r.at[1], SIB),
    ]
    wo_f_in = [
        rc(wor(share_s), wor(share_s), ws_s.at[0], ws_r.at[0], SIB),
        rc(wor(share_sx), wor(share_sx), ws_s.at[1], ws_r.at[1], SIB),
    ]

    L_TOK.wait()
    L_WQ.wait()
    lane = lax.broadcasted_iota(jnp.int32, (T, L), 1)
    odd = (lane // HEAD_DIM) % 2
    qv = (nn(tok_v[...], wq_v[...]) + vec[V_QV : V_QV + 1, 0:L]).astype(bf16).astype(f32) * (HEAD_DIM**-0.5)
    for par in range(2):
        one = jnp.where(odd == par, qv, 0.0).astype(bf16)
        qz[par * T : (par + 1) * T, :] = one
        qTz[par * L : (par + 1) * L, :] = one.T
    L_WK.wait()
    kv = nn(tok_v[...], wk_v[...]).astype(bf16)
    kn[...] = kv
    kT[...] = kv.T
    L_WV.wait()
    vv = (nn(tok_v[...], wv_v[...]) + vec[V_QV : V_QV + 1, L : 2 * L]).astype(bf16)
    vn[...] = vv
    vT[...] = vv.T

    segf, padf = seg[...].astype(f32), pad[...].astype(f32)
    rows8 = jnp.concatenate([segf, padf, tcot[...], jnp.zeros((5, T), f32)], axis=0)
    col[...] = rows8.T
    for qc in range(2):
        ki = lax.broadcasted_iota(jnp.int32, (T, CH), 0)
        qi = lax.broadcasted_iota(jnp.int32, (T, CH), 1) + qc * CH
        same = col[:, 0:1] == segf[:, qc * CH : (qc + 1) * CH]
        allowed = same & ((col[:, 1:2] == 0.0) | (ki == qi))
        G[r_bias : r_bias + T, qc * CH : (qc + 1) * CH] = jnp.where(allowed, 0.0, -1e9)

    def ctx_copy(qc):
        cols = pl.ds(qc * CH, CH)
        return rc(
            G.at[pl.ds(r_cs, L), cols], G.at[pl.ds(r_cr, L), cols], y_s.at[1 + qc], y_r.at[1 + qc], YN
        )

    def attend(qc):
        cols = pl.ds(qc * CH, CH)

        def body(hp, _):
            blk = pl.ds(pl.multiple_of(hp * 128, 128), 128)
            for par in range(2):
                qrows = pl.ds(pl.multiple_of(par * L + hp * 128, 128), 128)
                head = pl.multiple_of(hp * 128 + par * HEAD_DIM, HEAD_DIM)
                s = nn(kn[:, blk], qTz[qrows, cols]) + G[r_bias : r_bias + T, cols]
                e = jnp.exp(s - jnp.max(s, axis=0, keepdims=True))
                p = (e * (1.0 / colsum(e))).astype(bf16)
                pm[hp, :, pl.ds(par * T + qc * CH, CH)] = p
                c = nn(vT[pl.ds(head, HEAD_DIM), :], p).astype(bf16)
                ctxT[pl.ds(head, HEAD_DIM), cols] = c
                G[pl.ds(pl.multiple_of(r_cs + head, HEAD_DIM), HEAD_DIM), cols] = c.astype(f32)
            return 0

        lax.fori_loop(0, NP, body, 0)

    attend(0)
    ctx_copy(0).start()
    wo_y.wait_recv()
    wo_x.start()
    wo_f[0].start()
    attend(1)
    ctx_copy(1).start()
    wo_x_in.wait_recv()
    wo_f[1].start()

    def attn_ln(qc):
        c0 = qc * CH
        cols = pl.ds(c0, CH)
        ctx_copy(qc).wait_recv()
        other = G[r_cr : r_cr + L, cols].astype(bf16)
        bs[c0 : c0 + CH, :] = tn(ctxT[:, cols], wo_v[...]) + tn(other, woo_v[...])

        def body(i, _):
            rows = pl.ds(pl.multiple_of(c0 + i * PC, PC), PC)
            res = tok_v[rows, :].astype(f32) + bs[rows, :] + vec[V_OB : V_OB + 1, :]
            cen = res - rowmean(res)
            rstd = lax.rsqrt(rowmean(cen * cen) + EPS)
            xv = cen * rstd
            xh[rows, :] = xv
            rs[rows, :] = jnp.broadcast_to(rstd, (PC, 128))
            first = xv * vec[V_G1 : V_G1 + 1, :] + vec[V_S1 : V_S1 + 1, :]
            G[pl.ds(pl.multiple_of(r_first + c0 + i * PC, PC), PC), :] = first
            fl[rows, :] = first.astype(bf16)
            return 0

        lax.fori_loop(0, CH // PC, body, 0)

    def ffn(qc):
        rows = pl.ds(qc * CH, CH)
        bs[rows, :] = jnp.zeros((CH, D), f32)

        def body(fb, _):
            cols = pl.ds(pl.multiple_of(fb * FB, FB), FB)
            u = nn(fl[rows, :], wu_v[:, cols]) + ubv[:, cols]
            ph = 0.5 + 0.5 * lax.erf(u * 0.7071067811865476)
            a = (u * ph).astype(bf16)
            act[rows, cols] = a
            gp[rows, cols] = (ph + u * (jnp.exp(-0.5 * u * u) * 0.3989422804014327)).astype(bf16)
            bs[rows, :] += nn(a, wd_v[cols, :])
            return 0

        lax.fori_loop(0, F // FB, body, 0)

    def piece(buf, i):
        return buf.at[pl.ds(pl.multiple_of(i * PC, PC), PC)]

    def y_piece(dst, first_sem, i):
        return rc(piece(bs, i), piece(dst, i), y_s.at[first_sem + i], y_r.at[first_sem + i], YN)

    Y_BR, Y_FP, Y_TP = 3, 3 + NPC, 3 + 2 * NPC

    for c in wo_f_in:
        c.wait_recv()
    woo_v[...] = G[r_wor : r_wor + L, :].astype(bf16)
    L_WU.wait()
    L_WD.wait()
    for qc in range(2):
        attn_ln(qc)
        ffn(qc)
        for i in range(2 * qc, 2 * qc + 2):
            y_piece(br, Y_BR, i).start()
    wo_y.wait_send()
    wo_x.wait_send()
    for c in wo_f:
        c.wait_send()
    for qc in range(2):
        ctx_copy(qc).wait_send()

    sm[0] = jnp.zeros((16, D), f32)
    L_HC.wait()

    def tail(i, _):
        rows = pl.ds(pl.multiple_of(i * PC, PC), PC)
        y_piece(br, Y_BR, i).wait_recv()
        first = G[pl.ds(pl.multiple_of(r_first + i * PC, PC), PC), :]
        res = first + (bs[rows, :] + br[rows, :]) + vec[V_DB : V_DB + 1, :]
        cen = res - rowmean(res)
        rstd = lax.rsqrt(rowmean(cen * cen) + EPS)
        xv = cen * rstd
        g2 = vec[V_G2 : V_G2 + 1, :]
        tw = vec[V_TW : V_TW + 1, :]
        second = xv * g2 + vec[V_S2 : V_S2 + 1, :]
        hid[rows, :] = second.astype(bf16)
        v = jnp.sum(second * tw, axis=-1, keepdims=True) + vec[V_TB : V_TB + 1, 0:1]
        keep = 1.0 - col[rows, 1:2]
        soft = jnp.maximum(v, 0.0) + jnp.log1p(jnp.exp(-jnp.abs(v)))
        trm[rows, :] = jnp.broadcast_to(soft * keep, (PC, 8))
        dterm = col[rows, 2:3] * keep * lax.logistic(v)
        dsec = hc[rows, :] + dterm * tw
        sm[0, G_G2 : G_G2 + 1, :] += colsum(dsec * xv)
        sm[0, G_S2 : G_S2 + 1, :] += colsum(dsec)
        sm[0, G_TW : G_TW + 1, :] += colsum(dterm * second)
        sm[0, G_TB : G_TB + 1, :] += jnp.broadcast_to(colsum(dterm), (1, D))
        dx = dsec * g2
        dr = rstd * (dx - rowmean(dx) - xv * rowmean(dx * xv))
        hc[rows, :] = dr
        low = dr.astype(bf16)
        db[rows, :] = low
        sm[0, G_DB : G_DB + 1, :] += colsum(low.astype(f32))
        return 0

    lax.fori_loop(0, NPC, tail, 0)

    def chunk(b, j):
        return pl.ds(pl.multiple_of(b * SUB + core * HALF + j * CK, 8), CK)

    def chunk_s(b, j):
        return pl.ds(pl.multiple_of(b * SUB + (1 - core) * HALF + j * CK, 8), CK)

    def mine(b, j):
        return G[chunk(b, j), :] + S[b, pl.ds(pl.multiple_of(j * CK, 8), CK), :]

    def sib_copy(b):
        src = G.at[pl.ds(pl.multiple_of(b * SUB + (1 - core) * HALF, 8), HALF)]
        return rc(src, S.at[b], sib_s.at[b], sib_r.at[b], SIB)

    def rs_copy(b, k):
        src = G.at[chunk(b, vp)] if k == 0 else R.at[b, k - 1]
        return rc(src, R.at[b, k], rs_s.at[b, k], rs_r.at[b, k], NXT)

    def ag_copy(b, k):
        rows = chunk(b, (vp + 1 - k + RING) % RING)
        return rc(G.at[rows], G.at[rows], ag_s.at[b, k], ag_r.at[b, k], NXT)

    def ag_in(b, k):
        rows = chunk(b, (vp - k + RING) % RING)
        return rc(G.at[rows], G.at[rows], ag_s.at[b, k], ag_r.at[b, k], NXT)

    def fw_copy(b, k):
        rows = chunk(b, (vp + 1 - k + RING) % RING)
        return rc(G.at[rows], G.at[rows], fw_s.at[b, k], fw_r.at[b, k], SIB)

    def fw_in(b, k):
        rows = chunk_s(b, (vps + 1 - k + RING) % RING)
        return rc(G.at[rows], G.at[rows], fw_s.at[b, k], fw_r.at[b, k], SIB)

    def give(sem, dev):
        pl.semaphore_signal(sem, inc=1, device_id=dev, device_id_type=MESH)

    outs = []

    def put(src, dst):
        c = pltpu.make_async_copy(src, dst, out_sem.at[len(outs)])
        c.start()
        outs.append(c)

    def gblk(r, n, c0=0, c1=None):
        return G.at[pl.ds(r, n), pl.ds(c0, (D if c1 is None else c1) - c0)]

    def write_out(b):
        if b < 2:
            put(gblk(b * SUB, SUB), o_wd.at[pl.ds(b * SUB, SUB)])
        elif b < 4:
            put(gblk(b * SUB, SUB), o_wu.at[:, pl.ds((b - 2) * D, D)])
        elif b == 4:
            put(gblk(4 * SUB, L), o_wo)
            put(gblk(4 * SUB + L, L, 0, L), o_wq.at[pl.ds(0, L)])
            put(gblk(4 * SUB + L, L, L, 2 * L), o_wk.at[pl.ds(0, L)])
        else:
            put(gblk(5 * SUB, L, 0, L), o_wq.at[pl.ds(L, L)])
            put(gblk(5 * SUB, L, L, 2 * L), o_wk.at[pl.ds(L, L)])
            put(gblk(5 * SUB + L, L, 0, L), o_wv.at[pl.ds(0, L)])
            put(gblk(5 * SUB + L, L, L, 2 * L), o_wv.at[pl.ds(L, L)])

    def event(b, e):
        if e == 0:
            sib_copy(b).start()
        elif e == 1:
            sib_copy(b).wait_recv()
            G[chunk(b, vp), :] = mine(b, vp)
            rs_copy(b, 0).start()
            sib_copy(b).wait_send()
            give(free_sib.at[b], SIB)
        elif e < RING:
            k = e - 1
            rs_copy(b, k - 1).wait_recv()
            R[b, k - 1] += mine(b, (vp - k + RING) % RING)
            rs_copy(b, k).start()
            if k == 1:
                rs_copy(b, 0).wait_send()
                give(free_ring.at[b], PRV)
        elif e == RING:
            rs_copy(b, RING - 2).wait_recv()
            j = (vp + 1) % RING
            G[chunk(b, j), :] = R[b, RING - 2] + mine(b, j)
            pl.semaphore_wait(free_ring.at[b], 1)
            ag_copy(b, 0).start()
            pl.semaphore_wait(free_sib.at[b], 1)
            fw_copy(b, 0).start()
        elif e < 2 * RING:
            k = e - RING
            ag_in(b, k - 1).wait_recv()
            if k < RING - 1:
                ag_copy(b, k).start()
            fw_copy(b, k).start()
        else:
            for k in range(RING - 1):
                if k:
                    rs_copy(b, k).wait_send()
                ag_copy(b, k).wait_send()
            for k in range(RING):
                fw_copy(b, k).wait_send()
                fw_in(b, k).wait_recv()
            write_out(b)

    progress = {}
    turn = [0]

    def start_batch(b):
        event(b, 0)
        progress[b] = 1

    def pump(n):
        for _ in range(n):
            live = sorted(b for b in progress if progress[b] <= 2 * RING)
            if not live:
                return
            b = live[turn[0] % len(live)]
            turn[0] += 1
            event(b, progress[b])
            progress[b] += 1

    def dwd(rb, _):
        cols = pl.ds(pl.multiple_of(rb * 256, 256), 256)
        G[cols, :] = tn(act[:, cols], db[...])
        return 0

    per = SUB // 256
    lax.fori_loop(0, per, dwd, 0)
    start_batch(0)
    lax.fori_loop(per, 2 * per, dwd, 0)
    start_batch(1)
    pump(1)
    put(hid, o_hid)

    for i in range(NPC):
        y_piece(br, Y_BR, i).wait_send()

    def ffn_back(qc):
        rows = pl.ds(qc * CH, CH)
        bs[rows, :] = jnp.zeros((CH, D), f32)

        def body(fb, _):
            cols = pl.ds(pl.multiple_of(fb * FB, FB), FB)
            low = (nt(db[rows, :], wd_v[cols, :]) * gp[rows, cols].astype(f32)).astype(bf16)
            du[rows, cols] = low
            bs[rows, :] += nt(low, wu_v[:, cols])
            return 0

        lax.fori_loop(0, F // FB, body, 0)

    for qc in range(2):
        ffn_back(qc)
        for i in range(2 * qc, 2 * qc + 2):
            y_piece(fr, Y_FP, i).start()
        pump(2)

    def dwu(base_row):
        def body(cb, _):
            cols = pl.ds(pl.multiple_of(cb * 256, 256), 256)
            fcols = pl.ds(pl.multiple_of(base_row - 2 * SUB + cb * 256, 256), 256)
            G[base_row : base_row + SUB, cols] = tn(fl[...], du[:, fcols])
            return 0

        return body

    lax.fori_loop(0, D // 256, dwu(2 * SUB), 0)
    start_batch(2)
    pump(2)
    lax.fori_loop(0, D // 256, dwu(3 * SUB), 0)
    start_batch(3)
    pump(2)
    for h in range(F // D):
        sm[0, G_UB0 + h : G_UB0 + h + 1, :] = colsum(du[:, h * D : (h + 1) * D].astype(f32))

    pump(6)

    def norm_back(i, _):
        rows = pl.ds(pl.multiple_of(i * PC, PC), PC)
        y_piece(fr, Y_FP, i).wait_recv()
        dfirst = hc[rows, :] + (bs[rows, :] + fr[rows, :])
        xv = xh[rows, :]
        sm[0, G_G1 : G_G1 + 1, :] += colsum(dfirst * xv)
        sm[0, G_S1 : G_S1 + 1, :] += colsum(dfirst)
        dx = dfirst * vec[V_G1 : V_G1 + 1, :]
        dr = rs[rows, 0:1] * (dx - rowmean(dx) - xv * rowmean(dx * xv))
        hc[rows, :] = dr
        low = dr.astype(bf16)
        db[rows, :] = low
        sm[0, G_OB : G_OB + 1, :] += colsum(low.astype(f32))
        return 0

    for i in range(NPC):
        norm_back(i, 0)
        pump(4 if i < NPC - 1 else 1)

    dc = nt(db[...], wo_v[...])
    for par in range(2):
        one = jnp.where(odd == par, dc, 0.0).astype(bf16)
        dcz[par * T : (par + 1) * T, :] = one
        dcTz[par * L : (par + 1) * L, :] = one.T
    pump(1)

    def attend_back(hp, _):
        blk = pl.ds(pl.multiple_of(hp * 128, 128), 128)
        for par in range(2):
            qrows = pl.ds(pl.multiple_of(par * L + hp * 128, 128), 128)
            head = pl.ds(pl.multiple_of(hp * 128 + par * HEAD_DIM, HEAD_DIM), HEAD_DIM)
            for qc in range(2):
                pcols = pl.ds(par * T + qc * CH, CH)
                dp = nn(vn[:, blk], dcTz[qrows, qc * CH : (qc + 1) * CH])
                p = pm[hp, :, pcols].astype(f32)
                t = dp * p
                dsb[:, pcols] = (t - p * colsum(t)).astype(bf16)
            d = nn(kT[head, :], dsb[:, par * T : (par + 1) * T]) * (HEAD_DIM**-0.5)
            dqT[head, :] = d.astype(bf16)
        dk[:, blk] = nn(dsb[...], qz[:, blk]).astype(bf16)
        dv[:, blk] = nn(pm[hp], dcz[:, blk]).astype(bf16)
        return 0

    for hp in range(NP):
        attend_back(hp, 0)
        pump(2)
    dq[...] = dqT[...].T

    for i in range(NPC):
        y_piece(fr, Y_FP, i).wait_send()
    for qc in range(2):
        rows = pl.ds(qc * CH, CH)
        bs[rows, :] = nt(dq[rows, :], wq_v[...]) + nt(dk[rows, :], wk_v[...]) + nt(dv[rows, :], wv_v[...])
        for i in range(2 * qc, 2 * qc + 2):
            y_piece(br, Y_TP, i).start()
    pump(1)
    G[4 * SUB : 4 * SUB + L, :] = nn(ctxT[...], db[...])
    G[4 * SUB + L : 4 * SUB + L + D, 0:L] = tn(tok_v[...], dq[...])
    G[4 * SUB + L : 4 * SUB + L + D, L : 2 * L] = tn(tok_v[...], dk[...])
    start_batch(4)
    pump(2)
    g = tn(tok_v[...], dv[...])
    G[5 * SUB + L : 6 * SUB, 0:L] = g[0:L]
    G[5 * SUB + L : 6 * SUB, L : 2 * L] = g[L : 2 * L]
    start_batch(5)
    pump(2)

    sm[0, G_QV : G_QV + 1, 0:L] = colsum(dq[...].astype(f32))
    sm[0, G_QV : G_QV + 1, L : 2 * L] = colsum(dv[...].astype(f32))

    def sm_copy(k):
        return rc(sm.at[k], smr.at[k], sm_s.at[k], sm_r.at[k], (SIB, XN, Z1, Z2)[k])

    for k in range(4):
        sm_copy(k).start()
        pump(3)
        sm_copy(k).wait()
        sm[k + 1] = sm[k] + smr[k]
    put(sm.at[4], o_sm)
    o_term[...] = trm[...].T[0:1, :]

    for i in range(NPC):
        pump(4)
        rows = pl.ds(i * PC, PC)
        y_piece(br, Y_TP, i).wait_recv()
        hc[rows, :] += bs[rows, :] + br[rows, :]
        put(piece(hc, i), piece(o_tok, i))
    pump(BATCHES * 2 * RING)
    for i in range(NPC):
        y_piece(br, Y_TP, i).wait_send()
    for c in outs:
        c.wait()


def per_device(
    tokens, segment_ids, pad_flags, query_weight, query_bias, key_weight, value_weight, value_bias, output_weight,
    output_bias, first_gain, first_shift, up_weight, up_bias, down_weight, down_bias, second_gain, second_shift,
    term_weight, term_bias, hidden_cot, term_cot, *, groups,
):
    T, D = tokens.shape
    L, F = query_weight.shape[1], up_weight.shape[1]
    vec = jnp.concatenate(
        [query_bias, value_bias, output_bias, first_gain, first_shift, down_bias, second_gain, second_shift, term_weight,
         jnp.broadcast_to(term_bias, (D,))]
    ).astype(f32).reshape(9, D)
    anywhere, vmem = pl.BlockSpec(memory_space=pl.ANY), pl.BlockSpec(memory_space=pltpu.VMEM)
    sub = 3 * F // BATCHES
    dma = pltpu.SemaphoreType.DMA
    V = pltpu.VMEM
    outs = pl.pallas_call(
        kernel,
        out_shape=[
            jax.ShapeDtypeStruct((T, D), bf16),
            jax.ShapeDtypeStruct((1, T), f32),
            jax.ShapeDtypeStruct((T, D), f32),
            jax.ShapeDtypeStruct((D, L), f32),
            jax.ShapeDtypeStruct((D, L), f32),
            jax.ShapeDtypeStruct((D, L), f32),
            jax.ShapeDtypeStruct((L, D), f32),
            jax.ShapeDtypeStruct((D, F), f32),
            jax.ShapeDtypeStruct((F, D), f32),
            jax.ShapeDtypeStruct((16, D), f32),
        ],
        in_specs=[anywhere] + [vmem] * 5 + [anywhere] * 7,
        out_specs=[anywhere, vmem] + [anywhere] * 8,
        scratch_shapes=[
            V((T, D), bf16), V((D, L), bf16), V((D, L), bf16), V((D, L), bf16), V((L, D), bf16), V((L, D), bf16),
            V((D, F), bf16), V((F, D), bf16), V((T, D), f32),
            V((T, L), bf16), V((T, L), bf16), V((L, T), bf16), V((L, T), bf16),
            V((2 * T, L), bf16), V((2 * L, T), bf16), V((L // 128, T, 2 * T), bf16), V((L, T), bf16),
            V((T, D), f32), V((T, 128), f32), V((T, D), bf16),
            V((T, F), bf16), V((T, F), bf16), V((T, D), f32), V((T, D), f32), V((T, D), f32),
            V((T, D), bf16), V((T, F), bf16),
            V((2 * T, L), bf16), V((2 * L, T), bf16), V((T, 2 * T), bf16), V((L, T), bf16),
            V((T, L), bf16), V((T, L), bf16), V((T, L), bf16), V((T, D), bf16), V((T, 8), f32), V((T, 8), f32),
            V((5, 16, D), f32), V((4, 16, D), f32),
            V((3 * F, D), f32), V((BATCHES, sub // 2, D), f32), V((BATCHES, RING - 1, sub // 2 // RING, D), f32),
            dma((8,)), dma((20,)), dma((15,)), dma((15,)), dma((1,)), dma((1,)), dma((2,)), dma((2,)), dma((4,)), dma((4,)),
            dma((BATCHES,)), dma((BATCHES,)), dma((BATCHES, RING - 1)), dma((BATCHES, RING - 1)),
            dma((BATCHES, RING - 1)), dma((BATCHES, RING - 1)), dma((BATCHES, RING)), dma((BATCHES, RING)),
            pltpu.SemaphoreType.REGULAR((BATCHES,)), pltpu.SemaphoreType.REGULAR((BATCHES,)),
        ],
        compiler_params=pltpu.CompilerParams(
            collective_id=0, has_side_effects=True, vmem_limit_bytes=64 * 2**20 - 2**18
        ),
    )(
        tokens, segment_ids, pad_flags, term_cot.reshape(1, T), vec, up_bias.astype(f32).reshape(1, F), query_weight,
        key_weight, value_weight, output_weight, up_weight, down_weight, hidden_cot,
    )
    hidden, term, tokens_grad, gq, gk, gv, go, gu, gd, sm = outs
    if groups > 1:
        gq, gk, gv, go, gu, gd, sm = lax.psum(
            tuple(v * (1.0 / GROUP) for v in (gq, gk, gv, go, gu, gd, sm)), "dp"
        )
    return (
        hidden, term.reshape(T), tokens_grad, gq, sm[G_QV, 0:L], gk, gv, sm[G_QV, L:], go, sm[G_OB], sm[G_G1], sm[G_S1],
        gu, sm[G_UB0 : G_UB1 + 1].reshape(F), gd, sm[G_DB], sm[G_G2], sm[G_S2], sm[G_TW], sm[G_TB, 0:1],
    )


def solution(mesh):
    rows, cols, vec = P("dp", None), P(None, "mp"), P("mp")
    return jax.shard_map(
        partial(per_device, groups=mesh.shape["dp"] // GROUP),
        mesh=mesh,
        in_specs=(
            rows, rows, rows, cols, vec, cols, cols, vec, P("mp", None), P(), P(), P(), cols, vec, P("mp", None), P(), P(),
            P(), P(), P(), rows, P("dp"),
        ),
        out_specs=(
            rows, P("dp"), rows, cols, vec, cols, cols, vec, P("mp", None), P(), P(), P(), cols, vec, P("mp", None), P(),
            P(), P(), P(), P(),
        ),
        check_vma=False,
    )
```

```python
from functools import partial

import jax
import jax.numpy as jnp
from jax import lax
from jax.experimental import pallas as pl
from jax.experimental.pallas import tpu as pltpu
from jax.sharding import PartitionSpec as P

HEAD_DIM = 64
EPS = 1e-06
GROUP = 16
RING = 8
BATCHES = 6
MESH = pl.DeviceIdType.MESH
VMEM_LIMIT = 47 * 2**20
bf16, f32 = jnp.bfloat16, jnp.float32

V_QV, V_OB, V_G1, V_S1, V_DB, V_G2, V_S2, V_TW, V_TB = range(9)
G_QV, G_OB, G_G1, G_S1, G_UB0, G_UB1, G_DB, G_G2, G_S2, G_TW, G_TB = range(11)


def nn(a, b):
    return jnp.dot(a, b, preferred_element_type=f32)


def nt(a, b):
    return lax.dot_general(a, b, (((1,), (1,)), ((), ())), preferred_element_type=f32)


def tn(a, b):
    return lax.dot_general(a, b, (((0,), (0,)), ((), ())), preferred_element_type=f32)


def colsum(v):
    return jnp.sum(v, axis=0, keepdims=True)


def rowmean(v):
    return jnp.mean(v, axis=-1, keepdims=True)


def kernel(
    tokens, seg, pad, tcot, i_qb, i_vb, i_ob, i_g1, i_s1, i_ub, i_db, i_g2, i_s2, i_tw, i_tb, wq, wk, wv, wo, wu, wd, hcot,
    G, hc, hid, o_term, smt,
    v_tcot, v_qb, v_vb, v_ob, v_g1, v_s1, v_ub, v_db, v_g2, v_s2, v_tw, vec, ubv,
    tok_v, wq_v, wk_v, wv_v, wo_v, woo_v, wu_v, wd_v,
    kn, vn, kT, vT, qz, qTz, pm, ctxT, xh, rs, fl, gp, act, bs, br, fr, db, du,
    dcz, dcTz, dsb, dqT, dq, dk, dv, col, trm, sm, smr, S, R,
    ld_sem, y_s, y_r, wx_s, wx_r, ws_s, ws_r, sm_s, sm_r,
    sib_s, sib_r, rs_s, rs_r, ag_s, ag_r, fw_s, fw_r, free_sib, free_ring,
):
    T, D = tokens.shape
    L, F = wq.shape[1], wu.shape[1]
    NP = L // 128
    CH, PC, FB = T // 2, T // 4, 512
    NPC = T // PC
    SUB = G.shape[0] // BATCHES
    HALF, CK = SUB // 2, SUB // 2 // RING

    me, mp = lax.axis_index("dp"), lax.axis_index("mp")
    base, rank = me // GROUP * GROUP, me % GROUP
    core, chip = rank % 2, rank // 2
    x, z = chip % 2, chip // 2
    pos = jnp.where(x == 0, z, RING - 1 - z)
    vp = jnp.where(core == 0, pos, (RING - pos) % RING)
    vps = (RING - vp) % RING

    def at_vp(v):
        p = jnp.where(core == 0, v, (RING - v) % RING)
        c = jnp.where(p < RING // 2, 2 * p, 2 * (RING - 1 - p) + 1)
        return (base + 2 * c + core, mp)

    def at_xz(ax, az):
        return (base + 2 * (2 * az + ax) + core, mp)

    YN = (me, 1 - mp)
    SIB = (base + 2 * chip + 1 - core, mp)
    NXT, PRV = at_vp((vp + 1) % RING), at_vp((vp + RING - 1) % RING)
    XN = at_xz(1 - x, z)
    Z1 = at_xz(x, z // 2 * 2 + 1 - z % 2)
    Z2 = at_xz(x, (z + 2) % 4)

    def rc(src, dst, ss, rr, dev):
        return pltpu.make_async_remote_copy(
            src_ref=src, dst_ref=dst, send_sem=ss, recv_sem=rr, device_id=dev, device_id_type=MESH
        )

    pairs = [
        (tokens, tok_v), (wq, wq_v), (wk, wk_v), (wv, wv_v), (wo, wo_v), (wu, wu_v), (wd, wd_v), (hcot, hc),
        (tcot, v_tcot), (i_qb, v_qb), (i_vb, v_vb), (i_ob, v_ob), (i_g1, v_g1), (i_s1, v_s1), (i_ub, v_ub), (i_db, v_db),
        (i_g2, v_g2), (i_s2, v_s2), (i_tw, v_tw),
    ]
    loads = [pltpu.make_async_copy(a, b, ld_sem.at[i]) for i, (a, b) in enumerate(pairs)]
    for c in loads:
        c.start()
    L_TOK, L_WQ, L_WK, L_WV, L_WO, L_WU, L_WD, L_HC, *L_VEC = loads

    peers = (YN, SIB, NXT, PRV, XN, Z1, Z2)
    bar = pltpu.get_barrier_semaphore()
    for d in peers:
        pl.semaphore_signal(bar, inc=1, device_id=d, device_id_type=MESH)
    pl.semaphore_wait(bar, len(peers))

    r_first = 1 * F
    r_wor = r_first + T
    r_wos = r_wor + L
    r_bias = 2 * F
    r_cs = r_bias + T
    r_cr = r_cs + L
    SH = L // 4

    L_WO.wait()
    share = pl.multiple_of((2 * x + core) * SH, SH)
    share_x = pl.multiple_of((2 * (1 - x) + core) * SH, SH)
    share_s = pl.multiple_of((2 * x + 1 - core) * SH, SH)
    share_sx = pl.multiple_of((2 * (1 - x) + 1 - core) * SH, SH)
    G[r_wos : r_wos + SH, :] = wo_v[pl.ds(share, SH), :].astype(f32)

    def wor(s):
        return G.at[pl.ds(pl.multiple_of(r_wor + s, 32), SH)]

    wo_y = rc(G.at[pl.ds(r_wos, SH)], wor(share), y_s.at[0], y_r.at[0], YN)
    wo_y.start()
    wo_x = rc(wor(share), wor(share), wx_s.at[0], wx_r.at[0], XN)
    wo_x_in = rc(wor(share_x), wor(share_x), wx_s.at[0], wx_r.at[0], XN)
    wo_f = [
        rc(wor(share), wor(share), ws_s.at[0], ws_r.at[0], SIB),
        rc(wor(share_x), wor(share_x), ws_s.at[1], ws_r.at[1], SIB),
    ]
    wo_f_in = [
        rc(wor(share_s), wor(share_s), ws_s.at[0], ws_r.at[0], SIB),
        rc(wor(share_sx), wor(share_sx), ws_s.at[1], ws_r.at[1], SIB),
    ]

    for c in L_VEC:
        c.wait()
    vec[V_QV : V_QV + 1, 0:L] = v_qb[...].astype(f32).reshape(1, L)
    vec[V_QV : V_QV + 1, L : 2 * L] = v_vb[...].astype(f32).reshape(1, L)
    vec[V_OB : V_OB + 1, :] = v_ob[...].astype(f32).reshape(1, D)
    vec[V_G1 : V_G1 + 1, :] = v_g1[...].astype(f32).reshape(1, D)
    vec[V_S1 : V_S1 + 1, :] = v_s1[...].astype(f32).reshape(1, D)
    vec[V_DB : V_DB + 1, :] = v_db[...].astype(f32).reshape(1, D)
    vec[V_G2 : V_G2 + 1, :] = v_g2[...].astype(f32).reshape(1, D)
    vec[V_S2 : V_S2 + 1, :] = v_s2[...].astype(f32).reshape(1, D)
    vec[V_TW : V_TW + 1, :] = v_tw[...].astype(f32).reshape(1, D)
    vec[V_TB : V_TB + 1, :] = jnp.broadcast_to(i_tb[...].astype(f32).reshape(1, 1), (1, D))
    ubv[...] = v_ub[...].astype(f32).reshape(1, F)

    L_TOK.wait()
    L_WQ.wait()
    lane = lax.broadcasted_iota(jnp.int32, (T, L), 1)
    odd = (lane // HEAD_DIM) % 2
    qv = (nn(tok_v[...], wq_v[...]) + vec[V_QV : V_QV + 1, 0:L]).astype(bf16).astype(f32) * (HEAD_DIM**-0.5)
    for par in range(2):
        one = jnp.where(odd == par, qv, 0.0).astype(bf16)
        qz[par * T : (par + 1) * T, :] = one
        qTz[par * L : (par + 1) * L, :] = one.T
    L_WK.wait()
    kv = nn(tok_v[...], wk_v[...]).astype(bf16)
    kn[...] = kv
    kT[...] = kv.T
    L_WV.wait()
    vv = (nn(tok_v[...], wv_v[...]) + vec[V_QV : V_QV + 1, L : 2 * L]).astype(bf16)
    vn[...] = vv
    vT[...] = vv.T

    segf, padf = seg[...].astype(f32), pad[...].astype(f32)
    rows8 = jnp.concatenate([segf, padf, v_tcot[...].reshape(1, T), jnp.zeros((5, T), f32)], axis=0)
    col[...] = rows8.T
    for qc in range(2):
        ki = lax.broadcasted_iota(jnp.int32, (T, CH), 0)
        qi = lax.broadcasted_iota(jnp.int32, (T, CH), 1) + qc * CH
        same = col[:, 0:1] == segf[:, qc * CH : (qc + 1) * CH]
        allowed = same & ((col[:, 1:2] == 0.0) | (ki == qi))
        G[r_bias : r_bias + T, qc * CH : (qc + 1) * CH] = jnp.where(allowed, 0.0, -1e9)

    def ctx_copy(qc):
        cols = pl.ds(qc * CH, CH)
        return rc(
            G.at[pl.ds(r_cs, L), cols], G.at[pl.ds(r_cr, L), cols], y_s.at[1 + qc], y_r.at[1 + qc], YN
        )

    def attend(qc):
        cols = pl.ds(qc * CH, CH)

        def body(hp, _):
            blk = pl.ds(pl.multiple_of(hp * 128, 128), 128)
            for par in range(2):
                qrows = pl.ds(pl.multiple_of(par * L + hp * 128, 128), 128)
                head = pl.multiple_of(hp * 128 + par * HEAD_DIM, HEAD_DIM)
                s = nn(kn[:, blk], qTz[qrows, cols]) + G[r_bias : r_bias + T, cols]
                e = jnp.exp(s - jnp.max(s, axis=0, keepdims=True))
                p = (e * (1.0 / colsum(e))).astype(bf16)
                pm[hp, :, pl.ds(par * T + qc * CH, CH)] = p
                c = nn(vT[pl.ds(head, HEAD_DIM), :], p).astype(bf16)
                ctxT[pl.ds(head, HEAD_DIM), cols] = c
                G[pl.ds(pl.multiple_of(r_cs + head, HEAD_DIM), HEAD_DIM), cols] = c.astype(f32)
            return 0

        lax.fori_loop(0, NP, body, 0)

    attend(0)
    ctx_copy(0).start()
    wo_y.wait_recv()
    wo_x.start()
    wo_f[0].start()
    attend(1)
    ctx_copy(1).start()
    wo_x_in.wait_recv()
    wo_f[1].start()

    def attn_ln(qc):
        c0 = qc * CH
        cols = pl.ds(c0, CH)
        ctx_copy(qc).wait_recv()
        other = G[r_cr : r_cr + L, cols].astype(bf16)
        bs[c0 : c0 + CH, :] = tn(ctxT[:, cols], wo_v[...]) + tn(other, woo_v[...])

        def body(i, _):
            rows = pl.ds(pl.multiple_of(c0 + i * PC, PC), PC)
            res = tok_v[rows, :].astype(f32) + bs[rows, :] + vec[V_OB : V_OB + 1, :]
            cen = res - rowmean(res)
            rstd = lax.rsqrt(rowmean(cen * cen) + EPS)
            xv = cen * rstd
            xh[rows, :] = xv
            rs[rows, :] = jnp.broadcast_to(rstd, (PC, 128))
            first = xv * vec[V_G1 : V_G1 + 1, :] + vec[V_S1 : V_S1 + 1, :]
            G[pl.ds(pl.multiple_of(r_first + c0 + i * PC, PC), PC), :] = first
            fl[rows, :] = first.astype(bf16)
            return 0

        lax.fori_loop(0, CH // PC, body, 0)

    def ffn(qc):
        rows = pl.ds(qc * CH, CH)
        bs[rows, :] = jnp.zeros((CH, D), f32)

        def body(fb, _):
            cols = pl.ds(pl.multiple_of(fb * FB, FB), FB)
            u = nn(fl[rows, :], wu_v[:, cols]) + ubv[:, cols]
            ph = 0.5 + 0.5 * lax.erf(u * 0.7071067811865476)
            a = (u * ph).astype(bf16)
            act[rows, cols] = a
            gp[rows, cols] = (ph + u * (jnp.exp(-0.5 * u * u) * 0.3989422804014327)).astype(bf16)
            bs[rows, :] += nn(a, wd_v[cols, :])
            return 0

        lax.fori_loop(0, F // FB, body, 0)

    def piece(buf, i):
        return buf.at[pl.ds(pl.multiple_of(i * PC, PC), PC)]

    def y_piece(dst, first_sem, i):
        return rc(piece(bs, i), piece(dst, i), y_s.at[first_sem + i], y_r.at[first_sem + i], YN)

    Y_BR, Y_FP, Y_TP = 3, 3 + NPC, 3 + 2 * NPC

    for c in wo_f_in:
        c.wait_recv()
    woo_v[...] = G[r_wor : r_wor + L, :].astype(bf16)
    L_WU.wait()
    L_WD.wait()
    for qc in range(2):
        attn_ln(qc)
        ffn(qc)
        for i in range(2 * qc, 2 * qc + 2):
            y_piece(br, Y_BR, i).start()
    wo_y.wait_send()
    wo_x.wait_send()
    for c in wo_f:
        c.wait_send()
    for qc in range(2):
        ctx_copy(qc).wait_send()

    sm[0] = jnp.zeros((16, D), f32)
    L_HC.wait()

    def tail(i, _):
        rows = pl.ds(pl.multiple_of(i * PC, PC), PC)
        y_piece(br, Y_BR, i).wait_recv()
        first = G[pl.ds(pl.multiple_of(r_first + i * PC, PC), PC), :]
        res = first + (bs[rows, :] + br[rows, :]) + vec[V_DB : V_DB + 1, :]
        cen = res - rowmean(res)
        rstd = lax.rsqrt(rowmean(cen * cen) + EPS)
        xv = cen * rstd
        g2 = vec[V_G2 : V_G2 + 1, :]
        tw = vec[V_TW : V_TW + 1, :]
        second = xv * g2 + vec[V_S2 : V_S2 + 1, :]
        hid[rows, :] = second.astype(bf16)
        v = jnp.sum(second * tw, axis=-1, keepdims=True) + vec[V_TB : V_TB + 1, 0:1]
        keep = 1.0 - col[rows, 1:2]
        soft = jnp.maximum(v, 0.0) + jnp.log1p(jnp.exp(-jnp.abs(v)))
        trm[rows, :] = jnp.broadcast_to(soft * keep, (PC, 8))
        dterm = col[rows, 2:3] * keep * lax.logistic(v)
        dsec = hc[rows, :] + dterm * tw
        sm[0, G_G2 : G_G2 + 1, :] += colsum(dsec * xv)
        sm[0, G_S2 : G_S2 + 1, :] += colsum(dsec)
        sm[0, G_TW : G_TW + 1, :] += colsum(dterm * second)
        sm[0, G_TB : G_TB + 1, :] += jnp.broadcast_to(colsum(dterm), (1, D))
        dx = dsec * g2
        dr = rstd * (dx - rowmean(dx) - xv * rowmean(dx * xv))
        hc[rows, :] = dr
        low = dr.astype(bf16)
        db[rows, :] = low
        sm[0, G_DB : G_DB + 1, :] += colsum(low.astype(f32))
        return 0

    lax.fori_loop(0, NPC, tail, 0)

    def chunk(b, j):
        return pl.ds(pl.multiple_of(b * SUB + core * HALF + j * CK, 8), CK)

    def chunk_s(b, j):
        return pl.ds(pl.multiple_of(b * SUB + (1 - core) * HALF + j * CK, 8), CK)

    def mine(b, j):
        return G[chunk(b, j), :] + S[b, pl.ds(pl.multiple_of(j * CK, 8), CK), :]

    def sib_copy(b):
        src = G.at[pl.ds(pl.multiple_of(b * SUB + (1 - core) * HALF, 8), HALF)]
        return rc(src, S.at[b], sib_s.at[b], sib_r.at[b], SIB)

    def rs_copy(b, k):
        src = G.at[chunk(b, vp)] if k == 0 else R.at[b, k - 1]
        return rc(src, R.at[b, k], rs_s.at[b, k], rs_r.at[b, k], NXT)

    def ag_copy(b, k):
        rows = chunk(b, (vp + 1 - k + RING) % RING)
        return rc(G.at[rows], G.at[rows], ag_s.at[b, k], ag_r.at[b, k], NXT)

    def ag_in(b, k):
        rows = chunk(b, (vp - k + RING) % RING)
        return rc(G.at[rows], G.at[rows], ag_s.at[b, k], ag_r.at[b, k], NXT)

    def fw_copy(b, k):
        rows = chunk(b, (vp + 1 - k + RING) % RING)
        return rc(G.at[rows], G.at[rows], fw_s.at[b, k], fw_r.at[b, k], SIB)

    def fw_in(b, k):
        rows = chunk_s(b, (vps + 1 - k + RING) % RING)
        return rc(G.at[rows], G.at[rows], fw_s.at[b, k], fw_r.at[b, k], SIB)

    def give(sem, dev):
        pl.semaphore_signal(sem, inc=1, device_id=dev, device_id_type=MESH)

    def event(b, e):
        if e == 0:
            sib_copy(b).start()
        elif e == 1:
            sib_copy(b).wait_recv()
            G[chunk(b, vp), :] = mine(b, vp)
            rs_copy(b, 0).start()
            sib_copy(b).wait_send()
            give(free_sib.at[b], SIB)
        elif e < RING:
            k = e - 1
            rs_copy(b, k - 1).wait_recv()
            R[b, k - 1] += mine(b, (vp - k + RING) % RING)
            rs_copy(b, k).start()
            if k == 1:
                rs_copy(b, 0).wait_send()
                give(free_ring.at[b], PRV)
        elif e == RING:
            rs_copy(b, RING - 2).wait_recv()
            j = (vp + 1) % RING
            G[chunk(b, j), :] = R[b, RING - 2] + mine(b, j)
            pl.semaphore_wait(free_ring.at[b], 1)
            ag_copy(b, 0).start()
            pl.semaphore_wait(free_sib.at[b], 1)
            fw_copy(b, 0).start()
        elif e < 2 * RING:
            k = e - RING
            ag_in(b, k - 1).wait_recv()
            if k < RING - 1:
                ag_copy(b, k).start()
            fw_copy(b, k).start()
        else:
            for k in range(RING - 1):
                if k:
                    rs_copy(b, k).wait_send()
                ag_copy(b, k).wait_send()
            for k in range(RING):
                fw_copy(b, k).wait_send()
                fw_in(b, k).wait_recv()

    progress = {}
    turn = [0]

    def start_batch(b):
        event(b, 0)
        progress[b] = 1

    def pump(n):
        for _ in range(n):
            live = sorted(b for b in progress if progress[b] <= 2 * RING)
            if not live:
                return
            b = live[turn[0] % len(live)]
            turn[0] += 1
            event(b, progress[b])
            progress[b] += 1

    def dwd(rb, _):
        cols = pl.ds(pl.multiple_of(rb * 256, 256), 256)
        G[cols, :] = tn(act[:, cols], db[...])
        return 0

    per = SUB // 256
    lax.fori_loop(0, per, dwd, 0)
    start_batch(0)
    lax.fori_loop(per, 2 * per, dwd, 0)
    start_batch(1)
    pump(1)

    for i in range(NPC):
        y_piece(br, Y_BR, i).wait_send()

    def ffn_back(qc):
        rows = pl.ds(qc * CH, CH)
        bs[rows, :] = jnp.zeros((CH, D), f32)

        def body(fb, _):
            cols = pl.ds(pl.multiple_of(fb * FB, FB), FB)
            low = (nt(db[rows, :], wd_v[cols, :]) * gp[rows, cols].astype(f32)).astype(bf16)
            du[rows, cols] = low
            bs[rows, :] += nt(low, wu_v[:, cols])
            return 0

        lax.fori_loop(0, F // FB, body, 0)

    for qc in range(2):
        ffn_back(qc)
        for i in range(2 * qc, 2 * qc + 2):
            y_piece(fr, Y_FP, i).start()
        pump(2)

    def dwu(base_row):
        def body(cb, _):
            cols = pl.ds(pl.multiple_of(cb * 256, 256), 256)
            fcols = pl.ds(pl.multiple_of(base_row - 2 * SUB + cb * 256, 256), 256)
            G[base_row : base_row + SUB, cols] = tn(fl[...], du[:, fcols])
            return 0

        return body

    lax.fori_loop(0, D // 256, dwu(2 * SUB), 0)
    start_batch(2)
    pump(2)
    lax.fori_loop(0, D // 256, dwu(3 * SUB), 0)
    start_batch(3)
    pump(2)
    for h in range(F // D):
        sm[0, G_UB0 + h : G_UB0 + h + 1, :] = colsum(du[:, h * D : (h + 1) * D].astype(f32))

    pump(6)

    def norm_back(i, _):
        rows = pl.ds(pl.multiple_of(i * PC, PC), PC)
        y_piece(fr, Y_FP, i).wait_recv()
        dfirst = hc[rows, :] + (bs[rows, :] + fr[rows, :])
        xv = xh[rows, :]
        sm[0, G_G1 : G_G1 + 1, :] += colsum(dfirst * xv)
        sm[0, G_S1 : G_S1 + 1, :] += colsum(dfirst)
        dx = dfirst * vec[V_G1 : V_G1 + 1, :]
        dr = rs[rows, 0:1] * (dx - rowmean(dx) - xv * rowmean(dx * xv))
        hc[rows, :] = dr
        low = dr.astype(bf16)
        db[rows, :] = low
        sm[0, G_OB : G_OB + 1, :] += colsum(low.astype(f32))
        return 0

    for i in range(NPC):
        norm_back(i, 0)
        pump(4 if i < NPC - 1 else 1)

    dc = nt(db[...], wo_v[...])
    for par in range(2):
        one = jnp.where(odd == par, dc, 0.0).astype(bf16)
        dcz[par * T : (par + 1) * T, :] = one
        dcTz[par * L : (par + 1) * L, :] = one.T
    pump(1)

    def attend_back(hp, _):
        blk = pl.ds(pl.multiple_of(hp * 128, 128), 128)
        for par in range(2):
            qrows = pl.ds(pl.multiple_of(par * L + hp * 128, 128), 128)
            head = pl.ds(pl.multiple_of(hp * 128 + par * HEAD_DIM, HEAD_DIM), HEAD_DIM)
            for qc in range(2):
                pcols = pl.ds(par * T + qc * CH, CH)
                dp = nn(vn[:, blk], dcTz[qrows, qc * CH : (qc + 1) * CH])
                p = pm[hp, :, pcols].astype(f32)
                t = dp * p
                dsb[:, pcols] = (t - p * colsum(t)).astype(bf16)
            d = nn(kT[head, :], dsb[:, par * T : (par + 1) * T]) * (HEAD_DIM**-0.5)
            dqT[head, :] = d.astype(bf16)
        dk[:, blk] = nn(dsb[...], qz[:, blk]).astype(bf16)
        dv[:, blk] = nn(pm[hp], dcz[:, blk]).astype(bf16)
        return 0

    for hp in range(NP):
        attend_back(hp, 0)
        pump(2)
    dq[...] = dqT[...].T

    for i in range(NPC):
        y_piece(fr, Y_FP, i).wait_send()
    for qc in range(2):
        rows = pl.ds(qc * CH, CH)
        bs[rows, :] = nt(dq[rows, :], wq_v[...]) + nt(dk[rows, :], wk_v[...]) + nt(dv[rows, :], wv_v[...])
        for i in range(2 * qc, 2 * qc + 2):
            y_piece(br, Y_TP, i).start()
    pump(1)
    G[4 * SUB : 4 * SUB + L, :] = nn(ctxT[...], db[...])
    G[4 * SUB + L : 4 * SUB + L + D, 0:L] = tn(tok_v[...], dq[...])
    G[4 * SUB + L : 4 * SUB + L + D, L : 2 * L] = tn(tok_v[...], dk[...])
    start_batch(4)
    pump(2)
    g = tn(tok_v[...], dv[...])
    G[5 * SUB + L : 6 * SUB, 0:L] = g[0:L]
    G[5 * SUB + L : 6 * SUB, L : 2 * L] = g[L : 2 * L]
    start_batch(5)
    pump(2)

    sm[0, G_QV : G_QV + 1, 0:L] = colsum(dq[...].astype(f32))
    sm[0, G_QV : G_QV + 1, L : 2 * L] = colsum(dv[...].astype(f32))

    def sm_copy(k):
        return rc(sm.at[k], smr.at[k], sm_s.at[k], sm_r.at[k], (SIB, XN, Z1, Z2)[k])

    for k in range(4):
        sm_copy(k).start()
        pump(3)
        sm_copy(k).wait()
        if k < 3:
            sm[k + 1] = sm[k] + smr[k]
        else:
            smt[...] = sm[k] + smr[k]
    o_term[...] = trm[...].T

    for i in range(NPC):
        pump(4)
        rows = pl.ds(i * PC, PC)
        y_piece(br, Y_TP, i).wait_recv()
        hc[rows, :] += bs[rows, :] + br[rows, :]
    pump(BATCHES * 2 * RING)
    for i in range(NPC):
        y_piece(br, Y_TP, i).wait_send()


def spread(
    G, hc, hid, term, smt,
    o_hid, o_term, o_tok, o_wq, o_qb, o_wk, o_wv, o_vb, o_wo, o_ob, o_g1, o_s1, o_wu, o_ub, o_wd, o_db, o_g2, o_s2, o_tw,
    o_tb,
    sem,
):
    D, L = o_wq.shape
    F = o_wu.shape[1]
    SUB = G.shape[0] // BATCHES

    def g(r, n, c0=0, c1=D):
        return G.at[pl.ds(r, n), pl.ds(c0, c1 - c0)]

    q = 4 * SUB + L
    copies = [(g(0, F), o_wd)]
    copies += [(g(F + h * D, D), o_wu.at[:, pl.ds(h * D, D)]) for h in range(F // D)]
    copies += [
        (hc, o_tok), (hid, o_hid), (g(4 * SUB, L), o_wo), (g(q, D, 0, L), o_wq), (g(q, D, L, 2 * L), o_wk),
        (g(q + D, L, 0, L), o_wv.at[pl.ds(0, L)]), (g(q + D, L, L, 2 * L), o_wv.at[pl.ds(L, L)]),
    ]
    started = [pltpu.make_async_copy(a, b, sem.at[i]) for i, (a, b) in enumerate(copies)]
    for c in started:
        c.start()
    o_term[...] = term[0, :]
    o_qb[...] = smt[G_QV, 0:L]
    o_vb[...] = smt[G_QV, L : 2 * L]
    o_ob[...] = smt[G_OB, :]
    o_g1[...] = smt[G_G1, :]
    o_s1[...] = smt[G_S1, :]
    o_ub[...] = jnp.concatenate([smt[G_UB0 + h : G_UB0 + h + 1, :] for h in range(F // D)], axis=1).reshape(F)
    o_db[...] = smt[G_DB, :]
    o_g2[...] = smt[G_G2, :]
    o_s2[...] = smt[G_S2, :]
    o_tw[...] = smt[G_TW, :]
    o_tb[...] = smt[G_TB : G_TB + 1, 0:1].reshape(1)
    for c in started:
        c.wait()


def per_device(
    tokens, segment_ids, pad_flags, query_weight, query_bias, key_weight, value_weight, value_bias, output_weight,
    output_bias, first_gain, first_shift, up_weight, up_bias, down_weight, down_bias, second_gain, second_shift,
    term_weight, term_bias, hidden_cot, term_cot, *, groups,
):
    T, D = tokens.shape
    L, F = query_weight.shape[1], up_weight.shape[1]
    anywhere, vmem = pl.BlockSpec(memory_space=pl.ANY), pl.BlockSpec(memory_space=pltpu.VMEM)
    sub = 3 * F // BATCHES
    dma = pltpu.SemaphoreType.DMA
    V = pltpu.VMEM
    G, hc, hid, term, smt = pl.pallas_call(
        kernel,
        out_shape=[V((3 * F, D), f32), V((T, D), f32), V((T, D), bf16), V((8, T), f32), V((16, D), f32)],
        in_specs=[anywhere, vmem, vmem] + [anywhere] * 11 + [vmem] + [anywhere] * 7,
        out_specs=[vmem] * 5,
        scratch_shapes=[
            V((T,), f32), V((L,), bf16), V((L,), bf16), V((D,), bf16), V((D,), bf16), V((D,), bf16), V((F,), bf16),
            V((D,), bf16), V((D,), bf16), V((D,), bf16), V((D,), bf16), V((16, D), f32), V((1, F), f32),
            V((T, D), bf16), V((D, L), bf16), V((D, L), bf16), V((D, L), bf16), V((L, D), bf16), V((L, D), bf16),
            V((D, F), bf16), V((F, D), bf16),
            V((T, L), bf16), V((T, L), bf16), V((L, T), bf16), V((L, T), bf16),
            V((2 * T, L), bf16), V((2 * L, T), bf16), V((L // 128, T, 2 * T), bf16), V((L, T), bf16),
            V((T, D), f32), V((T, 128), f32), V((T, D), bf16),
            V((T, F), bf16), V((T, F), bf16), V((T, D), f32), V((T, D), f32), V((T, D), f32),
            V((T, D), bf16), V((T, F), bf16),
            V((2 * T, L), bf16), V((2 * L, T), bf16), V((T, 2 * T), bf16), V((L, T), bf16),
            V((T, L), bf16), V((T, L), bf16), V((T, L), bf16), V((T, 8), f32), V((T, 8), f32),
            V((4, 16, D), f32), V((4, 16, D), f32),
            V((BATCHES, sub // 2, D), f32), V((BATCHES, RING - 1, sub // 2 // RING, D), f32),
            dma((19,)), dma((15,)), dma((15,)), dma((1,)), dma((1,)), dma((2,)), dma((2,)), dma((4,)), dma((4,)),
            dma((BATCHES,)), dma((BATCHES,)), dma((BATCHES, RING - 1)), dma((BATCHES, RING - 1)),
            dma((BATCHES, RING - 1)), dma((BATCHES, RING - 1)), dma((BATCHES, RING)), dma((BATCHES, RING)),
            pltpu.SemaphoreType.REGULAR((BATCHES,)), pltpu.SemaphoreType.REGULAR((BATCHES,)),
        ],
        compiler_params=pltpu.CompilerParams(
            collective_id=0, has_side_effects=True, vmem_limit_bytes=VMEM_LIMIT
        ),
    )(
        tokens, segment_ids, pad_flags, term_cot, query_bias, value_bias, output_bias, first_gain, first_shift, up_bias,
        down_bias, second_gain, second_shift, term_weight, term_bias, query_weight, key_weight, value_weight,
        output_weight, up_weight, down_weight, hidden_cot,
    )
    vector = [jax.ShapeDtypeStruct((n,), f32) for n in (D, L, F, T, 1)]
    vd, vl, vf, vt, v1 = vector
    dl = jax.ShapeDtypeStruct((D, L), f32)
    outs = pl.pallas_call(
        spread,
        out_shape=[
            jax.ShapeDtypeStruct((T, D), bf16), vt, jax.ShapeDtypeStruct((T, D), f32), dl, vl, dl, dl, vl,
            jax.ShapeDtypeStruct((L, D), f32), vd, vd, vd, jax.ShapeDtypeStruct((D, F), f32), vf,
            jax.ShapeDtypeStruct((F, D), f32), vd, vd, vd, vd, v1,
        ],
        in_specs=[vmem] * 5,
        out_specs=[
            anywhere, vmem, anywhere, anywhere, vmem, anywhere, anywhere, vmem, anywhere, vmem, vmem, vmem, anywhere, vmem,
            anywhere, vmem, vmem, vmem, vmem, vmem,
        ],
        scratch_shapes=[dma((16,))],
        compiler_params=pltpu.CompilerParams(vmem_limit_bytes=2**20),
    )(G, hc, hid, term, smt)
    if groups > 1:
        outs = list(outs[:3]) + list(lax.psum(tuple(v * (1.0 / GROUP) for v in outs[3:]), "dp"))
    return tuple(outs)


def solution(mesh):
    rows, cols, vec = P("dp", None), P(None, "mp"), P("mp")
    return jax.shard_map(
        partial(per_device, groups=mesh.shape["dp"] // GROUP),
        mesh=mesh,
        in_specs=(
            rows, rows, rows, cols, vec, cols, cols, vec, P("mp", None), P(), P(), P(), cols, vec, P("mp", None), P(), P(),
            P(), P(), P(), rows, P("dp"),
        ),
        out_specs=(
            rows, P("dp"), rows, cols, vec, cols, cols, vec, P("mp", None), P(), P(), P(), cols, vec, P("mp", None), P(),
            P(), P(), P(), P(),
        ),
        check_vma=False,
    )
```

```python
from collections import deque
from functools import partial

import jax
import jax.numpy as jnp
from jax import lax
from jax.experimental import pallas as pl
from jax.experimental.pallas import tpu as pltpu
from jax.sharding import PartitionSpec as P

HEAD_DIM = 64
EPS = 1e-06
GROUP = 16
RING = 8
BATCHES = 12
MESH = pl.DeviceIdType.MESH
VMEM_LIMIT = 47 * 2**20
bf16, f32 = jnp.bfloat16, jnp.float32

V_QV, V_OB, V_G1, V_S1, V_DB, V_G2, V_S2, V_TW, V_TB = range(9)
G_QV, G_OB, G_G1, G_S1, G_UB0, G_UB1, G_DB, G_G2, G_S2, G_TW, G_TB = range(11)


def nn(a, b):
    return jnp.dot(a, b, preferred_element_type=f32)


def nt(a, b):
    return lax.dot_general(a, b, (((1,), (1,)), ((), ())), preferred_element_type=f32)


def tn(a, b):
    return lax.dot_general(a, b, (((0,), (0,)), ((), ())), preferred_element_type=f32)


def colsum(v):
    return jnp.sum(v, axis=0, keepdims=True)


def rowmean(v):
    return jnp.mean(v, axis=-1, keepdims=True)


def kernel(
    tokens, seg, pad, tcot, i_qb, i_vb, i_ob, i_g1, i_s1, i_ub, i_db, i_g2, i_s2, i_tw, i_tb, wq, wk, wv, wo, wu, wd, hcot,
    G, hc, hid, o_term, smt,
    v_tcot, v_qb, v_vb, v_ob, v_g1, v_s1, v_ub, v_db, v_g2, v_s2, v_tw, vec, ubv,
    tok_v, wq_v, wk_v, wv_v, wo_v, woo_v, wu_v, wd_v,
    kn, vn, kT, vT, qz, qTz, pm, ctxT, xh, rs, fl, gp, act, bs, br, fr, db, du,
    dcz, dcTz, dsb, dqT, dq, dk, dv, col, trm, sm, smr, S, R,
    ld_sem, y_s, y_r, wx_s, wx_r, ws_s, ws_r, sm_s, sm_r,
    sib_s, sib_r, rs_s, rs_r, ag_s, ag_r, fw_s, fw_r, free_sib, free_ring,
):
    T, D = tokens.shape
    L, F = wq.shape[1], wu.shape[1]
    NP = L // 128
    CH, PC, FB = T // 2, T // 4, 512
    NPC = T // PC
    SUB = G.shape[0] // BATCHES
    HALF, CK = SUB // 2, SUB // 2 // RING

    me, mp = lax.axis_index("dp"), lax.axis_index("mp")
    base, rank = me // GROUP * GROUP, me % GROUP
    core, chip = rank % 2, rank // 2
    x, z = chip % 2, chip // 2
    pos = jnp.where(x == 0, z, RING - 1 - z)
    vp = jnp.where(core == 0, pos, (RING - pos) % RING)
    vps = (RING - vp) % RING

    def at_vp(v):
        p = jnp.where(core == 0, v, (RING - v) % RING)
        c = jnp.where(p < RING // 2, 2 * p, 2 * (RING - 1 - p) + 1)
        return (base + 2 * c + core, mp)

    def at_xz(ax, az):
        return (base + 2 * (2 * az + ax) + core, mp)

    YN = (me, 1 - mp)
    SIB = (base + 2 * chip + 1 - core, mp)
    NXT, PRV = at_vp((vp + 1) % RING), at_vp((vp + RING - 1) % RING)
    XN = at_xz(1 - x, z)
    Z1 = at_xz(x, z // 2 * 2 + 1 - z % 2)
    Z2 = at_xz(x, (z + 2) % 4)

    def rc(src, dst, ss, rr, dev):
        return pltpu.make_async_remote_copy(
            src_ref=src, dst_ref=dst, send_sem=ss, recv_sem=rr, device_id=dev, device_id_type=MESH
        )

    pairs = [
        (tokens, tok_v), (wq, wq_v), (wk, wk_v), (wv, wv_v), (wo, wo_v), (wu, wu_v), (wd, wd_v), (hcot, hc),
        (tcot, v_tcot), (i_qb, v_qb), (i_vb, v_vb), (i_ob, v_ob), (i_g1, v_g1), (i_s1, v_s1), (i_ub, v_ub), (i_db, v_db),
        (i_g2, v_g2), (i_s2, v_s2), (i_tw, v_tw),
    ]
    loads = [pltpu.make_async_copy(a, b, ld_sem.at[i]) for i, (a, b) in enumerate(pairs)]
    for c in loads:
        c.start()
    L_TOK, L_WQ, L_WK, L_WV, L_WO, L_WU, L_WD, L_HC, *L_VEC = loads

    peers = (YN, SIB, NXT, PRV, XN, Z1, Z2)
    bar = pltpu.get_barrier_semaphore()
    for d in peers:
        pl.semaphore_signal(bar, inc=1, device_id=d, device_id_type=MESH)
    pl.semaphore_wait(bar, len(peers))

    r_first = 1 * F
    r_wor = r_first + T
    r_wos = r_wor + L
    r_bias = 2 * F
    r_cs = r_bias + T
    r_cr = r_cs + L
    SH = L // 4

    L_WO.wait()
    share = pl.multiple_of((2 * x + core) * SH, SH)
    share_x = pl.multiple_of((2 * (1 - x) + core) * SH, SH)
    share_s = pl.multiple_of((2 * x + 1 - core) * SH, SH)
    share_sx = pl.multiple_of((2 * (1 - x) + 1 - core) * SH, SH)
    G[r_wos : r_wos + SH, :] = wo_v[pl.ds(share, SH), :].astype(f32)

    def wor(s):
        return G.at[pl.ds(pl.multiple_of(r_wor + s, 32), SH)]

    wo_y = rc(G.at[pl.ds(r_wos, SH)], wor(share), y_s.at[0], y_r.at[0], YN)
    wo_y.start()
    wo_x = rc(wor(share), wor(share), wx_s.at[0], wx_r.at[0], XN)
    wo_x_in = rc(wor(share_x), wor(share_x), wx_s.at[0], wx_r.at[0], XN)
    wo_f = [
        rc(wor(share), wor(share), ws_s.at[0], ws_r.at[0], SIB),
        rc(wor(share_x), wor(share_x), ws_s.at[1], ws_r.at[1], SIB),
    ]
    wo_f_in = [
        rc(wor(share_s), wor(share_s), ws_s.at[0], ws_r.at[0], SIB),
        rc(wor(share_sx), wor(share_sx), ws_s.at[1], ws_r.at[1], SIB),
    ]

    for c in L_VEC:
        c.wait()
    vec[V_QV : V_QV + 1, 0:L] = v_qb[...].astype(f32).reshape(1, L)
    vec[V_QV : V_QV + 1, L : 2 * L] = v_vb[...].astype(f32).reshape(1, L)
    vec[V_OB : V_OB + 1, :] = v_ob[...].astype(f32).reshape(1, D)
    vec[V_G1 : V_G1 + 1, :] = v_g1[...].astype(f32).reshape(1, D)
    vec[V_S1 : V_S1 + 1, :] = v_s1[...].astype(f32).reshape(1, D)
    vec[V_DB : V_DB + 1, :] = v_db[...].astype(f32).reshape(1, D)
    vec[V_G2 : V_G2 + 1, :] = v_g2[...].astype(f32).reshape(1, D)
    vec[V_S2 : V_S2 + 1, :] = v_s2[...].astype(f32).reshape(1, D)
    vec[V_TW : V_TW + 1, :] = v_tw[...].astype(f32).reshape(1, D)
    vec[V_TB : V_TB + 1, :] = jnp.broadcast_to(i_tb[...].astype(f32).reshape(1, 1), (1, D))
    ubv[...] = v_ub[...].astype(f32).reshape(1, F)

    L_TOK.wait()
    L_WQ.wait()
    lane = lax.broadcasted_iota(jnp.int32, (T, L), 1)
    odd = (lane // HEAD_DIM) % 2
    qv = (nn(tok_v[...], wq_v[...]) + vec[V_QV : V_QV + 1, 0:L]).astype(bf16).astype(f32) * (HEAD_DIM**-0.5)
    for par in range(2):
        one = jnp.where(odd == par, qv, 0.0).astype(bf16)
        qz[par * T : (par + 1) * T, :] = one
        qTz[par * L : (par + 1) * L, :] = one.T
    L_WK.wait()
    kv = nn(tok_v[...], wk_v[...]).astype(bf16)
    kn[...] = kv
    kT[...] = kv.T
    L_WV.wait()
    vv = (nn(tok_v[...], wv_v[...]) + vec[V_QV : V_QV + 1, L : 2 * L]).astype(bf16)
    vn[...] = vv
    vT[...] = vv.T

    segf, padf = seg[...].astype(f32), pad[...].astype(f32)
    rows8 = jnp.concatenate([segf, padf, v_tcot[...].reshape(1, T), jnp.zeros((5, T), f32)], axis=0)
    col[...] = rows8.T
    for qc in range(2):
        ki = lax.broadcasted_iota(jnp.int32, (T, CH), 0)
        qi = lax.broadcasted_iota(jnp.int32, (T, CH), 1) + qc * CH
        same = col[:, 0:1] == segf[:, qc * CH : (qc + 1) * CH]
        allowed = same & ((col[:, 1:2] == 0.0) | (ki == qi))
        G[r_bias : r_bias + T, qc * CH : (qc + 1) * CH] = jnp.where(allowed, 0.0, -1e9)

    def ctx_copy(qc):
        cols = pl.ds(qc * CH, CH)
        return rc(
            G.at[pl.ds(r_cs, L), cols], G.at[pl.ds(r_cr, L), cols], y_s.at[1 + qc], y_r.at[1 + qc], YN
        )

    def attend(qc):
        cols = pl.ds(qc * CH, CH)

        def body(hp, _):
            blk = pl.ds(pl.multiple_of(hp * 128, 128), 128)
            for par in range(2):
                qrows = pl.ds(pl.multiple_of(par * L + hp * 128, 128), 128)
                head = pl.multiple_of(hp * 128 + par * HEAD_DIM, HEAD_DIM)
                s = nn(kn[:, blk], qTz[qrows, cols]) + G[r_bias : r_bias + T, cols]
                e = jnp.exp(s - jnp.max(s, axis=0, keepdims=True))
                p = (e * (1.0 / colsum(e))).astype(bf16)
                pm[hp, :, pl.ds(par * T + qc * CH, CH)] = p
                c = nn(vT[pl.ds(head, HEAD_DIM), :], p).astype(bf16)
                ctxT[pl.ds(head, HEAD_DIM), cols] = c
                G[pl.ds(pl.multiple_of(r_cs + head, HEAD_DIM), HEAD_DIM), cols] = c.astype(f32)
            return 0

        lax.fori_loop(0, NP, body, 0)

    attend(0)
    ctx_copy(0).start()
    wo_y.wait_recv()
    wo_x.start()
    wo_f[0].start()
    attend(1)
    ctx_copy(1).start()
    wo_x_in.wait_recv()
    wo_f[1].start()

    def attn_ln(qc):
        c0 = qc * CH
        cols = pl.ds(c0, CH)
        ctx_copy(qc).wait_recv()
        other = G[r_cr : r_cr + L, cols].astype(bf16)
        bs[c0 : c0 + CH, :] = tn(ctxT[:, cols], wo_v[...]) + tn(other, woo_v[...])

        def body(i, _):
            rows = pl.ds(pl.multiple_of(c0 + i * PC, PC), PC)
            res = tok_v[rows, :].astype(f32) + bs[rows, :] + vec[V_OB : V_OB + 1, :]
            cen = res - rowmean(res)
            rstd = lax.rsqrt(rowmean(cen * cen) + EPS)
            xv = cen * rstd
            xh[rows, :] = xv
            rs[rows, :] = jnp.broadcast_to(rstd, (PC, 128))
            first = xv * vec[V_G1 : V_G1 + 1, :] + vec[V_S1 : V_S1 + 1, :]
            G[pl.ds(pl.multiple_of(r_first + c0 + i * PC, PC), PC), :] = first
            fl[rows, :] = first.astype(bf16)
            return 0

        lax.fori_loop(0, CH // PC, body, 0)

    def ffn(qc):
        rows = pl.ds(qc * CH, CH)
        bs[rows, :] = jnp.zeros((CH, D), f32)

        def body(fb, _):
            cols = pl.ds(pl.multiple_of(fb * FB, FB), FB)
            u = nn(fl[rows, :], wu_v[:, cols]) + ubv[:, cols]
            ph = 0.5 + 0.5 * lax.erf(u * 0.7071067811865476)
            a = (u * ph).astype(bf16)
            act[rows, cols] = a
            gp[rows, cols] = (ph + u * (jnp.exp(-0.5 * u * u) * 0.3989422804014327)).astype(bf16)
            bs[rows, :] += nn(a, wd_v[cols, :])
            return 0

        lax.fori_loop(0, F // FB, body, 0)

    def piece(buf, i):
        return buf.at[pl.ds(pl.multiple_of(i * PC, PC), PC)]

    def y_piece(dst, first_sem, i):
        return rc(piece(bs, i), piece(dst, i), y_s.at[first_sem + i], y_r.at[first_sem + i], YN)

    Y_BR, Y_FP, Y_TP = 3, 3 + NPC, 3 + 2 * NPC

    for c in wo_f_in:
        c.wait_recv()
    woo_v[...] = G[r_wor : r_wor + L, :].astype(bf16)
    L_WU.wait()
    L_WD.wait()
    for qc in range(2):
        attn_ln(qc)
        ffn(qc)
        for i in range(2 * qc, 2 * qc + 2):
            y_piece(br, Y_BR, i).start()
    wo_y.wait_send()
    wo_x.wait_send()
    for c in wo_f:
        c.wait_send()
    for qc in range(2):
        ctx_copy(qc).wait_send()

    sm[0] = jnp.zeros((16, D), f32)
    L_HC.wait()

    def tail(i, _):
        rows = pl.ds(pl.multiple_of(i * PC, PC), PC)
        y_piece(br, Y_BR, i).wait_recv()
        first = G[pl.ds(pl.multiple_of(r_first + i * PC, PC), PC), :]
        res = first + (bs[rows, :] + br[rows, :]) + vec[V_DB : V_DB + 1, :]
        cen = res - rowmean(res)
        rstd = lax.rsqrt(rowmean(cen * cen) + EPS)
        xv = cen * rstd
        g2 = vec[V_G2 : V_G2 + 1, :]
        tw = vec[V_TW : V_TW + 1, :]
        second = xv * g2 + vec[V_S2 : V_S2 + 1, :]
        hid[rows, :] = second.astype(bf16)
        v = jnp.sum(second * tw, axis=-1, keepdims=True) + vec[V_TB : V_TB + 1, 0:1]
        keep = 1.0 - col[rows, 1:2]
        soft = jnp.maximum(v, 0.0) + jnp.log1p(jnp.exp(-jnp.abs(v)))
        trm[rows, :] = jnp.broadcast_to(soft * keep, (PC, 8))
        dterm = col[rows, 2:3] * keep * lax.logistic(v)
        dsec = hc[rows, :] + dterm * tw
        sm[0, G_G2 : G_G2 + 1, :] += colsum(dsec * xv)
        sm[0, G_S2 : G_S2 + 1, :] += colsum(dsec)
        sm[0, G_TW : G_TW + 1, :] += colsum(dterm * second)
        sm[0, G_TB : G_TB + 1, :] += jnp.broadcast_to(colsum(dterm), (1, D))
        dx = dsec * g2
        dr = rstd * (dx - rowmean(dx) - xv * rowmean(dx * xv))
        hc[rows, :] = dr
        low = dr.astype(bf16)
        db[rows, :] = low
        sm[0, G_DB : G_DB + 1, :] += colsum(low.astype(f32))
        return 0

    lax.fori_loop(0, NPC, tail, 0)

    def chunk(b, j):
        return pl.ds(pl.multiple_of(b * SUB + core * HALF + j * CK, 8), CK)

    def chunk_s(b, j):
        return pl.ds(pl.multiple_of(b * SUB + (1 - core) * HALF + j * CK, 8), CK)

    def mine(b, j):
        return G[chunk(b, j), :] + S[b, pl.ds(pl.multiple_of(j * CK, 8), CK), :]

    def sib_copy(b):
        src = G.at[pl.ds(pl.multiple_of(b * SUB + (1 - core) * HALF, 8), HALF)]
        return rc(src, S.at[b], sib_s.at[b], sib_r.at[b], SIB)

    def rs_copy(b, k):
        src = G.at[chunk(b, vp)] if k == 0 else R.at[b, k - 1]
        return rc(src, R.at[b, k], rs_s.at[b, k], rs_r.at[b, k], NXT)

    def ag_copy(b, k):
        rows = chunk(b, (vp + 1 - k + RING) % RING)
        return rc(G.at[rows], G.at[rows], ag_s.at[b, k], ag_r.at[b, k], NXT)

    def ag_in(b, k):
        rows = chunk(b, (vp - k + RING) % RING)
        return rc(G.at[rows], G.at[rows], ag_s.at[b, k], ag_r.at[b, k], NXT)

    def fw_copy(b, k):
        rows = chunk(b, (vp + 1 - k + RING) % RING)
        return rc(G.at[rows], G.at[rows], fw_s.at[b, k], fw_r.at[b, k], SIB)

    def fw_in(b, k):
        rows = chunk_s(b, (vps + 1 - k + RING) % RING)
        return rc(G.at[rows], G.at[rows], fw_s.at[b, k], fw_r.at[b, k], SIB)

    def give(sem, dev):
        pl.semaphore_signal(sem, inc=1, device_id=dev, device_id_type=MESH)

    def event(b, e):
        if e == 0:
            sib_copy(b).start()
        elif e == 1:
            sib_copy(b).wait_recv()
            G[chunk(b, vp), :] = mine(b, vp)
            rs_copy(b, 0).start()
            sib_copy(b).wait_send()
            give(free_sib.at[b], SIB)
        elif e < RING:
            k = e - 1
            rs_copy(b, k - 1).wait_recv()
            R[b, k - 1] += mine(b, (vp - k + RING) % RING)
            rs_copy(b, k).start()
            if k == 1:
                rs_copy(b, 0).wait_send()
                give(free_ring.at[b], PRV)
        elif e == RING:
            rs_copy(b, RING - 2).wait_recv()
            j = (vp + 1) % RING
            G[chunk(b, j), :] = R[b, RING - 2] + mine(b, j)
            pl.semaphore_wait(free_ring.at[b], 1)
            ag_copy(b, 0).start()
            pl.semaphore_wait(free_sib.at[b], 1)
            fw_copy(b, 0).start()
        elif e < 2 * RING:
            k = e - RING
            ag_in(b, k - 1).wait_recv()
            if k < RING - 1:
                ag_copy(b, k).start()
            fw_copy(b, k).start()

    def finish(b):
        for k in range(RING - 1):
            if k:
                rs_copy(b, k).wait_send()
            ag_copy(b, k).wait_send()
        for k in range(RING):
            fw_copy(b, k).wait_send()
            fw_in(b, k).wait_recv()

    queue = deque()

    def start_batch(b):
        event(b, 0)
        queue.append((b, 1))

    def pump(n):
        for _ in range(n):
            if not queue:
                return
            b, e = queue.popleft()
            event(b, e)
            if e + 1 < 2 * RING:
                queue.append((b, e + 1))

    for b in range(4):
        G[b * SUB : (b + 1) * SUB, :] = tn(act[:, b * SUB : (b + 1) * SUB], db[...])
        start_batch(b)

    for i in range(NPC):
        y_piece(br, Y_BR, i).wait_send()

    def ffn_back(qc):
        rows = pl.ds(qc * CH, CH)
        bs[rows, :] = jnp.zeros((CH, D), f32)

        def body(fb, _):
            cols = pl.ds(pl.multiple_of(fb * FB, FB), FB)
            low = (nt(db[rows, :], wd_v[cols, :]) * gp[rows, cols].astype(f32)).astype(bf16)
            du[rows, cols] = low
            bs[rows, :] += nt(low, wu_v[:, cols])
            return 0

        lax.fori_loop(0, F // FB, body, 0)

    for qc in range(2):
        ffn_back(qc)
        for i in range(2 * qc, 2 * qc + 2):
            y_piece(fr, Y_FP, i).start()
        pump(2)

    for b in range(4):
        rows, cols = b % 2 * SUB, b // 2 * D
        G[(4 + b) * SUB : (5 + b) * SUB, :] = tn(fl[:, rows : rows + SUB], du[:, cols : cols + D])
        start_batch(4 + b)
        pump(2)
    for h in range(F // D):
        sm[0, G_UB0 + h : G_UB0 + h + 1, :] = colsum(du[:, h * D : (h + 1) * D].astype(f32))

    pump(7)

    def norm_back(i, _):
        rows = pl.ds(pl.multiple_of(i * PC, PC), PC)
        y_piece(fr, Y_FP, i).wait_recv()
        dfirst = hc[rows, :] + (bs[rows, :] + fr[rows, :])
        xv = xh[rows, :]
        sm[0, G_G1 : G_G1 + 1, :] += colsum(dfirst * xv)
        sm[0, G_S1 : G_S1 + 1, :] += colsum(dfirst)
        dx = dfirst * vec[V_G1 : V_G1 + 1, :]
        dr = rs[rows, 0:1] * (dx - rowmean(dx) - xv * rowmean(dx * xv))
        hc[rows, :] = dr
        low = dr.astype(bf16)
        db[rows, :] = low
        sm[0, G_OB : G_OB + 1, :] += colsum(low.astype(f32))
        return 0

    for i in range(NPC):
        norm_back(i, 0)
        pump(11 if i < NPC - 1 else 1)

    dc = nt(db[...], wo_v[...])
    for par in range(2):
        one = jnp.where(odd == par, dc, 0.0).astype(bf16)
        dcz[par * T : (par + 1) * T, :] = one
        dcTz[par * L : (par + 1) * L, :] = one.T
    pump(1)

    def attend_back(hp, _):
        blk = pl.ds(pl.multiple_of(hp * 128, 128), 128)
        for par in range(2):
            qrows = pl.ds(pl.multiple_of(par * L + hp * 128, 128), 128)
            head = pl.ds(pl.multiple_of(hp * 128 + par * HEAD_DIM, HEAD_DIM), HEAD_DIM)
            for qc in range(2):
                pcols = pl.ds(par * T + qc * CH, CH)
                dp = nn(vn[:, blk], dcTz[qrows, qc * CH : (qc + 1) * CH])
                p = pm[hp, :, pcols].astype(f32)
                t = dp * p
                dsb[:, pcols] = (t - p * colsum(t)).astype(bf16)
            d = nn(kT[head, :], dsb[:, par * T : (par + 1) * T]) * (HEAD_DIM**-0.5)
            dqT[head, :] = d.astype(bf16)
        dk[:, blk] = nn(dsb[...], qz[:, blk]).astype(bf16)
        dv[:, blk] = nn(pm[hp], dcz[:, blk]).astype(bf16)
        return 0

    for hp in range(NP):
        attend_back(hp, 0)
        pump(3)
    dq[...] = dqT[...].T

    for i in range(NPC):
        y_piece(fr, Y_FP, i).wait_send()
    for qc in range(2):
        rows = pl.ds(qc * CH, CH)
        bs[rows, :] = nt(dq[rows, :], wq_v[...]) + nt(dk[rows, :], wk_v[...]) + nt(dv[rows, :], wv_v[...])
        for i in range(2 * qc, 2 * qc + 2):
            y_piece(br, Y_TP, i).start()
    pump(2)
    G[8 * SUB : 9 * SUB, :] = nn(ctxT[...], db[...])
    start_batch(8)
    for b in range(2):
        half = pl.ds(b * SUB, SUB)
        G[(9 + b) * SUB : (10 + b) * SUB, 0:L] = tn(tok_v[:, half], dq[...])
        G[(9 + b) * SUB : (10 + b) * SUB, L : 2 * L] = tn(tok_v[:, half], dk[...])
        start_batch(9 + b)
        pump(2)
    for b in range(2):
        G[11 * SUB : 12 * SUB, b * L : (b + 1) * L] = tn(tok_v[:, b * SUB : (b + 1) * SUB], dv[...])
    start_batch(11)
    pump(2)

    sm[0, G_QV : G_QV + 1, 0:L] = colsum(dq[...].astype(f32))
    sm[0, G_QV : G_QV + 1, L : 2 * L] = colsum(dv[...].astype(f32))

    def sm_copy(k):
        return rc(sm.at[k], smr.at[k], sm_s.at[k], sm_r.at[k], (SIB, XN, Z1, Z2)[k])

    for k in range(4):
        sm_copy(k).start()
        pump(4)
        sm_copy(k).wait()
        if k < 3:
            sm[k + 1] = sm[k] + smr[k]
        else:
            smt[...] = sm[k] + smr[k]
    o_term[...] = trm[...].T

    for i in range(NPC):
        pump(10)
        rows = pl.ds(i * PC, PC)
        y_piece(br, Y_TP, i).wait_recv()
        hc[rows, :] += bs[rows, :] + br[rows, :]
    pump(BATCHES * 2 * RING)
    for b in range(BATCHES):
        finish(b)
    for i in range(NPC):
        y_piece(br, Y_TP, i).wait_send()


def spread(
    G, hc, hid, term, smt,
    o_hid, o_term, o_tok, o_wq, o_qb, o_wk, o_wv, o_vb, o_wo, o_ob, o_g1, o_s1, o_wu, o_ub, o_wd, o_db, o_g2, o_s2, o_tw,
    o_tb,
    sem,
):
    D, L = o_wq.shape
    F = o_wu.shape[1]

    def g(r, n, c0=0, c1=D):
        return G.at[pl.ds(r, n), pl.ds(c0, c1 - c0)]

    q = 2 * F + L
    copies = [(g(0, F), o_wd)]
    copies += [(g(F + h * D, D), o_wu.at[:, pl.ds(h * D, D)]) for h in range(F // D)]
    copies += [
        (hc, o_tok), (hid, o_hid), (g(2 * F, L), o_wo), (g(q, D, 0, L), o_wq), (g(q, D, L, 2 * L), o_wk),
        (g(q + D, L, 0, L), o_wv.at[pl.ds(0, L)]), (g(q + D, L, L, 2 * L), o_wv.at[pl.ds(L, L)]),
    ]
    started = [pltpu.make_async_copy(a, b, sem.at[i]) for i, (a, b) in enumerate(copies)]
    for c in started:
        c.start()
    o_term[...] = term[0, :]
    o_qb[...] = smt[G_QV, 0:L]
    o_vb[...] = smt[G_QV, L : 2 * L]
    o_ob[...] = smt[G_OB, :]
    o_g1[...] = smt[G_G1, :]
    o_s1[...] = smt[G_S1, :]
    o_ub[...] = jnp.concatenate([smt[G_UB0 + h : G_UB0 + h + 1, :] for h in range(F // D)], axis=1).reshape(F)
    o_db[...] = smt[G_DB, :]
    o_g2[...] = smt[G_G2, :]
    o_s2[...] = smt[G_S2, :]
    o_tw[...] = smt[G_TW, :]
    o_tb[...] = smt[G_TB : G_TB + 1, 0:1].reshape(1)
    for c in started:
        c.wait()


def per_device(
    tokens, segment_ids, pad_flags, query_weight, query_bias, key_weight, value_weight, value_bias, output_weight,
    output_bias, first_gain, first_shift, up_weight, up_bias, down_weight, down_bias, second_gain, second_shift,
    term_weight, term_bias, hidden_cot, term_cot, *, groups,
):
    T, D = tokens.shape
    L, F = query_weight.shape[1], up_weight.shape[1]
    anywhere, vmem = pl.BlockSpec(memory_space=pl.ANY), pl.BlockSpec(memory_space=pltpu.VMEM)
    sub = 3 * F // BATCHES
    dma = pltpu.SemaphoreType.DMA
    V = pltpu.VMEM
    G, hc, hid, term, smt = pl.pallas_call(
        kernel,
        out_shape=[V((3 * F, D), f32), V((T, D), f32), V((T, D), bf16), V((8, T), f32), V((16, D), f32)],
        in_specs=[anywhere, vmem, vmem] + [anywhere] * 11 + [vmem] + [anywhere] * 7,
        out_specs=[vmem] * 5,
        scratch_shapes=[
            V((T,), f32), V((L,), bf16), V((L,), bf16), V((D,), bf16), V((D,), bf16), V((D,), bf16), V((F,), bf16),
            V((D,), bf16), V((D,), bf16), V((D,), bf16), V((D,), bf16), V((16, D), f32), V((1, F), f32),
            V((T, D), bf16), V((D, L), bf16), V((D, L), bf16), V((D, L), bf16), V((L, D), bf16), V((L, D), bf16),
            V((D, F), bf16), V((F, D), bf16),
            V((T, L), bf16), V((T, L), bf16), V((L, T), bf16), V((L, T), bf16),
            V((2 * T, L), bf16), V((2 * L, T), bf16), V((L // 128, T, 2 * T), bf16), V((L, T), bf16),
            V((T, D), f32), V((T, 128), f32), V((T, D), bf16),
            V((T, F), bf16), V((T, F), bf16), V((T, D), f32), V((T, D), f32), V((T, D), f32),
            V((T, D), bf16), V((T, F), bf16),
            V((2 * T, L), bf16), V((2 * L, T), bf16), V((T, 2 * T), bf16), V((L, T), bf16),
            V((T, L), bf16), V((T, L), bf16), V((T, L), bf16), V((T, 8), f32), V((T, 8), f32),
            V((4, 16, D), f32), V((4, 16, D), f32),
            V((BATCHES, sub // 2, D), f32), V((BATCHES, RING - 1, sub // 2 // RING, D), f32),
            dma((19,)), dma((15,)), dma((15,)), dma((1,)), dma((1,)), dma((2,)), dma((2,)), dma((4,)), dma((4,)),
            dma((BATCHES,)), dma((BATCHES,)), dma((BATCHES, RING - 1)), dma((BATCHES, RING - 1)),
            dma((BATCHES, RING - 1)), dma((BATCHES, RING - 1)), dma((BATCHES, RING)), dma((BATCHES, RING)),
            pltpu.SemaphoreType.REGULAR((BATCHES,)), pltpu.SemaphoreType.REGULAR((BATCHES,)),
        ],
        compiler_params=pltpu.CompilerParams(
            collective_id=0, has_side_effects=True, vmem_limit_bytes=VMEM_LIMIT
        ),
    )(
        tokens, segment_ids, pad_flags, term_cot, query_bias, value_bias, output_bias, first_gain, first_shift, up_bias,
        down_bias, second_gain, second_shift, term_weight, term_bias, query_weight, key_weight, value_weight,
        output_weight, up_weight, down_weight, hidden_cot,
    )
    vector = [jax.ShapeDtypeStruct((n,), f32) for n in (D, L, F, T, 1)]
    vd, vl, vf, vt, v1 = vector
    dl = jax.ShapeDtypeStruct((D, L), f32)
    outs = pl.pallas_call(
        spread,
        out_shape=[
            jax.ShapeDtypeStruct((T, D), bf16), vt, jax.ShapeDtypeStruct((T, D), f32), dl, vl, dl, dl, vl,
            jax.ShapeDtypeStruct((L, D), f32), vd, vd, vd, jax.ShapeDtypeStruct((D, F), f32), vf,
            jax.ShapeDtypeStruct((F, D), f32), vd, vd, vd, vd, v1,
        ],
        in_specs=[vmem] * 5,
        out_specs=[
            anywhere, vmem, anywhere, anywhere, vmem, anywhere, anywhere, vmem, anywhere, vmem, vmem, vmem, anywhere, vmem,
            anywhere, vmem, vmem, vmem, vmem, vmem,
        ],
        scratch_shapes=[dma((16,))],
        compiler_params=pltpu.CompilerParams(vmem_limit_bytes=2**20),
    )(G, hc, hid, term, smt)
    if groups > 1:
        outs = list(outs[:3]) + list(lax.psum(tuple(v * (1.0 / GROUP) for v in outs[3:]), "dp"))
    return tuple(outs)


def solution(mesh):
    rows, cols, vec = P("dp", None), P(None, "mp"), P("mp")
    return jax.shard_map(
        partial(per_device, groups=mesh.shape["dp"] // GROUP),
        mesh=mesh,
        in_specs=(
            rows, rows, rows, cols, vec, cols, cols, vec, P("mp", None), P(), P(), P(), cols, vec, P("mp", None), P(), P(),
            P(), P(), P(), rows, P("dp"),
        ),
        out_specs=(
            rows, P("dp"), rows, cols, vec, cols, cols, vec, P("mp", None), P(), P(), P(), cols, vec, P("mp", None), P(),
            P(), P(), P(), P(),
        ),
        check_vma=False,
    )
```

```python
from collections import deque
from functools import partial

import jax
import jax.numpy as jnp
from jax import lax
from jax.experimental import pallas as pl
from jax.experimental.pallas import tpu as pltpu
from jax.sharding import PartitionSpec as P

HEAD_DIM = 64
EPS = 1e-06
GROUP = 16
RING = 8
BATCHES = 12
MESH = pl.DeviceIdType.MESH
PUMPS = (2, 2, 5, 10, 3, 2, 4, 10)
VMEM_LIMIT = 47 * 2**20
bf16, f32 = jnp.bfloat16, jnp.float32

V_QV, V_OB, V_G1, V_S1, V_DB, V_G2, V_S2, V_TW, V_TB = range(9)
G_QV, G_OB, G_G1, G_S1, G_UB0, G_UB1, G_DB, G_G2, G_S2, G_TW, G_TB = range(11)


def nn(a, b):
    return jnp.dot(a, b, preferred_element_type=f32)


def nt(a, b):
    return lax.dot_general(a, b, (((1,), (1,)), ((), ())), preferred_element_type=f32)


def tn(a, b):
    return lax.dot_general(a, b, (((0,), (0,)), ((), ())), preferred_element_type=f32)


def colsum(v):
    return jnp.sum(v, axis=0, keepdims=True)


def rowmean(v):
    return jnp.mean(v, axis=-1, keepdims=True)


def kernel(
    tokens, i_seg, i_pad, tcot, i_qb, i_vb, i_ob, i_g1, i_s1, i_ub, i_db, i_g2, i_s2, i_tw, i_tb, wq, wk, wv, wo, wu, wd, hcot,
    G, hc, hid, o_term, smt,
    v_tcot, v_qb, v_vb, v_ob, v_g1, v_s1, v_ub, v_db, v_g2, v_s2, v_tw, v_tb, seg, pad, vec, ubv,
    tok_v, wq_v, wk_v, wv_v, wo_v, woo_v, wu_v, wd_v,
    kn, vn, kT, vT, qz, qTz, pm, ctxT, xh, rs, first_v, fl, gp, act, bs, br, fr, db, du,
    dcz, dcTz, dqT, col, trm, sm, smr, S, R,
    ld_sem, y_s, y_r, wo_s, wo_r, sm_s, sm_r, sib_s, sib_r, ring_s, ring_r, fw_s, fw_r, free_sib,
):
    T, D = tokens.shape
    L, F = wq.shape[1], wu.shape[1]
    NP = L // 128
    CH, PC, FB = T // 2, T // 4, 512
    NPC = T // PC
    SUB = G.shape[0] // BATCHES
    HALF, CK = SUB // 2, SUB // 2 // RING

    me, mp = lax.axis_index("dp"), lax.axis_index("mp")
    base, rank = me // GROUP * GROUP, me % GROUP
    core, chip = rank % 2, rank // 2
    x, z = chip % 2, chip // 2
    pos = jnp.where(x == 0, z, RING - 1 - z)
    vp = jnp.where(core == 0, pos, (RING - pos) % RING)

    def at_vp(v):
        p = jnp.where(core == 0, v, (RING - v) % RING)
        c = jnp.where(p < RING // 2, 2 * p, 2 * (RING - 1 - p) + 1)
        return (base + 2 * c + core, mp)

    def at_xz(ax, az):
        return (base + 2 * (2 * az + ax) + core, mp)

    YN = (me, 1 - mp)
    SIB = (base + 2 * chip + 1 - core, mp)
    NXT, PRV = at_vp((vp + 1) % RING), at_vp((vp + RING - 1) % RING)
    XN = at_xz(1 - x, z)
    Z1 = at_xz(x, z // 2 * 2 + 1 - z % 2)
    Z2 = at_xz(x, (z + 2) % 4)

    def rc(src, dst, ss, rr, dev):
        return pltpu.make_async_remote_copy(
            src_ref=src, dst_ref=dst, send_sem=ss, recv_sem=rr, device_id=dev, device_id_type=MESH
        )

    pairs = [
        (wo, wo_v), (tokens, tok_v), (wq, wq_v), (wk, wk_v), (wv, wv_v), (wu, wu_v), (wd, wd_v), (hcot, hc),
        (tcot, v_tcot), (i_qb, v_qb), (i_vb, v_vb), (i_ob, v_ob), (i_g1, v_g1), (i_s1, v_s1), (i_ub, v_ub), (i_db, v_db),
        (i_g2, v_g2), (i_s2, v_s2), (i_tw, v_tw), (i_tb, v_tb), (i_seg, seg), (i_pad, pad),
    ]
    loads = [pltpu.make_async_copy(a, b, ld_sem.at[i]) for i, (a, b) in enumerate(pairs)]
    for c in loads:
        c.start()
    L_WO, L_TOK, L_WQ, L_WK, L_WV, L_WU, L_WD, L_HC, *L_VEC = loads

    peers = (YN, SIB, NXT, PRV, XN, Z1, Z2)
    bar = pltpu.get_barrier_semaphore()
    for d in peers:
        pl.semaphore_signal(bar, inc=1, device_id=d, device_id_type=MESH)
    pl.semaphore_wait(bar, len(peers))

    r_wor = 4 * SUB
    r_wos = r_wor + L
    r_bias = 8 * SUB
    r_cs = r_bias + T
    r_cr = r_cs + L
    SH = L // 8

    def wor(ax, az, ac):
        return G.at[pl.ds(pl.multiple_of(r_wor + ((az * 2 + ax) * 2 + ac) * SH, 16), SH)]

    zp = z % 2
    L_WO.wait()
    G[r_wos : r_wos + SH, :] = wo_v[pl.ds(pl.multiple_of(((zp * 2 + x) * 2 + core) * SH, 16), SH), :].astype(f32)

    def wo_copy(k):
        ax, az = ((x, zp), (x, zp), (x, zp), (1 - x, zp), (x, zp), (1 - x, zp), (x, 1 - zp), (1 - x, 1 - zp))[k]
        place = wor(ax, az, core)
        if k == 0:
            return rc(G.at[pl.ds(r_wos, SH)], place, y_s.at[0], y_r.at[0], YN)
        return rc(place, place, wo_s, wo_r.at[min(k, 4) - 1], (XN, Z1, Z1, SIB, SIB, SIB, SIB)[k - 1])

    wo_copy(0).start()

    for c in L_VEC:
        c.wait()
    vec[V_QV : V_QV + 1, 0:L] = v_qb[...].astype(f32).reshape(1, L)
    vec[V_QV : V_QV + 1, L : 2 * L] = v_vb[...].astype(f32).reshape(1, L)
    vec[V_OB : V_OB + 1, :] = v_ob[...].astype(f32).reshape(1, D)
    vec[V_G1 : V_G1 + 1, :] = v_g1[...].astype(f32).reshape(1, D)
    vec[V_S1 : V_S1 + 1, :] = v_s1[...].astype(f32).reshape(1, D)
    vec[V_DB : V_DB + 1, :] = v_db[...].astype(f32).reshape(1, D)
    vec[V_G2 : V_G2 + 1, :] = v_g2[...].astype(f32).reshape(1, D)
    vec[V_S2 : V_S2 + 1, :] = v_s2[...].astype(f32).reshape(1, D)
    vec[V_TW : V_TW + 1, :] = v_tw[...].astype(f32).reshape(1, D)
    vec[V_TB : V_TB + 1, :] = jnp.broadcast_to(v_tb[...].astype(f32).reshape(1, 1), (1, D))
    ubv[...] = v_ub[...].astype(f32).reshape(1, F)

    L_TOK.wait()
    L_WQ.wait()
    lane = lax.broadcasted_iota(jnp.int32, (T, L), 1)
    odd = (lane // HEAD_DIM) % 2
    qv = (nn(tok_v[...], wq_v[...]) + vec[V_QV : V_QV + 1, 0:L]).astype(bf16).astype(f32) * (HEAD_DIM**-0.5)
    for par in range(2):
        one = jnp.where(odd == par, qv, 0.0).astype(bf16)
        qz[par * T : (par + 1) * T, :] = one
        qTz[par * L : (par + 1) * L, :] = one.T
    L_WK.wait()
    kv = nn(tok_v[...], wk_v[...]).astype(bf16)
    kn[...] = kv
    kT[...] = kv.T
    L_WV.wait()
    vv = (nn(tok_v[...], wv_v[...]) + vec[V_QV : V_QV + 1, L : 2 * L]).astype(bf16)
    vn[...] = vv
    vT[...] = vv.T

    segf, padf = seg[...].astype(f32), pad[...].astype(f32)
    rows8 = jnp.concatenate([segf, padf, v_tcot[...].reshape(1, T), jnp.zeros((5, T), f32)], axis=0)
    col[...] = rows8.T
    for qc in range(T // CH):
        ki = lax.broadcasted_iota(jnp.int32, (T, CH), 0)
        qi = lax.broadcasted_iota(jnp.int32, (T, CH), 1) + qc * CH
        same = col[:, 0:1] == segf[:, qc * CH : (qc + 1) * CH]
        allowed = same & ((col[:, 1:2] == 0.0) | (ki == qi))
        G[r_bias : r_bias + T, qc * CH : (qc + 1) * CH] = jnp.where(allowed, 0.0, -1e9)

    Y_CTX, Y_BR, Y_FP, Y_TP = 1, 1 + NPC, 1 + 2 * NPC, 1 + 3 * NPC

    def span(i):
        return pl.ds(pl.multiple_of(i * PC, PC), PC)

    def ctx_copy(i):
        return rc(G.at[pl.ds(r_cs, L), span(i)], G.at[pl.ds(r_cr, L), span(i)], y_s.at[1], y_r.at[Y_CTX + i], YN)

    def attend(i):
        def body(hp, _):
            blk = pl.ds(pl.multiple_of(hp * 128, 128), 128)
            for par in range(2):
                qrows = pl.ds(pl.multiple_of(par * L + hp * 128, 128), 128)
                head = pl.multiple_of(hp * 128 + par * HEAD_DIM, HEAD_DIM)
                s = nn(kn[:, blk], qTz[qrows, span(i)]) + G[r_bias : r_bias + T, span(i)]
                e = jnp.exp(s - jnp.max(s, axis=0, keepdims=True))
                p = (e * (1.0 / colsum(e))).astype(bf16)
                pm[hp, :, pl.ds(par * T + i * PC, PC)] = p
                c = nn(vT[pl.ds(head, HEAD_DIM), :], p).astype(bf16)
                ctxT[pl.ds(head, HEAD_DIM), span(i)] = c
                G[pl.ds(pl.multiple_of(r_cs + head, HEAD_DIM), HEAD_DIM), span(i)] = c.astype(f32)
            return 0

        lax.fori_loop(0, NP, body, 0)

    for i in range(NPC):
        attend(i)
        ctx_copy(i).start()
        if i == 1:
            wo_copy(0).wait_recv()
            for k in (1, 2, 4):
                wo_copy(k).start()
        if i == 3:
            wo_copy(1).wait_recv()
            for k in (3, 5):
                wo_copy(k).start()
    for k in (2, 3):
        wo_copy(k).wait_recv()
        wo_copy(k + 4).start()

    def piece(buf, i):
        return buf.at[span(i)]

    def y_piece(dst, which, i):
        return rc(piece(bs, i), piece(dst, i), y_s.at[which - 3 + i], y_r.at[which + i], YN)

    def y_sent(dst, which):
        for i in range(NPC):
            y_piece(dst, which, i).wait_send()

    L_WU.wait()
    L_WD.wait()
    some = G.at[pl.ds(r_wor, 4 * SH)]
    rc(some, some, wo_s, wo_r.at[3], SIB).wait_recv()
    woo_v[...] = G[r_wor : r_wor + L, :].astype(bf16)

    def forward(i, _):
        rows = span(i)
        ctx_copy(i).wait_recv()
        other = G[r_cr : r_cr + L, rows].astype(bf16)
        res = tok_v[rows, :].astype(f32) + (tn(ctxT[:, rows], wo_v[...]) + tn(other, woo_v[...])) + vec[V_OB : V_OB + 1, :]
        cen = res - rowmean(res)
        rstd = lax.rsqrt(rowmean(cen * cen) + EPS)
        xv = cen * rstd
        xh[rows, :] = xv
        rs[rows, :] = jnp.broadcast_to(rstd, (PC, 128))
        first = xv * vec[V_G1 : V_G1 + 1, :] + vec[V_S1 : V_S1 + 1, :]
        first_v[rows, :] = first
        fl[rows, :] = first.astype(bf16)
        bs[rows, :] = jnp.zeros((PC, D), f32)

        def body(fb, _):
            cols = pl.ds(pl.multiple_of(fb * FB, FB), FB)
            u = nn(fl[rows, :], wu_v[:, cols]) + ubv[:, cols]
            ph = 0.5 + 0.5 * lax.erf(u * 0.7071067811865476)
            a = (u * ph).astype(bf16)
            act[rows, cols] = a
            gp[rows, cols] = (ph + u * (jnp.exp(-0.5 * u * u) * 0.3989422804014327)).astype(bf16)
            bs[rows, :] += nn(a, wd_v[cols, :])
            return 0

        lax.fori_loop(0, F // FB, body, 0)
        y_piece(br, Y_BR, i).start()
        return 0

    lax.fori_loop(0, NPC, forward, 0)
    wo_copy(0).wait_send()
    some = G.at[pl.ds(r_wor, 7 * SH)]
    rc(some, some, wo_s, wo_r.at[3], SIB).wait_send()
    rc(G.at[pl.ds(r_cs, L), pl.ds(0, T)], G.at[pl.ds(r_cr, L), pl.ds(0, T)], y_s.at[1], y_r.at[Y_CTX], YN).wait_send()

    sm[0] = jnp.zeros((16, D), f32)
    L_HC.wait()

    def tail(i):
        rows = span(i)
        y_piece(br, Y_BR, i).wait_recv()
        first = first_v[rows, :]
        res = first + (bs[rows, :] + br[rows, :]) + vec[V_DB : V_DB + 1, :]
        cen = res - rowmean(res)
        rstd = lax.rsqrt(rowmean(cen * cen) + EPS)
        xv = cen * rstd
        g2 = vec[V_G2 : V_G2 + 1, :]
        tw = vec[V_TW : V_TW + 1, :]
        second = xv * g2 + vec[V_S2 : V_S2 + 1, :]
        hid[rows, :] = second.astype(bf16)
        v = jnp.sum(second * tw, axis=-1, keepdims=True) + vec[V_TB : V_TB + 1, 0:1]
        keep = 1.0 - col[rows, 1:2]
        soft = jnp.maximum(v, 0.0) + jnp.log1p(jnp.exp(-jnp.abs(v)))
        trm[rows, :] = jnp.broadcast_to(soft * keep, (PC, 8))
        dterm = col[rows, 2:3] * keep * lax.logistic(v)
        dsec = hc[rows, :] + dterm * tw
        sm[0, G_G2 : G_G2 + 1, :] += colsum(dsec * xv)
        sm[0, G_S2 : G_S2 + 1, :] += colsum(dsec)
        sm[0, G_TW : G_TW + 1, :] += colsum(dterm * second)
        sm[0, G_TB : G_TB + 1, :] += jnp.broadcast_to(colsum(dterm), (1, D))
        dx = dsec * g2
        dr = rstd * (dx - rowmean(dx) - xv * rowmean(dx * xv))
        hc[rows, :] = dr
        low = dr.astype(bf16)
        db[rows, :] = low
        sm[0, G_DB : G_DB + 1, :] += colsum(low.astype(f32))

    def ffn_back(i, between):
        rows = span(i)
        y_piece(br, Y_BR, i).wait_send()
        for fb in range(F // FB):
            cols = pl.ds(fb * FB, FB)
            low = (nt(db[rows, :], wd_v[cols, :]) * gp[rows, cols].astype(f32)).astype(bf16)
            du[rows, cols] = low
            part = nt(low, wu_v[:, cols])
            if fb == 0:
                bs[rows, :] = part
            else:
                bs[rows, :] += part
            between()
        y_piece(fr, Y_FP, i).start()

    def tail_back(i, _):
        tail(i)
        ffn_back(i, lambda: None)
        return 0

    early = (NPC - 1) * PC

    def down_grad(b, part):
        return tn(act[part, b * SUB : (b + 1) * SUB], db[part, :])

    def up_grad(b, part):
        rows, cols = b % 2 * SUB, b // 2 * D
        return tn(fl[part, rows : rows + SUB], du[part, cols : cols + D])

    lax.fori_loop(0, NPC - 1, tail_back, 0)
    for b in range(4):
        G[b * SUB : (b + 1) * SUB, :] = down_grad(b, pl.ds(0, early))
    for b in range(4):
        G[(4 + b) * SUB : (5 + b) * SUB, :] = up_grad(b, pl.ds(0, early))
    tail(NPC - 1)

    def chunk(b, j):
        return pl.ds(pl.multiple_of(b * SUB + core * HALF + j * CK, 8), CK)

    def own(b, j):
        return S.at[b, pl.ds(pl.multiple_of(j * CK, 8), CK)]

    def mine(b, j):
        return G[chunk(b, j), :] + own(b, j)[...]

    def sib_copy(b):
        src = G.at[pl.ds(pl.multiple_of(b * SUB + (1 - core) * HALF, 8), HALF)]
        return rc(src, S.at[b], sib_s.at[b], sib_r.at[b], SIB)

    def rs_copy(b, k):
        src = own(b, vp) if k == 0 else R.at[b, k - 1]
        return rc(src, R.at[b, k], ring_s, ring_r.at[b, k], NXT)

    def ag_copy(b, k, back):
        rows = G.at[chunk(b, (vp + 1 - back - k + RING) % RING)]
        return rc(rows, rows, ring_s, ring_r.at[b, k - 1 if k else RING - 1], NXT)

    def fw_copy(b, k):
        rows = G.at[chunk(b, (vp + 1 - k + RING) % RING)]
        return rc(rows, rows, fw_s, fw_r, SIB)

    def event(b, e):
        if e == 0:
            sib_copy(b).start()
        elif e == 1:
            sib_copy(b).wait_recv()
            own(b, vp)[...] += G[chunk(b, vp), :]
            rs_copy(b, 0).start()
            sib_copy(b).wait_send()
            pl.semaphore_signal(free_sib.at[b], inc=1, device_id=SIB, device_id_type=MESH)
        elif e < RING:
            k = e - 1
            rs_copy(b, k - 1).wait_recv()
            R[b, k - 1] += mine(b, (vp - k + RING) % RING)
            rs_copy(b, k).start()
        elif e == RING:
            rs_copy(b, RING - 2).wait_recv()
            j = (vp + 1) % RING
            G[chunk(b, j), :] = R[b, RING - 2] + mine(b, j)
            ag_copy(b, 0, 0).start()
            pl.semaphore_wait(free_sib.at[b], 1)
            fw_copy(b, 0).start()
        else:
            k = e - RING
            ag_copy(b, k - 1, 1).wait_recv()
            if k < RING - 1:
                ag_copy(b, k, 0).start()
            fw_copy(b, k).start()

    def finish():
        sent = G.at[pl.ds(0, BATCHES * 2 * (RING - 1) * CK)]
        rc(sent, sent, ring_s, ring_r.at[0, 0], NXT).wait_send()
        half = G.at[pl.ds(0, BATCHES * HALF)]
        rc(half, half, fw_s, fw_r, SIB).wait()

    queue = deque()

    def start_batch(b):
        event(b, 0)
        queue.append((b, 1))

    def pump(n):
        for _ in range(n):
            if not queue:
                return
            b, e = queue.popleft()
            event(b, e)
            if e + 1 < 2 * RING:
                queue.append((b, e + 1))

    last = pl.ds(early, PC)
    for b in range(4):
        G[b * SUB : (b + 1) * SUB, :] += down_grad(b, last)
        start_batch(b)
    ffn_back(NPC - 1, lambda: pump(PUMPS[0]))
    for b in range(4):
        G[(4 + b) * SUB : (5 + b) * SUB, :] += up_grad(b, last)
        start_batch(4 + b)
        pump(PUMPS[1])
    for h in range(F // D):
        sm[0, G_UB0 + h : G_UB0 + h + 1, :] = colsum(du[:, h * D : (h + 1) * D].astype(f32))

    pump(PUMPS[2])

    def norm_back(i, _):
        rows = span(i)
        y_piece(fr, Y_FP, i).wait_recv()
        dfirst = hc[rows, :] + (bs[rows, :] + fr[rows, :])
        xv = xh[rows, :]
        sm[0, G_G1 : G_G1 + 1, :] += colsum(dfirst * xv)
        sm[0, G_S1 : G_S1 + 1, :] += colsum(dfirst)
        dx = dfirst * vec[V_G1 : V_G1 + 1, :]
        dr = rs[rows, 0:1] * (dx - rowmean(dx) - xv * rowmean(dx * xv))
        hc[rows, :] = dr
        low = dr.astype(bf16)
        db[rows, :] = low
        sm[0, G_OB : G_OB + 1, :] += colsum(low.astype(f32))
        return 0

    for i in range(NPC):
        norm_back(i, 0)
        pump(PUMPS[3] if i < NPC - 1 else 1)

    dc = nt(db[...], wo_v[...])
    for par in range(2):
        one = jnp.where(odd == par, dc, 0.0).astype(bf16)
        dcz[par * T : (par + 1) * T, :] = one
        dcTz[par * L : (par + 1) * L, :] = one.T
    pump(1)

    dsb = act.at[:, pl.ds(0, 2 * T)]
    dq, dk, dv = (gp.at[:, pl.ds(k * L, L)] for k in range(3))

    def attend_back(hp, _):
        blk = pl.ds(pl.multiple_of(hp * 128, 128), 128)
        for par in range(2):
            qrows = pl.ds(pl.multiple_of(par * L + hp * 128, 128), 128)
            head = pl.ds(pl.multiple_of(hp * 128 + par * HEAD_DIM, HEAD_DIM), HEAD_DIM)
            for qc in range(2):
                pcols = pl.ds(par * T + qc * CH, CH)
                dp = nn(vn[:, blk], dcTz[qrows, qc * CH : (qc + 1) * CH])
                p = pm[hp, :, pcols].astype(f32)
                t = dp * p
                dsb[:, pcols] = (t - p * colsum(t)).astype(bf16)
            d = nn(kT[head, :], dsb[:, par * T : (par + 1) * T]) * (HEAD_DIM**-0.5)
            dqT[head, :] = d.astype(bf16)
        dk[:, blk] = nn(dsb[...], qz[:, blk]).astype(bf16)
        dv[:, blk] = nn(pm[hp], dcz[:, blk]).astype(bf16)
        return 0

    for hp in range(NP):
        attend_back(hp, 0)
        pump(PUMPS[4])
    dq[...] = dqT[...].T

    y_sent(fr, Y_FP)
    for qc in range(2):
        rows = pl.ds(qc * CH, CH)
        bs[rows, :] = nt(dq[rows, :], wq_v[...]) + nt(dk[rows, :], wk_v[...]) + nt(dv[rows, :], wv_v[...])
        for i in range(2 * qc, 2 * qc + 2):
            y_piece(br, Y_TP, i).start()
    pump(PUMPS[5])
    G[8 * SUB : 9 * SUB, :] = nn(ctxT[...], db[...])
    start_batch(8)
    for b in range(2):
        half = pl.ds(b * SUB, SUB)
        G[(9 + b) * SUB : (10 + b) * SUB, 0:L] = tn(tok_v[:, half], dq[...])
        G[(9 + b) * SUB : (10 + b) * SUB, L : 2 * L] = tn(tok_v[:, half], dk[...])
        start_batch(9 + b)
        pump(PUMPS[5])
    for b in range(2):
        G[11 * SUB : 12 * SUB, b * L : (b + 1) * L] = tn(tok_v[:, b * SUB : (b + 1) * SUB], dv[...])
    start_batch(11)
    pump(PUMPS[5])

    sm[0, G_QV : G_QV + 1, 0:L] = colsum(dq[...].astype(f32))
    sm[0, G_QV : G_QV + 1, L : 2 * L] = colsum(dv[...].astype(f32))

    def sm_copy(k):
        return rc(sm.at[k], smr.at[k], sm_s.at[k], sm_r.at[k], (SIB, XN, Z1, Z2)[k])

    for k in range(4):
        sm_copy(k).start()
        pump(PUMPS[6])
        sm_copy(k).wait()
        if k < 3:
            sm[k + 1] = sm[k] + smr[k]
        else:
            smt[...] = sm[k] + smr[k]
    o_term[...] = trm[...].T

    for i in range(NPC):
        pump(PUMPS[7])
        rows = pl.ds(i * PC, PC)
        y_piece(br, Y_TP, i).wait_recv()
        hc[rows, :] += bs[rows, :] + br[rows, :]
    pump(BATCHES * 2 * RING)
    finish()
    y_sent(br, Y_TP)


def spread(
    G, hc, hid, term, smt,
    o_hid, o_term, o_tok, o_wq, o_qb, o_wk, o_wv, o_vb, o_wo, o_ob, o_g1, o_s1, o_wu, o_ub, o_wd, o_db, o_g2, o_s2, o_tw,
    o_tb,
    sem, *small,
):
    D, L = o_wq.shape
    F = o_wu.shape[1]

    def g(r, n, c0=0, c1=D):
        return G.at[pl.ds(r, n), pl.ds(c0, c1 - c0)]

    q = 2 * F + L
    copies = [(g(0, F), o_wd)]
    copies += [(g(F + h * D, D), o_wu.at[:, pl.ds(h * D, D)]) for h in range(F // D)]
    copies += [
        (hc, o_tok), (hid, o_hid), (g(2 * F, L), o_wo), (g(q, D, 0, L), o_wq), (g(q, D, L, 2 * L), o_wk),
        (g(q + D, L, 0, L), o_wv.at[pl.ds(0, L)]), (g(q + D, L, L, 2 * L), o_wv.at[pl.ds(L, L)]),
    ]
    started = [pltpu.make_async_copy(a, b, sem.at[i]) for i, (a, b) in enumerate(copies)]
    for c in started:
        c.start()
    rows = [term[0, :], smt[G_QV, 0:L], smt[G_QV, L : 2 * L]]
    rows += [smt[r, :] for r in (G_OB, G_G1, G_S1, G_DB, G_G2, G_S2, G_TW)]
    rows.append(jnp.concatenate([smt[G_UB0 + h : G_UB0 + h + 1, :] for h in range(F // D)], axis=1).reshape(F))
    rows.append(smt[G_TB : G_TB + 1, 0:1].reshape(1))
    places = (o_term, o_qb, o_vb, o_ob, o_g1, o_s1, o_db, o_g2, o_s2, o_tw, o_ub, o_tb)
    for i, (row, held, place) in enumerate(zip(rows, small, places)):
        held[...] = row
        started.append(pltpu.make_async_copy(held, place, sem.at[len(copies) + i]))
        started[-1].start()
    for c in started:
        c.wait()


def per_device(
    tokens, segment_ids, pad_flags, query_weight, query_bias, key_weight, value_weight, value_bias, output_weight,
    output_bias, first_gain, first_shift, up_weight, up_bias, down_weight, down_bias, second_gain, second_shift,
    term_weight, term_bias, hidden_cot, term_cot, *, groups,
):
    T, D = tokens.shape
    L, F = query_weight.shape[1], up_weight.shape[1]
    anywhere, vmem = pl.BlockSpec(memory_space=pl.ANY), pl.BlockSpec(memory_space=pltpu.VMEM)
    sub = 3 * F // BATCHES
    dma = pltpu.SemaphoreType.DMA
    V = pltpu.VMEM
    G, hc, hid, term, smt = pl.pallas_call(
        kernel,
        out_shape=[V((3 * F, D), f32), V((T, D), f32), V((T, D), bf16), V((8, T), f32), V((16, D), f32)],
        in_specs=[anywhere] * 22,
        out_specs=[vmem] * 5,
        scratch_shapes=[
            V((T,), f32), V((L,), bf16), V((L,), bf16), V((D,), bf16), V((D,), bf16), V((D,), bf16), V((F,), bf16),
            V((D,), bf16), V((D,), bf16), V((D,), bf16), V((D,), bf16), V((1,), bf16), V((1, T), jnp.int32), V((1, T), jnp.int32),
            V((16, D), f32), V((1, F), f32),
            V((T, D), bf16), V((D, L), bf16), V((D, L), bf16), V((D, L), bf16), V((L, D), bf16), V((L, D), bf16),
            V((D, F), bf16), V((F, D), bf16),
            V((T, L), bf16), V((T, L), bf16), V((L, T), bf16), V((L, T), bf16),
            V((2 * T, L), bf16), V((2 * L, T), bf16), V((L // 128, T, 2 * T), bf16), V((L, T), bf16),
            V((T, D), f32), V((T, 128), f32), V((T, D), f32), V((T, D), bf16),
            V((T, F), bf16), V((T, F), bf16), V((T, D), f32), V((T, D), f32), V((T, D), f32),
            V((T, D), bf16), V((T, F), bf16),
            V((2 * T, L), bf16), V((2 * L, T), bf16), V((L, T), bf16),
            V((T, 8), f32), V((T, 8), f32),
            V((4, 16, D), f32), V((4, 16, D), f32),
            V((BATCHES, sub // 2, D), f32), V((BATCHES, RING - 1, sub // 2 // RING, D), f32),
            dma((22,)), dma((14,)), dma((17,)), dma, dma((4,)), dma((4,)), dma((4,)),
            dma((BATCHES,)), dma((BATCHES,)), dma, dma((BATCHES, RING)), dma, dma, pltpu.SemaphoreType.REGULAR((BATCHES,)),
        ],
        compiler_params=pltpu.CompilerParams(
            collective_id=0, has_side_effects=True, vmem_limit_bytes=VMEM_LIMIT
        ),
    )(
        tokens, segment_ids, pad_flags, term_cot, query_bias, value_bias, output_bias, first_gain, first_shift, up_bias,
        down_bias, second_gain, second_shift, term_weight, term_bias, query_weight, key_weight, value_weight,
        output_weight, up_weight, down_weight, hidden_cot,
    )
    vector = [jax.ShapeDtypeStruct((n,), f32) for n in (D, L, F, T, 1)]
    vd, vl, vf, vt, v1 = vector
    dl = jax.ShapeDtypeStruct((D, L), f32)
    outs = pl.pallas_call(
        spread,
        out_shape=[
            jax.ShapeDtypeStruct((T, D), bf16), vt, jax.ShapeDtypeStruct((T, D), f32), dl, vl, dl, dl, vl,
            jax.ShapeDtypeStruct((L, D), f32), vd, vd, vd, jax.ShapeDtypeStruct((D, F), f32), vf,
            jax.ShapeDtypeStruct((F, D), f32), vd, vd, vd, vd, v1,
        ],
        in_specs=[vmem] * 5,
        out_specs=[anywhere] * 20,
        scratch_shapes=[dma((24,)), V((T,), f32), V((L,), f32), V((L,), f32)]
        + [V((D,), f32)] * 7
        + [V((F,), f32), V((1,), f32)],
        compiler_params=pltpu.CompilerParams(vmem_limit_bytes=2**20),
    )(G, hc, hid, term, smt)
    if groups > 1:
        outs = list(outs[:3]) + list(lax.psum(tuple(v * (1.0 / GROUP) for v in outs[3:]), "dp"))
    return tuple(outs)


def solution(mesh):
    rows, cols, vec = P("dp", None), P(None, "mp"), P("mp")
    return jax.shard_map(
        partial(per_device, groups=mesh.shape["dp"] // GROUP),
        mesh=mesh,
        in_specs=(
            rows, rows, rows, cols, vec, cols, cols, vec, P("mp", None), P(), P(), P(), cols, vec, P("mp", None), P(), P(),
            P(), P(), P(), rows, P("dp"),
        ),
        out_specs=(
            rows, P("dp"), rows, cols, vec, cols, cols, vec, P("mp", None), P(), P(), P(), cols, vec, P("mp", None), P(),
            P(), P(), P(), P(),
        ),
        check_vma=False,
    )
```

```python
from functools import partial

import jax
import jax.numpy as jnp
from jax import lax
from jax.experimental import pallas as pl
from jax.experimental.pallas import tpu as pltpu
from jax.sharding import PartitionSpec as P

HEAD_DIM = 64
EPS = 1e-06
GROUP = 16
RING = 8
MESH = pl.DeviceIdType.MESH
DOWN, UP, ATTN = [3] * 4, [4] * 3, [4] * 3
PUMPS = (1, 1, 4, 9, 3, 3, 5, 10)
VMEM_LIMIT = 47 * 2**20
bf16, f32 = jnp.bfloat16, jnp.float32

V_QV, V_OB, V_G1, V_S1, V_DB, V_G2, V_S2, V_TW, V_TB = range(9)
G_QV, G_OB, G_G1, G_S1, G_UB0, G_UB1, G_DB, G_G2, G_S2, G_TW, G_TB = range(11)


def nn(a, b):
    return jnp.dot(a, b, preferred_element_type=f32)


def nt(a, b):
    return lax.dot_general(a, b, (((1,), (1,)), ((), ())), preferred_element_type=f32)


def tn(a, b):
    return lax.dot_general(a, b, (((0,), (0,)), ((), ())), preferred_element_type=f32)


def colsum(v):
    return jnp.sum(v, axis=0, keepdims=True)


def rowmean(v):
    return jnp.mean(v, axis=-1, keepdims=True)


def sub_batches(ff):
    unit = ff // 12
    sizes = [n * unit for n in DOWN + UP + ATTN]
    return [sum(sizes[:b]) for b in range(len(sizes))], sizes


def kernel(
    tokens, i_seg, i_pad, tcot, i_qb, i_vb, i_ob, i_g1, i_s1, i_ub, i_db, i_g2, i_s2, i_tw, i_tb, wq, wk, wv, wo, wu, wd, hcot,
    G, hc, hid, o_term, smt,
    v_tcot, v_qb, v_vb, v_ob, v_g1, v_s1, v_ub, v_db, v_g2, v_s2, v_tw, v_tb, seg, pad, vec, ubv,
    tok_v, wq_v, wk_v, wv_v, wo_v, woo_v, wu_v, wd_v,
    kn, vn, kT, vT, qz, qTz, pm, ctxT, xh, rs, first_v, fl, gp, act, bs, br, fr, db, du,
    dcz, dcTz, dqT, col, trm, sm, smr, S, R,
    ld_sem, y_s, y_r, wo_s, wo_r, sm_s, sm_r, sib_s, sib_r, ring_s, ring_r, fw_s, fw_r, free_sib,
):
    T, D = tokens.shape
    L, F = wq.shape[1], wu.shape[1]
    NP = L // 128
    CH, PC, FB = T // 2, T // 4, 512
    NPC = T // PC
    SUB = L
    starts, sizes = sub_batches(F)

    me, mp = lax.axis_index("dp"), lax.axis_index("mp")
    base, rank = me // GROUP * GROUP, me % GROUP
    core, chip = rank % 2, rank // 2
    x, z = chip % 2, chip // 2
    pos = jnp.where(x == 0, z, RING - 1 - z)
    vp = jnp.where(core == 0, pos, (RING - pos) % RING)

    def at_vp(v):
        p = jnp.where(core == 0, v, (RING - v) % RING)
        c = jnp.where(p < RING // 2, 2 * p, 2 * (RING - 1 - p) + 1)
        return (base + 2 * c + core, mp)

    def at_xz(ax, az):
        return (base + 2 * (2 * az + ax) + core, mp)

    YN = (me, 1 - mp)
    SIB = (base + 2 * chip + 1 - core, mp)
    NXT, PRV = at_vp((vp + 1) % RING), at_vp((vp + RING - 1) % RING)
    XN = at_xz(1 - x, z)
    Z1 = at_xz(x, z // 2 * 2 + 1 - z % 2)
    Z2 = at_xz(x, (z + 2) % 4)

    def rc(src, dst, ss, rr, dev):
        return pltpu.make_async_remote_copy(
            src_ref=src, dst_ref=dst, send_sem=ss, recv_sem=rr, device_id=dev, device_id_type=MESH
        )

    pairs = [
        (wo, wo_v), (tokens, tok_v), (wq, wq_v), (wk, wk_v), (wv, wv_v), (wu, wu_v), (wd, wd_v), (hcot, hc),
        (tcot, v_tcot), (i_qb, v_qb), (i_vb, v_vb), (i_ob, v_ob), (i_g1, v_g1), (i_s1, v_s1), (i_ub, v_ub), (i_db, v_db),
        (i_g2, v_g2), (i_s2, v_s2), (i_tw, v_tw), (i_tb, v_tb), (i_seg, seg), (i_pad, pad),
    ]
    loads = [pltpu.make_async_copy(a, b, ld_sem.at[i]) for i, (a, b) in enumerate(pairs)]
    for c in loads:
        c.start()
    L_WO, L_TOK, L_WQ, L_WK, L_WV, L_WU, L_WD, L_HC, *L_VEC = loads

    peers = (YN, SIB, NXT, PRV, XN, Z1, Z2)
    bar = pltpu.get_barrier_semaphore()
    for d in peers:
        pl.semaphore_signal(bar, inc=1, device_id=d, device_id_type=MESH)
    pl.semaphore_wait(bar, len(peers))

    r_wor = 4 * SUB
    r_wos = r_wor + L
    r_bias = 8 * SUB
    r_cs = r_bias + T
    r_cr = r_cs + L
    SH = L // 8

    def wor(ax, az, ac):
        return G.at[pl.ds(pl.multiple_of(r_wor + ((az * 2 + ax) * 2 + ac) * SH, 16), SH)]

    zp = z % 2
    L_WO.wait()
    G[r_wos : r_wos + SH, :] = wo_v[pl.ds(pl.multiple_of(((zp * 2 + x) * 2 + core) * SH, 16), SH), :].astype(f32)

    def wo_copy(k):
        ax, az = ((x, zp), (x, zp), (x, zp), (1 - x, zp), (x, zp), (1 - x, zp), (x, 1 - zp), (1 - x, 1 - zp))[k]
        place = wor(ax, az, core)
        if k == 0:
            return rc(G.at[pl.ds(r_wos, SH)], place, y_s.at[0], y_r.at[0], YN)
        return rc(place, place, wo_s, wo_r.at[min(k, 4) - 1], (XN, Z1, Z1, SIB, SIB, SIB, SIB)[k - 1])

    wo_copy(0).start()

    for c in L_VEC:
        c.wait()
    vec[V_QV : V_QV + 1, 0:L] = v_qb[...].astype(f32).reshape(1, L)
    vec[V_QV : V_QV + 1, L : 2 * L] = v_vb[...].astype(f32).reshape(1, L)
    vec[V_OB : V_OB + 1, :] = v_ob[...].astype(f32).reshape(1, D)
    vec[V_G1 : V_G1 + 1, :] = v_g1[...].astype(f32).reshape(1, D)
    vec[V_S1 : V_S1 + 1, :] = v_s1[...].astype(f32).reshape(1, D)
    vec[V_DB : V_DB + 1, :] = v_db[...].astype(f32).reshape(1, D)
    vec[V_G2 : V_G2 + 1, :] = v_g2[...].astype(f32).reshape(1, D)
    vec[V_S2 : V_S2 + 1, :] = v_s2[...].astype(f32).reshape(1, D)
    vec[V_TW : V_TW + 1, :] = v_tw[...].astype(f32).reshape(1, D)
    vec[V_TB : V_TB + 1, :] = jnp.broadcast_to(v_tb[...].astype(f32).reshape(1, 1), (1, D))
    ubv[...] = v_ub[...].astype(f32).reshape(1, F)

    L_TOK.wait()
    L_WQ.wait()
    lane = lax.broadcasted_iota(jnp.int32, (T, L), 1)
    odd = (lane // HEAD_DIM) % 2
    qv = (nn(tok_v[...], wq_v[...]) + vec[V_QV : V_QV + 1, 0:L]).astype(bf16).astype(f32) * (HEAD_DIM**-0.5)
    for par in range(2):
        one = jnp.where(odd == par, qv, 0.0).astype(bf16)
        qz[par * T : (par + 1) * T, :] = one
        qTz[par * L : (par + 1) * L, :] = one.T
    L_WK.wait()
    kv = nn(tok_v[...], wk_v[...]).astype(bf16)
    kn[...] = kv
    kT[...] = kv.T
    L_WV.wait()
    vv = (nn(tok_v[...], wv_v[...]) + vec[V_QV : V_QV + 1, L : 2 * L]).astype(bf16)
    vn[...] = vv
    vT[...] = vv.T

    segf, padf = seg[...].astype(f32), pad[...].astype(f32)
    rows8 = jnp.concatenate([segf, padf, v_tcot[...].reshape(1, T), jnp.zeros((5, T), f32)], axis=0)
    col[...] = rows8.T
    for qc in range(T // CH):
        ki = lax.broadcasted_iota(jnp.int32, (T, CH), 0)
        qi = lax.broadcasted_iota(jnp.int32, (T, CH), 1) + qc * CH
        same = col[:, 0:1] == segf[:, qc * CH : (qc + 1) * CH]
        allowed = same & ((col[:, 1:2] == 0.0) | (ki == qi))
        G[r_bias : r_bias + T, qc * CH : (qc + 1) * CH] = jnp.where(allowed, 0.0, -1e9)

    Y_CTX, Y_BR, Y_FP, Y_TP = 1, 1 + NPC, 1 + 2 * NPC, 1 + 3 * NPC

    def span(i):
        return pl.ds(pl.multiple_of(i * PC, PC), PC)

    def ctx_copy(i):
        return rc(G.at[pl.ds(r_cs, L), span(i)], G.at[pl.ds(r_cr, L), span(i)], y_s.at[1], y_r.at[Y_CTX + i], YN)

    def attend(i):
        def body(hp, _):
            blk = pl.ds(pl.multiple_of(hp * 128, 128), 128)
            for par in range(2):
                qrows = pl.ds(pl.multiple_of(par * L + hp * 128, 128), 128)
                head = pl.multiple_of(hp * 128 + par * HEAD_DIM, HEAD_DIM)
                s = nn(kn[:, blk], qTz[qrows, span(i)]) + G[r_bias : r_bias + T, span(i)]
                e = jnp.exp(s - jnp.max(s, axis=0, keepdims=True))
                p = (e * (1.0 / colsum(e))).astype(bf16)
                pm[hp, :, pl.ds(par * T + i * PC, PC)] = p
                c = nn(vT[pl.ds(head, HEAD_DIM), :], p).astype(bf16)
                ctxT[pl.ds(head, HEAD_DIM), span(i)] = c
                G[pl.ds(pl.multiple_of(r_cs + head, HEAD_DIM), HEAD_DIM), span(i)] = c.astype(f32)
            return 0

        lax.fori_loop(0, NP, body, 0)

    for i in range(NPC):
        attend(i)
        ctx_copy(i).start()
        if i == 1:
            wo_copy(0).wait_recv()
            for k in (1, 2, 4):
                wo_copy(k).start()
        if i == 3:
            wo_copy(1).wait_recv()
            for k in (3, 5):
                wo_copy(k).start()
    for k in (2, 3):
        wo_copy(k).wait_recv()
        wo_copy(k + 4).start()

    def piece(buf, i):
        return buf.at[span(i)]

    def y_piece(dst, which, i):
        return rc(piece(bs, i), piece(dst, i), y_s.at[which - 3 + i], y_r.at[which + i], YN)

    def y_sent(dst, which):
        for i in range(NPC):
            y_piece(dst, which, i).wait_send()

    L_WU.wait()
    L_WD.wait()
    some = G.at[pl.ds(r_wor, 4 * SH)]
    rc(some, some, wo_s, wo_r.at[3], SIB).wait_recv()
    woo_v[...] = G[r_wor : r_wor + L, :].astype(bf16)

    def forward(i, _):
        rows = span(i)
        ctx_copy(i).wait_recv()
        other = G[r_cr : r_cr + L, rows].astype(bf16)
        res = tok_v[rows, :].astype(f32) + (tn(ctxT[:, rows], wo_v[...]) + tn(other, woo_v[...])) + vec[V_OB : V_OB + 1, :]
        cen = res - rowmean(res)
        rstd = lax.rsqrt(rowmean(cen * cen) + EPS)
        xv = cen * rstd
        xh[rows, :] = xv
        rs[rows, :] = jnp.broadcast_to(rstd, (PC, 128))
        first = xv * vec[V_G1 : V_G1 + 1, :] + vec[V_S1 : V_S1 + 1, :]
        first_v[rows, :] = first
        fl[rows, :] = first.astype(bf16)
        bs[rows, :] = jnp.zeros((PC, D), f32)

        def body(fb, _):
            cols = pl.ds(pl.multiple_of(fb * FB, FB), FB)
            u = nn(fl[rows, :], wu_v[:, cols]) + ubv[:, cols]
            ph = 0.5 + 0.5 * lax.erf(u * 0.7071067811865476)
            a = (u * ph).astype(bf16)
            act[rows, cols] = a
            gp[rows, cols] = (ph + u * (jnp.exp(-0.5 * u * u) * 0.3989422804014327)).astype(bf16)
            bs[rows, :] += nn(a, wd_v[cols, :])
            return 0

        lax.fori_loop(0, F // FB, body, 0)
        y_piece(br, Y_BR, i).start()
        return 0

    lax.fori_loop(0, NPC, forward, 0)
    wo_copy(0).wait_send()
    some = G.at[pl.ds(r_wor, 7 * SH)]
    rc(some, some, wo_s, wo_r.at[3], SIB).wait_send()
    rc(G.at[pl.ds(r_cs, L), pl.ds(0, T)], G.at[pl.ds(r_cr, L), pl.ds(0, T)], y_s.at[1], y_r.at[Y_CTX], YN).wait_send()

    sm[0] = jnp.zeros((16, D), f32)
    L_HC.wait()

    def tail(i):
        rows = span(i)
        y_piece(br, Y_BR, i).wait_recv()
        first = first_v[rows, :]
        res = first + (bs[rows, :] + br[rows, :]) + vec[V_DB : V_DB + 1, :]
        cen = res - rowmean(res)
        rstd = lax.rsqrt(rowmean(cen * cen) + EPS)
        xv = cen * rstd
        g2 = vec[V_G2 : V_G2 + 1, :]
        tw = vec[V_TW : V_TW + 1, :]
        second = xv * g2 + vec[V_S2 : V_S2 + 1, :]
        hid[rows, :] = second.astype(bf16)
        v = jnp.sum(second * tw, axis=-1, keepdims=True) + vec[V_TB : V_TB + 1, 0:1]
        keep = 1.0 - col[rows, 1:2]
        soft = jnp.maximum(v, 0.0) + jnp.log1p(jnp.exp(-jnp.abs(v)))
        trm[rows, :] = jnp.broadcast_to(soft * keep, (PC, 8))
        dterm = col[rows, 2:3] * keep * lax.logistic(v)
        dsec = hc[rows, :] + dterm * tw
        sm[0, G_G2 : G_G2 + 1, :] += colsum(dsec * xv)
        sm[0, G_S2 : G_S2 + 1, :] += colsum(dsec)
        sm[0, G_TW : G_TW + 1, :] += colsum(dterm * second)
        sm[0, G_TB : G_TB + 1, :] += jnp.broadcast_to(colsum(dterm), (1, D))
        dx = dsec * g2
        dr = rstd * (dx - rowmean(dx) - xv * rowmean(dx * xv))
        hc[rows, :] = dr
        low = dr.astype(bf16)
        db[rows, :] = low
        sm[0, G_DB : G_DB + 1, :] += colsum(low.astype(f32))

    def ffn_back(i, between):
        rows = span(i)
        y_piece(br, Y_BR, i).wait_send()
        for fb in range(F // FB):
            cols = pl.ds(fb * FB, FB)
            low = (nt(db[rows, :], wd_v[cols, :]) * gp[rows, cols].astype(f32)).astype(bf16)
            du[rows, cols] = low
            part = nt(low, wu_v[:, cols])
            if fb == 0:
                bs[rows, :] = part
            else:
                bs[rows, :] += part
            between()
        y_piece(fr, Y_FP, i).start()

    def tail_back(i, _):
        tail(i)
        ffn_back(i, lambda: None)
        return 0

    early = (NPC - 1) * PC

    def down_grad(b, part):
        return tn(act[part, b * SUB : (b + 1) * SUB], db[part, :])

    def up_grad(b, part):
        rows, cols = b % 2 * SUB, b // 2 * D
        return tn(fl[part, rows : rows + SUB], du[part, cols : cols + D])

    lax.fori_loop(0, NPC - 1, tail_back, 0)
    for b in range(4):
        G[b * SUB : (b + 1) * SUB, :] = down_grad(b, pl.ds(0, early))
    for b in range(4):
        G[(4 + b) * SUB : (5 + b) * SUB, :] = up_grad(b, pl.ds(0, early))
    tail(NPC - 1)

    def chunk(b, j):
        return pl.ds(pl.multiple_of(starts[b] + core * (sizes[b] // 2) + j * (sizes[b] // 2 // RING), 8), sizes[b] // 2 // RING)

    def own(b, j):
        return S.at[pl.ds(pl.multiple_of(starts[b] // 2 + j * (sizes[b] // 2 // RING), 8), sizes[b] // 2 // RING)]

    def slot(b, k):
        size = sizes[b] // 2 // RING
        return R.at[pl.ds(starts[b] // 2 // RING * (RING - 1) + k * size, size)]

    def mine(b, j):
        return G[chunk(b, j), :] + own(b, j)[...]

    def sib_copy(b):
        half = sizes[b] // 2
        src = G.at[pl.ds(pl.multiple_of(starts[b] + (1 - core) * half, 8), half)]
        return rc(src, S.at[pl.ds(starts[b] // 2, half)], sib_s.at[b], sib_r.at[b], SIB)

    def rs_copy(b, k):
        return rc(own(b, vp) if k == 0 else slot(b, k - 1), slot(b, k), ring_s, ring_r.at[b, k], NXT)

    def ag_copy(b, k, back):
        rows = G.at[chunk(b, (vp + 1 - back - k + RING) % RING)]
        return rc(rows, rows, ring_s, ring_r.at[b, k - 1 if k else RING - 1], NXT)

    def fw_copy(b, k):
        rows = G.at[chunk(b, (vp + 1 - k + RING) % RING)]
        return rc(rows, rows, fw_s, fw_r, SIB)

    def event(b, e):
        if e == 0:
            sib_copy(b).start()
        elif e == 1:
            sib_copy(b).wait_recv()
            own(b, vp)[...] += G[chunk(b, vp), :]
            rs_copy(b, 0).start()
            sib_copy(b).wait_send()
            pl.semaphore_signal(free_sib.at[b], inc=1, device_id=SIB, device_id_type=MESH)
        elif e < RING:
            k = e - 1
            rs_copy(b, k - 1).wait_recv()
            slot(b, k - 1)[...] += mine(b, (vp - k + RING) % RING)
            rs_copy(b, k).start()
        elif e == RING:
            rs_copy(b, RING - 2).wait_recv()
            j = (vp + 1) % RING
            G[chunk(b, j), :] = slot(b, RING - 2)[...] + mine(b, j)
            ag_copy(b, 0, 0).start()
            pl.semaphore_wait(free_sib.at[b], 1)
            fw_copy(b, 0).start()
        else:
            k = e - RING
            ag_copy(b, k - 1, 1).wait_recv()
            if k < RING - 1:
                ag_copy(b, k, 0).start()
            fw_copy(b, k).start()

    def finish():
        sent = G.at[pl.ds(0, 3 * F // RING * (RING - 1))]
        rc(sent, sent, ring_s, ring_r.at[0, 0], NXT).wait_send()
        half = G.at[pl.ds(0, 3 * F // 2)]
        rc(half, half, fw_s, fw_r, SIB).wait()

    queue = []

    begun = [0]

    def complete(rows):
        while begun[0] < len(starts) and starts[begun[0]] + sizes[begun[0]] <= rows:
            event(begun[0], 0)
            queue.append((begun[0], 1))
            begun[0] += 1

    def pump(n):
        for _ in range(n):
            if not queue:
                return
            b, e = queue.pop(0)
            event(b, e)
            if e + 1 < 2 * RING:
                place = len(queue)
                while place > 4 and queue[place - 1][1] > e + 1:
                    place -= 1
                queue.insert(place, (b, e + 1))

    last = pl.ds(early, PC)
    for b in range(4):
        G[b * SUB : (b + 1) * SUB, :] += down_grad(b, last)
        complete((b + 1) * SUB)
    ffn_back(NPC - 1, lambda: pump(PUMPS[0]))
    for b in range(4):
        G[(4 + b) * SUB : (5 + b) * SUB, :] += up_grad(b, last)
        complete((5 + b) * SUB)
        pump(PUMPS[1])
    for h in range(F // D):
        sm[0, G_UB0 + h : G_UB0 + h + 1, :] = colsum(du[:, h * D : (h + 1) * D].astype(f32))

    pump(PUMPS[2])

    def norm_back(i, _):
        rows = span(i)
        y_piece(fr, Y_FP, i).wait_recv()
        dfirst = hc[rows, :] + (bs[rows, :] + fr[rows, :])
        xv = xh[rows, :]
        sm[0, G_G1 : G_G1 + 1, :] += colsum(dfirst * xv)
        sm[0, G_S1 : G_S1 + 1, :] += colsum(dfirst)
        dx = dfirst * vec[V_G1 : V_G1 + 1, :]
        dr = rs[rows, 0:1] * (dx - rowmean(dx) - xv * rowmean(dx * xv))
        hc[rows, :] = dr
        low = dr.astype(bf16)
        db[rows, :] = low
        sm[0, G_OB : G_OB + 1, :] += colsum(low.astype(f32))
        return 0

    for i in range(NPC):
        norm_back(i, 0)
        pump(PUMPS[3] if i < NPC - 1 else 1)

    dc = nt(db[...], wo_v[...])
    for par in range(2):
        one = jnp.where(odd == par, dc, 0.0).astype(bf16)
        dcz[par * T : (par + 1) * T, :] = one
        dcTz[par * L : (par + 1) * L, :] = one.T
    pump(1)

    dsb = act.at[:, pl.ds(0, 2 * T)]
    dq, dk, dv = (gp.at[:, pl.ds(k * L, L)] for k in range(3))

    def attend_back(hp, _):
        blk = pl.ds(pl.multiple_of(hp * 128, 128), 128)
        for par in range(2):
            qrows = pl.ds(pl.multiple_of(par * L + hp * 128, 128), 128)
            head = pl.ds(pl.multiple_of(hp * 128 + par * HEAD_DIM, HEAD_DIM), HEAD_DIM)
            for qc in range(2):
                pcols = pl.ds(par * T + qc * CH, CH)
                dp = nn(vn[:, blk], dcTz[qrows, qc * CH : (qc + 1) * CH])
                p = pm[hp, :, pcols].astype(f32)
                t = dp * p
                dsb[:, pcols] = (t - p * colsum(t)).astype(bf16)
            d = nn(kT[head, :], dsb[:, par * T : (par + 1) * T]) * (HEAD_DIM**-0.5)
            dqT[head, :] = d.astype(bf16)
        dk[:, blk] = nn(dsb[...], qz[:, blk]).astype(bf16)
        dv[:, blk] = nn(pm[hp], dcz[:, blk]).astype(bf16)
        return 0

    for hp in range(NP):
        attend_back(hp, 0)
        pump(PUMPS[4])
    dq[...] = dqT[...].T

    y_sent(fr, Y_FP)
    for qc in range(2):
        rows = pl.ds(qc * CH, CH)
        bs[rows, :] = nt(dq[rows, :], wq_v[...]) + nt(dk[rows, :], wk_v[...]) + nt(dv[rows, :], wv_v[...])
        for i in range(2 * qc, 2 * qc + 2):
            y_piece(br, Y_TP, i).start()
    pump(PUMPS[5])
    G[8 * SUB : 9 * SUB, :] = nn(ctxT[...], db[...])
    complete(9 * SUB)
    for b in range(2):
        half = pl.ds(b * SUB, SUB)
        G[(9 + b) * SUB : (10 + b) * SUB, 0:L] = tn(tok_v[:, half], dq[...])
        G[(9 + b) * SUB : (10 + b) * SUB, L : 2 * L] = tn(tok_v[:, half], dk[...])
        complete((10 + b) * SUB)
        pump(PUMPS[5])
    for b in range(2):
        G[11 * SUB : 12 * SUB, b * L : (b + 1) * L] = tn(tok_v[:, b * SUB : (b + 1) * SUB], dv[...])
    complete(12 * SUB)
    pump(PUMPS[5])

    sm[0, G_QV : G_QV + 1, 0:L] = colsum(dq[...].astype(f32))
    sm[0, G_QV : G_QV + 1, L : 2 * L] = colsum(dv[...].astype(f32))

    def sm_copy(k):
        return rc(sm.at[k], smr.at[k], sm_s.at[k], sm_r.at[k], (SIB, XN, Z1, Z2)[k])

    for k in range(4):
        sm_copy(k).start()
        pump(PUMPS[6])
        sm_copy(k).wait()
        if k < 3:
            sm[k + 1] = sm[k] + smr[k]
        else:
            smt[...] = sm[k] + smr[k]
    o_term[...] = trm[...].T

    for i in range(NPC):
        pump(PUMPS[7])
        rows = pl.ds(i * PC, PC)
        y_piece(br, Y_TP, i).wait_recv()
        hc[rows, :] += bs[rows, :] + br[rows, :]
    pump(len(starts) * 2 * RING)
    finish()
    y_sent(br, Y_TP)


def spread(
    G, hc, hid, term, smt,
    o_hid, o_term, o_tok, o_wq, o_qb, o_wk, o_wv, o_vb, o_wo, o_ob, o_g1, o_s1, o_wu, o_ub, o_wd, o_db, o_g2, o_s2, o_tw,
    o_tb,
    sem, *small,
):
    D, L = o_wq.shape
    F = o_wu.shape[1]

    def g(r, n, c0=0, c1=D):
        return G.at[pl.ds(r, n), pl.ds(c0, c1 - c0)]

    q = 2 * F + L
    copies = [(g(0, F), o_wd)]
    copies += [(g(F + h * D, D), o_wu.at[:, pl.ds(h * D, D)]) for h in range(F // D)]
    copies += [
        (hc, o_tok), (hid, o_hid), (g(2 * F, L), o_wo), (g(q, D, 0, L), o_wq), (g(q, D, L, 2 * L), o_wk),
        (g(q + D, L, 0, L), o_wv.at[pl.ds(0, L)]), (g(q + D, L, L, 2 * L), o_wv.at[pl.ds(L, L)]),
    ]
    started = [pltpu.make_async_copy(a, b, sem.at[i]) for i, (a, b) in enumerate(copies)]
    for c in started:
        c.start()
    rows = [term[0, :], smt[G_QV, 0:L], smt[G_QV, L : 2 * L]]
    rows += [smt[r, :] for r in (G_OB, G_G1, G_S1, G_DB, G_G2, G_S2, G_TW)]
    rows.append(jnp.concatenate([smt[G_UB0 + h : G_UB0 + h + 1, :] for h in range(F // D)], axis=1).reshape(F))
    rows.append(smt[G_TB : G_TB + 1, 0:1].reshape(1))
    places = (o_term, o_qb, o_vb, o_ob, o_g1, o_s1, o_db, o_g2, o_s2, o_tw, o_ub, o_tb)
    for i, (row, held, place) in enumerate(zip(rows, small, places)):
        held[...] = row
        started.append(pltpu.make_async_copy(held, place, sem.at[len(copies) + i]))
        started[-1].start()
    for c in started:
        c.wait()


def per_device(
    tokens, segment_ids, pad_flags, query_weight, query_bias, key_weight, value_weight, value_bias, output_weight,
    output_bias, first_gain, first_shift, up_weight, up_bias, down_weight, down_bias, second_gain, second_shift,
    term_weight, term_bias, hidden_cot, term_cot, *, groups,
):
    T, D = tokens.shape
    L, F = query_weight.shape[1], up_weight.shape[1]
    anywhere, vmem = pl.BlockSpec(memory_space=pl.ANY), pl.BlockSpec(memory_space=pltpu.VMEM)
    NB = len(sub_batches(F)[0])
    dma = pltpu.SemaphoreType.DMA
    V = pltpu.VMEM
    G, hc, hid, term, smt = pl.pallas_call(
        kernel,
        out_shape=[V((3 * F, D), f32), V((T, D), f32), V((T, D), bf16), V((8, T), f32), V((16, D), f32)],
        in_specs=[anywhere] * 22,
        out_specs=[vmem] * 5,
        scratch_shapes=[
            V((T,), f32), V((L,), bf16), V((L,), bf16), V((D,), bf16), V((D,), bf16), V((D,), bf16), V((F,), bf16),
            V((D,), bf16), V((D,), bf16), V((D,), bf16), V((D,), bf16), V((1,), bf16), V((1, T), jnp.int32), V((1, T), jnp.int32),
            V((16, D), f32), V((1, F), f32),
            V((T, D), bf16), V((D, L), bf16), V((D, L), bf16), V((D, L), bf16), V((L, D), bf16), V((L, D), bf16),
            V((D, F), bf16), V((F, D), bf16),
            V((T, L), bf16), V((T, L), bf16), V((L, T), bf16), V((L, T), bf16),
            V((2 * T, L), bf16), V((2 * L, T), bf16), V((L // 128, T, 2 * T), bf16), V((L, T), bf16),
            V((T, D), f32), V((T, 128), f32), V((T, D), f32), V((T, D), bf16),
            V((T, F), bf16), V((T, F), bf16), V((T, D), f32), V((T, D), f32), V((T, D), f32),
            V((T, D), bf16), V((T, F), bf16),
            V((2 * T, L), bf16), V((2 * L, T), bf16), V((L, T), bf16),
            V((T, 8), f32), V((T, 8), f32),
            V((4, 16, D), f32), V((4, 16, D), f32),
            V((3 * F // 2, D), f32), V((3 * F // 2 // RING * (RING - 1), D), f32),
            dma((22,)), dma((14,)), dma((17,)), dma, dma((4,)), dma((4,)), dma((4,)),
            dma((NB,)), dma((NB,)), dma, dma((NB, RING)), dma, dma, pltpu.SemaphoreType.REGULAR((NB,)),
        ],
        compiler_params=pltpu.CompilerParams(
            collective_id=0, has_side_effects=True, vmem_limit_bytes=VMEM_LIMIT
        ),
    )(
        tokens, segment_ids, pad_flags, term_cot, query_bias, value_bias, output_bias, first_gain, first_shift, up_bias,
        down_bias, second_gain, second_shift, term_weight, term_bias, query_weight, key_weight, value_weight,
        output_weight, up_weight, down_weight, hidden_cot,
    )
    vector = [jax.ShapeDtypeStruct((n,), f32) for n in (D, L, F, T, 1)]
    vd, vl, vf, vt, v1 = vector
    dl = jax.ShapeDtypeStruct((D, L), f32)
    outs = pl.pallas_call(
        spread,
        out_shape=[
            jax.ShapeDtypeStruct((T, D), bf16), vt, jax.ShapeDtypeStruct((T, D), f32), dl, vl, dl, dl, vl,
            jax.ShapeDtypeStruct((L, D), f32), vd, vd, vd, jax.ShapeDtypeStruct((D, F), f32), vf,
            jax.ShapeDtypeStruct((F, D), f32), vd, vd, vd, vd, v1,
        ],
        in_specs=[vmem] * 5,
        out_specs=[anywhere] * 20,
        scratch_shapes=[dma((24,)), V((T,), f32), V((L,), f32), V((L,), f32)]
        + [V((D,), f32)] * 7
        + [V((F,), f32), V((1,), f32)],
        compiler_params=pltpu.CompilerParams(vmem_limit_bytes=2**20),
    )(G, hc, hid, term, smt)
    if groups > 1:
        outs = list(outs[:3]) + list(lax.psum(tuple(v * (1.0 / GROUP) for v in outs[3:]), "dp"))
    return tuple(outs)


def solution(mesh):
    rows, cols, vec = P("dp", None), P(None, "mp"), P("mp")
    return jax.shard_map(
        partial(per_device, groups=mesh.shape["dp"] // GROUP),
        mesh=mesh,
        in_specs=(
            rows, rows, rows, cols, vec, cols, cols, vec, P("mp", None), P(), P(), P(), cols, vec, P("mp", None), P(), P(),
            P(), P(), P(), rows, P("dp"),
        ),
        out_specs=(
            rows, P("dp"), rows, cols, vec, cols, cols, vec, P("mp", None), P(), P(), P(), cols, vec, P("mp", None), P(),
            P(), P(), P(), P(),
        ),
        check_vma=False,
    )
```

```python
from functools import partial

import jax
import jax.numpy as jnp
from jax import lax
from jax.experimental import pallas as pl
from jax.experimental.pallas import tpu as pltpu
from jax.sharding import PartitionSpec as P

HEAD_DIM = 64
EPS = 1e-06
GROUP = 16
RING = 8
MESH = pl.DeviceIdType.MESH
DOWN, UP, ATTN = [3] * 4, [4] * 3, [4] * 3
PUMPS = (1, 1, 4, 9, 3, 3, 5, 10)
VMEM_LIMIT = 47 * 2**20
bf16, f32 = jnp.bfloat16, jnp.float32

V_QV, V_OB, V_G1, V_S1, V_DB, V_G2, V_S2, V_TW, V_TB = range(9)
G_QV, G_OB, G_G1, G_S1, G_UB0, G_UB1, G_DB, G_G2, G_S2, G_TW, G_TB = range(11)


def nn(a, b):
    return jnp.dot(a, b, preferred_element_type=f32)


def nt(a, b):
    return lax.dot_general(a, b, (((1,), (1,)), ((), ())), preferred_element_type=f32)


def tn(a, b):
    return lax.dot_general(a, b, (((0,), (0,)), ((), ())), preferred_element_type=f32)


def colsum(v):
    return jnp.sum(v, axis=0, keepdims=True)


def rowmean(v):
    return jnp.mean(v, axis=-1, keepdims=True)


def sub_batches(ff):
    unit = ff // 12
    sizes = [n * unit for n in DOWN + UP + ATTN]
    return [sum(sizes[:b]) for b in range(len(sizes))], sizes


def kernel(
    tokens, i_seg, i_pad, tcot, i_qb, i_vb, i_ob, i_g1, i_s1, i_ub, i_db, i_g2, i_s2, i_tw, i_tb, wq, wk, wv, wo, wu, wd, hcot,
    G, hc, hid, o_term, smt,
    v_tcot, v_qb, v_vb, v_ob, v_g1, v_s1, v_ub, v_db, v_g2, v_s2, v_tw, v_tb, seg, pad, vec, ubv,
    tok_v, wq_v, wk_v, wv_v, wo_v, woo_v, wu_v, wd_v,
    kn, vn, kT, vT, qz, qTz, pm, ctxT, xh, rs, first_v, fl, gp, act, bs, br, fr, db, du,
    dcz, dcTz, dqT, col, trm, sm, smr, S, R,
    ld_sem, y_s, y_r, wo_s, wo_r, sm_s, sm_r, sib_s, sib_r, ring_s, ring_r, fw_s, fw_r, free_sib,
):
    T, D = tokens.shape
    L, F = wq.shape[1], wu.shape[1]
    NP = L // 128
    CH, PC, FB = T // 2, T // 4, 512
    NPC = T // PC
    SUB = L
    starts, sizes = sub_batches(F)

    me, mp = lax.axis_index("dp"), lax.axis_index("mp")
    base, rank = me // GROUP * GROUP, me % GROUP
    core, chip = rank % 2, rank // 2
    x, z = chip % 2, chip // 2
    pos = jnp.where(x == 0, z, RING - 1 - z)
    vp = jnp.where(core == 0, pos, (RING - pos) % RING)

    def at_vp(v):
        p = jnp.where(core == 0, v, (RING - v) % RING)
        c = jnp.where(p < RING // 2, 2 * p, 2 * (RING - 1 - p) + 1)
        return (base + 2 * c + core, mp)

    def at_xz(ax, az):
        return (base + 2 * (2 * az + ax) + core, mp)

    YN = (me, 1 - mp)
    SIB = (base + 2 * chip + 1 - core, mp)
    NXT, PRV = at_vp((vp + 1) % RING), at_vp((vp + RING - 1) % RING)
    XN = at_xz(1 - x, z)
    Z1 = at_xz(x, z // 2 * 2 + 1 - z % 2)
    Z2 = at_xz(x, (z + 2) % 4)

    def rc(src, dst, ss, rr, dev):
        return pltpu.make_async_remote_copy(
            src_ref=src, dst_ref=dst, send_sem=ss, recv_sem=rr, device_id=dev, device_id_type=MESH
        )

    peers = (YN, SIB, NXT, PRV, XN, Z1, Z2)
    bar = pltpu.get_barrier_semaphore()
    for d in peers:
        pl.semaphore_signal(bar, inc=1, device_id=d, device_id_type=MESH)

    pairs = [
        (tokens, tok_v), (wq, wq_v), (wk, wk_v), (wv, wv_v), (wo, wo_v), (tcot, v_tcot), (i_qb, v_qb), (i_vb, v_vb),
        (i_ob, v_ob), (i_g1, v_g1), (i_s1, v_s1), (i_ub, v_ub), (i_db, v_db), (i_g2, v_g2), (i_s2, v_s2), (i_tw, v_tw),
        (i_tb, v_tb), (i_seg, seg), (i_pad, pad), (wu, wu_v), (wd, wd_v), (hcot, hc),
    ]
    loads = [pltpu.make_async_copy(a, b, ld_sem.at[i]) for i, (a, b) in enumerate(pairs)]
    L_TOK, L_WQ, L_WK, L_WV, L_WO, *L_VEC, L_WU, L_WD, L_HC = loads
    for c in loads[:-3]:
        c.start()

    r_wor = 4 * SUB
    r_wos = r_wor + L
    r_bias = 8 * SUB
    r_cs = r_bias + T
    r_cr = r_cs + L
    SH = L // 8

    def wor(ax, az, ac):
        return G.at[pl.ds(pl.multiple_of(r_wor + ((az * 2 + ax) * 2 + ac) * SH, 16), SH)]

    zp = z % 2

    def wo_copy(k):
        ax, az = ((x, zp), (x, zp), (x, zp), (1 - x, zp), (x, zp), (1 - x, zp), (x, 1 - zp), (1 - x, 1 - zp))[k]
        place = wor(ax, az, core)
        if k == 0:
            return rc(G.at[pl.ds(r_wos, SH)], place, y_s.at[0], y_r.at[0], YN)
        return rc(place, place, wo_s, wo_r.at[min(k, 4) - 1], (XN, Z1, Z1, SIB, SIB, SIB, SIB)[k - 1])

    for c in L_VEC:
        c.wait()
    vec[V_QV : V_QV + 1, 0:L] = v_qb[...].astype(f32).reshape(1, L)
    vec[V_QV : V_QV + 1, L : 2 * L] = v_vb[...].astype(f32).reshape(1, L)
    vec[V_OB : V_OB + 1, :] = v_ob[...].astype(f32).reshape(1, D)
    vec[V_G1 : V_G1 + 1, :] = v_g1[...].astype(f32).reshape(1, D)
    vec[V_S1 : V_S1 + 1, :] = v_s1[...].astype(f32).reshape(1, D)
    vec[V_DB : V_DB + 1, :] = v_db[...].astype(f32).reshape(1, D)
    vec[V_G2 : V_G2 + 1, :] = v_g2[...].astype(f32).reshape(1, D)
    vec[V_S2 : V_S2 + 1, :] = v_s2[...].astype(f32).reshape(1, D)
    vec[V_TW : V_TW + 1, :] = v_tw[...].astype(f32).reshape(1, D)
    vec[V_TB : V_TB + 1, :] = jnp.broadcast_to(v_tb[...].astype(f32).reshape(1, 1), (1, D))
    ubv[...] = v_ub[...].astype(f32).reshape(1, F)

    L_TOK.wait()
    L_WQ.wait()
    lane = lax.broadcasted_iota(jnp.int32, (T, L), 1)
    odd = (lane // HEAD_DIM) % 2
    qv = (nn(tok_v[...], wq_v[...]) + vec[V_QV : V_QV + 1, 0:L]).astype(bf16).astype(f32) * (HEAD_DIM**-0.5)
    for par in range(2):
        one = jnp.where(odd == par, qv, 0.0).astype(bf16)
        qz[par * T : (par + 1) * T, :] = one
        qTz[par * L : (par + 1) * L, :] = one.T
    L_WK.wait()
    kv = nn(tok_v[...], wk_v[...]).astype(bf16)
    kn[...] = kv
    kT[...] = kv.T
    L_WV.wait()
    vv = (nn(tok_v[...], wv_v[...]) + vec[V_QV : V_QV + 1, L : 2 * L]).astype(bf16)
    vn[...] = vv
    vT[...] = vv.T

    for c in loads[-3:]:
        c.start()
    L_WO.wait()
    G[r_wos : r_wos + SH, :] = wo_v[pl.ds(pl.multiple_of(((zp * 2 + x) * 2 + core) * SH, 16), SH), :].astype(f32)
    pl.semaphore_wait(bar, len(peers))
    wo_copy(0).start()

    segf, padf = seg[...].astype(f32), pad[...].astype(f32)
    rows8 = jnp.concatenate([segf, padf, v_tcot[...].reshape(1, T), jnp.zeros((5, T), f32)], axis=0)
    col[...] = rows8.T
    for qc in range(T // CH):
        ki = lax.broadcasted_iota(jnp.int32, (T, CH), 0)
        qi = lax.broadcasted_iota(jnp.int32, (T, CH), 1) + qc * CH
        same = col[:, 0:1] == segf[:, qc * CH : (qc + 1) * CH]
        allowed = same & ((col[:, 1:2] == 0.0) | (ki == qi))
        G[r_bias : r_bias + T, qc * CH : (qc + 1) * CH] = jnp.where(allowed, 0.0, -1e9)

    Y_CTX, Y_BR, Y_FP, Y_TP, Y_PART = 1, 1 + NPC, 1 + 2 * NPC, 1 + 3 * NPC, 1 + 4 * NPC

    def span(i):
        return pl.ds(pl.multiple_of(i * PC, PC), PC)

    def ctx_copy(i):
        return rc(G.at[pl.ds(r_cs, L), span(i)], G.at[pl.ds(r_cr, L), span(i)], y_s.at[1], y_r.at[Y_CTX + i], YN)

    def ctx_part(hp):
        rows = [pl.ds(pl.multiple_of(r + hp * 128, 128), 128) for r in (r_cs, r_cr)]
        return rc(G.at[rows[0], span(0)], G.at[rows[1], span(0)], y_s.at[1], y_r.at[Y_PART + hp], YN)

    def attend(i):
        def body(hp, _):
            blk = pl.ds(pl.multiple_of(hp * 128, 128), 128)
            for par in range(2):
                qrows = pl.ds(pl.multiple_of(par * L + hp * 128, 128), 128)
                head = pl.multiple_of(hp * 128 + par * HEAD_DIM, HEAD_DIM)
                s = nn(kn[:, blk], qTz[qrows, span(i)]) + G[r_bias : r_bias + T, span(i)]
                e = jnp.exp(s - jnp.max(s, axis=0, keepdims=True))
                p = (e * (1.0 / colsum(e))).astype(bf16)
                pm[hp, :, pl.ds(par * T + i * PC, PC)] = p
                c = nn(vT[pl.ds(head, HEAD_DIM), :], p).astype(bf16)
                ctxT[pl.ds(head, HEAD_DIM), span(i)] = c
                G[pl.ds(pl.multiple_of(r_cs + head, HEAD_DIM), HEAD_DIM), span(i)] = c.astype(f32)
            if i == 0:
                ctx_part(hp).start()
            return 0

        lax.fori_loop(0, NP, body, 0)

    for i in range(NPC):
        attend(i)
        if i > 0:
            ctx_copy(i).start()
        if i == 1:
            wo_copy(0).wait_recv()
            for k in (1, 2, 4):
                wo_copy(k).start()
        if i == 3:
            wo_copy(1).wait_recv()
            for k in (3, 5):
                wo_copy(k).start()
    for k in (2, 3):
        wo_copy(k).wait_recv()
        wo_copy(k + 4).start()

    def piece(buf, i):
        return buf.at[span(i)]

    def y_piece(dst, which, i):
        return rc(piece(bs, i), piece(dst, i), y_s.at[which - 3 + i], y_r.at[which + i], YN)

    def y_sent(dst, which):
        for i in range(NPC):
            y_piece(dst, which, i).wait_send()

    L_WU.wait()
    L_WD.wait()
    some = G.at[pl.ds(r_wor, 4 * SH)]
    rc(some, some, wo_s, wo_r.at[3], SIB).wait_recv()
    woo_v[...] = G[r_wor : r_wor + L, :].astype(bf16)

    def forward(i, _):
        rows = span(i)

        @pl.when(i == 0)
        def _():
            for hp in range(NP):
                ctx_part(hp).wait_recv()

        @pl.when(i > 0)
        def _():
            ctx_copy(i).wait_recv()

        other = G[r_cr : r_cr + L, rows].astype(bf16)
        res = tok_v[rows, :].astype(f32) + (tn(ctxT[:, rows], wo_v[...]) + tn(other, woo_v[...])) + vec[V_OB : V_OB + 1, :]
        cen = res - rowmean(res)
        rstd = lax.rsqrt(rowmean(cen * cen) + EPS)
        xv = cen * rstd
        xh[rows, :] = xv
        rs[rows, :] = jnp.broadcast_to(rstd, (PC, 128))
        first = xv * vec[V_G1 : V_G1 + 1, :] + vec[V_S1 : V_S1 + 1, :]
        first_v[rows, :] = first
        fl[rows, :] = first.astype(bf16)
        bs[rows, :] = jnp.zeros((PC, D), f32)

        def body(fb, _):
            cols = pl.ds(pl.multiple_of(fb * FB, FB), FB)
            u = nn(fl[rows, :], wu_v[:, cols]) + ubv[:, cols]
            ph = 0.5 + 0.5 * lax.erf(u * 0.7071067811865476)
            a = (u * ph).astype(bf16)
            act[rows, cols] = a
            gp[rows, cols] = (ph + u * (jnp.exp(-0.5 * u * u) * 0.3989422804014327)).astype(bf16)
            bs[rows, :] += nn(a, wd_v[cols, :])
            return 0

        lax.fori_loop(0, F // FB, body, 0)
        y_piece(br, Y_BR, i).start()
        return 0

    lax.fori_loop(0, NPC, forward, 0)
    wo_copy(0).wait_send()
    some = G.at[pl.ds(r_wor, 7 * SH)]
    rc(some, some, wo_s, wo_r.at[3], SIB).wait_send()
    rc(G.at[pl.ds(r_cs, L), pl.ds(0, T)], G.at[pl.ds(r_cr, L), pl.ds(0, T)], y_s.at[1], y_r.at[Y_CTX], YN).wait_send()

    sm[0] = jnp.zeros((16, D), f32)
    L_HC.wait()

    def tail(i):
        rows = span(i)
        y_piece(br, Y_BR, i).wait_recv()
        first = first_v[rows, :]
        res = first + (bs[rows, :] + br[rows, :]) + vec[V_DB : V_DB + 1, :]
        cen = res - rowmean(res)
        rstd = lax.rsqrt(rowmean(cen * cen) + EPS)
        xv = cen * rstd
        g2 = vec[V_G2 : V_G2 + 1, :]
        tw = vec[V_TW : V_TW + 1, :]
        second = xv * g2 + vec[V_S2 : V_S2 + 1, :]
        hid[rows, :] = second.astype(bf16)
        v = jnp.sum(second * tw, axis=-1, keepdims=True) + vec[V_TB : V_TB + 1, 0:1]
        keep = 1.0 - col[rows, 1:2]
        soft = jnp.maximum(v, 0.0) + jnp.log1p(jnp.exp(-jnp.abs(v)))
        trm[rows, :] = jnp.broadcast_to(soft * keep, (PC, 8))
        dterm = col[rows, 2:3] * keep * lax.logistic(v)
        dsec = hc[rows, :] + dterm * tw
        sm[0, G_G2 : G_G2 + 1, :] += colsum(dsec * xv)
        sm[0, G_S2 : G_S2 + 1, :] += colsum(dsec)
        sm[0, G_TW : G_TW + 1, :] += colsum(dterm * second)
        sm[0, G_TB : G_TB + 1, :] += jnp.broadcast_to(colsum(dterm), (1, D))
        dx = dsec * g2
        dr = rstd * (dx - rowmean(dx) - xv * rowmean(dx * xv))
        hc[rows, :] = dr
        low = dr.astype(bf16)
        db[rows, :] = low
        sm[0, G_DB : G_DB + 1, :] += colsum(low.astype(f32))

    def ffn_back(i, between):
        rows = span(i)
        y_piece(br, Y_BR, i).wait_send()
        for fb in range(F // FB):
            cols = pl.ds(fb * FB, FB)
            low = (nt(db[rows, :], wd_v[cols, :]) * gp[rows, cols].astype(f32)).astype(bf16)
            du[rows, cols] = low
            part = nt(low, wu_v[:, cols])
            if fb == 0:
                bs[rows, :] = part
            else:
                bs[rows, :] += part
            between()
        y_piece(fr, Y_FP, i).start()

    def tail_back(i, _):
        tail(i)
        ffn_back(i, lambda: None)
        return 0

    early = (NPC - 1) * PC

    def down_grad(b, part):
        return tn(act[part, b * SUB : (b + 1) * SUB], db[part, :])

    def up_grad(b, part):
        rows, cols = b % 2 * SUB, b // 2 * D
        return tn(fl[part, rows : rows + SUB], du[part, cols : cols + D])

    lax.fori_loop(0, NPC - 1, tail_back, 0)
    for b in range(4):
        G[b * SUB : (b + 1) * SUB, :] = down_grad(b, pl.ds(0, early))
    for b in range(4):
        G[(4 + b) * SUB : (5 + b) * SUB, :] = up_grad(b, pl.ds(0, early))
    tail(NPC - 1)

    def chunk(b, j):
        return pl.ds(pl.multiple_of(starts[b] + core * (sizes[b] // 2) + j * (sizes[b] // 2 // RING), 8), sizes[b] // 2 // RING)

    def own(b, j):
        return S.at[pl.ds(pl.multiple_of(starts[b] // 2 + j * (sizes[b] // 2 // RING), 8), sizes[b] // 2 // RING)]

    def slot(b, k):
        size = sizes[b] // 2 // RING
        return R.at[pl.ds(starts[b] // 2 // RING * (RING - 1) + k * size, size)]

    def mine(b, j):
        return G[chunk(b, j), :] + own(b, j)[...]

    def sib_copy(b):
        half = sizes[b] // 2
        src = G.at[pl.ds(pl.multiple_of(starts[b] + (1 - core) * half, 8), half)]
        return rc(src, S.at[pl.ds(starts[b] // 2, half)], sib_s.at[b], sib_r.at[b], SIB)

    def rs_copy(b, k):
        return rc(own(b, vp) if k == 0 else slot(b, k - 1), slot(b, k), ring_s, ring_r.at[b, k], NXT)

    def ag_copy(b, k, back):
        rows = G.at[chunk(b, (vp + 1 - back - k + RING) % RING)]
        return rc(rows, rows, ring_s, ring_r.at[b, k - 1 if k else RING - 1], NXT)

    def fw_copy(b, k):
        rows = G.at[chunk(b, (vp + 1 - k + RING) % RING)]
        return rc(rows, rows, fw_s, fw_r, SIB)

    def event(b, e):
        if e == 0:
            sib_copy(b).start()
        elif e == 1:
            sib_copy(b).wait_recv()
            own(b, vp)[...] += G[chunk(b, vp), :]
            rs_copy(b, 0).start()
            sib_copy(b).wait_send()
            pl.semaphore_signal(free_sib.at[b], inc=1, device_id=SIB, device_id_type=MESH)
        elif e < RING:
            k = e - 1
            rs_copy(b, k - 1).wait_recv()
            slot(b, k - 1)[...] += mine(b, (vp - k + RING) % RING)
            rs_copy(b, k).start()
        elif e == RING:
            rs_copy(b, RING - 2).wait_recv()
            j = (vp + 1) % RING
            G[chunk(b, j), :] = slot(b, RING - 2)[...] + mine(b, j)
            ag_copy(b, 0, 0).start()
            pl.semaphore_wait(free_sib.at[b], 1)
            fw_copy(b, 0).start()
        else:
            k = e - RING
            ag_copy(b, k - 1, 1).wait_recv()
            if k < RING - 1:
                ag_copy(b, k, 0).start()
            fw_copy(b, k).start()

    def finish():
        sent = G.at[pl.ds(0, 3 * F // RING * (RING - 1))]
        rc(sent, sent, ring_s, ring_r.at[0, 0], NXT).wait_send()
        half = G.at[pl.ds(0, 3 * F // 2)]
        rc(half, half, fw_s, fw_r, SIB).wait()

    queue = []

    begun = [0]

    def complete(rows):
        while begun[0] < len(starts) and starts[begun[0]] + sizes[begun[0]] <= rows:
            event(begun[0], 0)
            queue.append((begun[0], 1))
            begun[0] += 1

    def pump(n):
        for _ in range(n):
            if not queue:
                return
            b, e = queue.pop(0)
            event(b, e)
            if e + 1 < 2 * RING:
                place = len(queue)
                while place > 4 and queue[place - 1][1] > e + 1:
                    place -= 1
                queue.insert(place, (b, e + 1))

    last = pl.ds(early, PC)
    for b in range(4):
        G[b * SUB : (b + 1) * SUB, :] += down_grad(b, last)
        complete((b + 1) * SUB)
    ffn_back(NPC - 1, lambda: pump(PUMPS[0]))
    for b in range(4):
        G[(4 + b) * SUB : (5 + b) * SUB, :] += up_grad(b, last)
        complete((5 + b) * SUB)
        pump(PUMPS[1])
    for h in range(F // D):
        sm[0, G_UB0 + h : G_UB0 + h + 1, :] = colsum(du[:, h * D : (h + 1) * D].astype(f32))

    pump(PUMPS[2])

    def norm_back(i, _):
        rows = span(i)
        y_piece(fr, Y_FP, i).wait_recv()
        dfirst = hc[rows, :] + (bs[rows, :] + fr[rows, :])
        xv = xh[rows, :]
        sm[0, G_G1 : G_G1 + 1, :] += colsum(dfirst * xv)
        sm[0, G_S1 : G_S1 + 1, :] += colsum(dfirst)
        dx = dfirst * vec[V_G1 : V_G1 + 1, :]
        dr = rs[rows, 0:1] * (dx - rowmean(dx) - xv * rowmean(dx * xv))
        hc[rows, :] = dr
        low = dr.astype(bf16)
        db[rows, :] = low
        sm[0, G_OB : G_OB + 1, :] += colsum(low.astype(f32))
        return 0

    for i in range(NPC):
        norm_back(i, 0)
        pump(PUMPS[3] if i < NPC - 1 else 1)

    dc = nt(db[...], wo_v[...])
    for par in range(2):
        one = jnp.where(odd == par, dc, 0.0).astype(bf16)
        dcz[par * T : (par + 1) * T, :] = one
        dcTz[par * L : (par + 1) * L, :] = one.T
    pump(1)

    dsb = act.at[:, pl.ds(0, 2 * T)]
    dq, dk, dv = (gp.at[:, pl.ds(k * L, L)] for k in range(3))

    def attend_back(hp, _):
        blk = pl.ds(pl.multiple_of(hp * 128, 128), 128)
        for par in range(2):
            qrows = pl.ds(pl.multiple_of(par * L + hp * 128, 128), 128)
            head = pl.ds(pl.multiple_of(hp * 128 + par * HEAD_DIM, HEAD_DIM), HEAD_DIM)
            for qc in range(2):
                pcols = pl.ds(par * T + qc * CH, CH)
                dp = nn(vn[:, blk], dcTz[qrows, qc * CH : (qc + 1) * CH])
                p = pm[hp, :, pcols].astype(f32)
                t = dp * p
                dsb[:, pcols] = (t - p * colsum(t)).astype(bf16)
            d = nn(kT[head, :], dsb[:, par * T : (par + 1) * T]) * (HEAD_DIM**-0.5)
            dqT[head, :] = d.astype(bf16)
        dk[:, blk] = nn(dsb[...], qz[:, blk]).astype(bf16)
        dv[:, blk] = nn(pm[hp], dcz[:, blk]).astype(bf16)
        return 0

    for hp in range(NP):
        attend_back(hp, 0)
        pump(PUMPS[4])
    dq[...] = dqT[...].T

    y_sent(fr, Y_FP)
    for qc in range(2):
        rows = pl.ds(qc * CH, CH)
        bs[rows, :] = nt(dq[rows, :], wq_v[...]) + nt(dk[rows, :], wk_v[...]) + nt(dv[rows, :], wv_v[...])
        for i in range(2 * qc, 2 * qc + 2):
            y_piece(br, Y_TP, i).start()
    pump(PUMPS[5])
    G[8 * SUB : 9 * SUB, :] = nn(ctxT[...], db[...])
    complete(9 * SUB)
    for b in range(2):
        half = pl.ds(b * SUB, SUB)
        G[(9 + b) * SUB : (10 + b) * SUB, 0:L] = tn(tok_v[:, half], dq[...])
        G[(9 + b) * SUB : (10 + b) * SUB, L : 2 * L] = tn(tok_v[:, half], dk[...])
        complete((10 + b) * SUB)
        pump(PUMPS[5])
    for b in range(2):
        G[11 * SUB : 12 * SUB, b * L : (b + 1) * L] = tn(tok_v[:, b * SUB : (b + 1) * SUB], dv[...])
    complete(12 * SUB)
    pump(PUMPS[5])

    sm[0, G_QV : G_QV + 1, 0:L] = colsum(dq[...].astype(f32))
    sm[0, G_QV : G_QV + 1, L : 2 * L] = colsum(dv[...].astype(f32))

    mine_sm, other_sm = pl.ds(pl.multiple_of(core * 8, 8), 8), pl.ds(pl.multiple_of((1 - core) * 8, 8), 8)

    def sm_copy(k):
        if k == 0:
            return rc(sm.at[0], smr.at[0], sm_s.at[0], sm_r.at[0], SIB)
        if k == 4:
            return rc(sm.at[4, mine_sm], smr.at[4, mine_sm], sm_s.at[4], sm_r.at[4], SIB)
        return rc(sm.at[k, mine_sm], smr.at[k, mine_sm], sm_s.at[k], sm_r.at[k], (XN, Z1, Z2)[k - 1])

    for k in range(4):
        sm_copy(k).start()
        pump(PUMPS[6])
        sm_copy(k).wait()
        if k == 0:
            sm[1] = sm[0] + smr[0]
        else:
            sm[k + 1, mine_sm] = sm[k, mine_sm] + smr[k, mine_sm]
    sm_copy(4).start()
    smt[mine_sm, :] = sm[4, mine_sm]
    pump(2)
    sm_copy(4).wait()
    smt[other_sm, :] = smr[4, other_sm]
    o_term[...] = trm[...].T

    for i in range(NPC):
        pump(PUMPS[7])
        rows = pl.ds(i * PC, PC)
        y_piece(br, Y_TP, i).wait_recv()
        hc[rows, :] += bs[rows, :] + br[rows, :]
    pump(len(starts) * 2 * RING)
    finish()
    y_sent(br, Y_TP)


def spread(
    G, hc, hid, term, smt,
    o_hid, o_term, o_tok, o_wq, o_qb, o_wk, o_wv, o_vb, o_wo, o_ob, o_g1, o_s1, o_wu, o_ub, o_wd, o_db, o_g2, o_s2, o_tw,
    o_tb,
    sem, *small,
):
    D, L = o_wq.shape
    F = o_wu.shape[1]

    def g(r, n, c0=0, c1=D):
        return G.at[pl.ds(r, n), pl.ds(c0, c1 - c0)]

    q = 2 * F + L
    copies = [(g(0, F), o_wd)]
    copies += [(g(F + h * D, D), o_wu.at[:, pl.ds(h * D, D)]) for h in range(F // D)]
    copies += [
        (hc, o_tok), (hid, o_hid), (g(2 * F, L), o_wo), (g(q, D, 0, L), o_wq), (g(q, D, L, 2 * L), o_wk),
        (g(q + D, L, 0, L), o_wv.at[pl.ds(0, L)]), (g(q + D, L, L, 2 * L), o_wv.at[pl.ds(L, L)]),
    ]
    started = [pltpu.make_async_copy(a, b, sem.at[i]) for i, (a, b) in enumerate(copies)]
    for c in started:
        c.start()
    rows = [term[0, :], smt[G_QV, 0:L], smt[G_QV, L : 2 * L]]
    rows += [smt[r, :] for r in (G_OB, G_G1, G_S1, G_DB, G_G2, G_S2, G_TW)]
    rows.append(jnp.concatenate([smt[G_UB0 + h : G_UB0 + h + 1, :] for h in range(F // D)], axis=1).reshape(F))
    rows.append(smt[G_TB : G_TB + 1, 0:1].reshape(1))
    places = (o_term, o_qb, o_vb, o_ob, o_g1, o_s1, o_db, o_g2, o_s2, o_tw, o_ub, o_tb)
    for i, (row, held, place) in enumerate(zip(rows, small, places)):
        held[...] = row
        started.append(pltpu.make_async_copy(held, place, sem.at[len(copies) + i]))
        started[-1].start()
    for c in started:
        c.wait()


def per_device(
    tokens, segment_ids, pad_flags, query_weight, query_bias, key_weight, value_weight, value_bias, output_weight,
    output_bias, first_gain, first_shift, up_weight, up_bias, down_weight, down_bias, second_gain, second_shift,
    term_weight, term_bias, hidden_cot, term_cot, *, groups,
):
    T, D = tokens.shape
    L, F = query_weight.shape[1], up_weight.shape[1]
    anywhere, vmem = pl.BlockSpec(memory_space=pl.ANY), pl.BlockSpec(memory_space=pltpu.VMEM)
    NB = len(sub_batches(F)[0])
    dma = pltpu.SemaphoreType.DMA
    V = pltpu.VMEM
    G, hc, hid, term, smt = pl.pallas_call(
        kernel,
        out_shape=[V((3 * F, D), f32), V((T, D), f32), V((T, D), bf16), V((8, T), f32), V((16, D), f32)],
        in_specs=[anywhere] * 22,
        out_specs=[vmem] * 5,
        scratch_shapes=[
            V((T,), f32), V((L,), bf16), V((L,), bf16), V((D,), bf16), V((D,), bf16), V((D,), bf16), V((F,), bf16),
            V((D,), bf16), V((D,), bf16), V((D,), bf16), V((D,), bf16), V((1,), bf16), V((1, T), jnp.int32), V((1, T), jnp.int32),
            V((16, D), f32), V((1, F), f32),
            V((T, D), bf16), V((D, L), bf16), V((D, L), bf16), V((D, L), bf16), V((L, D), bf16), V((L, D), bf16),
            V((D, F), bf16), V((F, D), bf16),
            V((T, L), bf16), V((T, L), bf16), V((L, T), bf16), V((L, T), bf16),
            V((2 * T, L), bf16), V((2 * L, T), bf16), V((L // 128, T, 2 * T), bf16), V((L, T), bf16),
            V((T, D), f32), V((T, 128), f32), V((T, D), f32), V((T, D), bf16),
            V((T, F), bf16), V((T, F), bf16), V((T, D), f32), V((T, D), f32), V((T, D), f32),
            V((T, D), bf16), V((T, F), bf16),
            V((2 * T, L), bf16), V((2 * L, T), bf16), V((L, T), bf16),
            V((T, 8), f32), V((T, 8), f32),
            V((5, 16, D), f32), V((5, 16, D), f32),
            V((3 * F // 2, D), f32), V((3 * F // 2 // RING * (RING - 1), D), f32),
            dma((22,)), dma((14,)), dma((17 + L // 128,)), dma, dma((4,)), dma((5,)), dma((5,)),
            dma((NB,)), dma((NB,)), dma, dma((NB, RING)), dma, dma, pltpu.SemaphoreType.REGULAR((NB,)),
        ],
        compiler_params=pltpu.CompilerParams(
            collective_id=0, has_side_effects=True, vmem_limit_bytes=VMEM_LIMIT
        ),
    )(
        tokens, segment_ids, pad_flags, term_cot, query_bias, value_bias, output_bias, first_gain, first_shift, up_bias,
        down_bias, second_gain, second_shift, term_weight, term_bias, query_weight, key_weight, value_weight,
        output_weight, up_weight, down_weight, hidden_cot,
    )
    vector = [jax.ShapeDtypeStruct((n,), f32) for n in (D, L, F, T, 1)]
    vd, vl, vf, vt, v1 = vector
    dl = jax.ShapeDtypeStruct((D, L), f32)
    outs = pl.pallas_call(
        spread,
        out_shape=[
            jax.ShapeDtypeStruct((T, D), bf16), vt, jax.ShapeDtypeStruct((T, D), f32), dl, vl, dl, dl, vl,
            jax.ShapeDtypeStruct((L, D), f32), vd, vd, vd, jax.ShapeDtypeStruct((D, F), f32), vf,
            jax.ShapeDtypeStruct((F, D), f32), vd, vd, vd, vd, v1,
        ],
        in_specs=[vmem] * 5,
        out_specs=[anywhere] * 20,
        scratch_shapes=[dma((24,)), V((T,), f32), V((L,), f32), V((L,), f32)]
        + [V((D,), f32)] * 7
        + [V((F,), f32), V((1,), f32)],
        compiler_params=pltpu.CompilerParams(vmem_limit_bytes=2**20),
    )(G, hc, hid, term, smt)
    if groups > 1:
        outs = list(outs[:3]) + list(lax.psum(tuple(v * (1.0 / GROUP) for v in outs[3:]), "dp"))
    return tuple(outs)


def solution(mesh):
    rows, cols, vec = P("dp", None), P(None, "mp"), P("mp")
    return jax.shard_map(
        partial(per_device, groups=mesh.shape["dp"] // GROUP),
        mesh=mesh,
        in_specs=(
            rows, rows, rows, cols, vec, cols, cols, vec, P("mp", None), P(), P(), P(), cols, vec, P("mp", None), P(), P(),
            P(), P(), P(), rows, P("dp"),
        ),
        out_specs=(
            rows, P("dp"), rows, cols, vec, cols, cols, vec, P("mp", None), P(), P(), P(), cols, vec, P("mp", None), P(),
            P(), P(), P(), P(),
        ),
        check_vma=False,
    )
```

```python
from functools import partial

import jax
import jax.numpy as jnp
from jax import lax
from jax.experimental import pallas as pl
from jax.experimental.pallas import tpu as pltpu
from jax.sharding import PartitionSpec as P

HEAD_DIM = 64
EPS = 1e-06
GROUP = 16
RING = 8
MESH = pl.DeviceIdType.MESH
DOWN, UP, ATTN = [3] * 4, [4] * 3, [4] * 3
PUMPS = (1, 1, 4, 9, 3, 3, 5, 10)
VMEM_LIMIT = 47 * 2**20
bf16, f32 = jnp.bfloat16, jnp.float32

V_QV, V_OB, V_G1, V_S1, V_DB, V_G2, V_S2, V_TW, V_TB = range(9)
G_QV, G_OB, G_G1, G_S1, G_UB0, G_UB1, G_DB, G_G2, G_S2, G_TW, G_TB = range(11)


def nn(a, b):
    return jnp.dot(a, b, preferred_element_type=f32)


def nt(a, b):
    return lax.dot_general(a, b, (((1,), (1,)), ((), ())), preferred_element_type=f32)


def tn(a, b):
    return lax.dot_general(a, b, (((0,), (0,)), ((), ())), preferred_element_type=f32)


def colsum(v):
    return jnp.sum(v, axis=0, keepdims=True)


def rowmean(v):
    return jnp.mean(v, axis=-1, keepdims=True)


def sub_batches(ff):
    unit = ff // 12
    sizes = [n * unit for n in DOWN + UP + ATTN]
    return [sum(sizes[:b]) for b in range(len(sizes))], sizes


def kernel(
    tokens, i_seg, i_pad, tcot, i_qb, i_vb, i_ob, i_g1, i_s1, i_ub, i_db, i_g2, i_s2, i_tw, i_tb, wq, wk, wv, wo, wu, wd, hcot,
    G, hc, hid, o_term, smt,
    v_tcot, v_qb, v_vb, v_ob, v_g1, v_s1, v_ub, v_db, v_g2, v_s2, v_tw, v_tb, seg, pad, vec, ubv,
    tok_v, wq_v, wk_v, wv_v, wo_v, woo_v, wu_v, wd_v,
    kn, vn, kT, vT, qz, qTz, pm, ctxT, xh, rs, first_v, fl, gp, act, bs, br, fr, db, du,
    dcz, dcTz, dqT, col, trm, sm, smr, S, S1, R,
    ld_sem, y_s, y_r, wo_s, wo_r, sm_s, sm_r, sib_s, sib_r, one_s, one_r, ring_s, ring_r, fw_s, fw_r, free_sib,
):
    T, D = tokens.shape
    L, F = wq.shape[1], wu.shape[1]
    NP = L // 128
    CH, PC, FB = T // 2, T // 4, 512
    NPC = T // PC
    SUB = L
    starts, sizes = sub_batches(F)

    me, mp = lax.axis_index("dp"), lax.axis_index("mp")
    base, rank = me // GROUP * GROUP, me % GROUP
    core, chip = rank % 2, rank // 2
    x, z = chip % 2, chip // 2
    pos = jnp.where(x == 0, z, RING - 1 - z)
    vp = jnp.where(core == 0, pos, (RING - pos) % RING)

    def at_vp(v):
        p = jnp.where(core == 0, v, (RING - v) % RING)
        c = jnp.where(p < RING // 2, 2 * p, 2 * (RING - 1 - p) + 1)
        return (base + 2 * c + core, mp)

    def at_xz(ax, az):
        return (base + 2 * (2 * az + ax) + core, mp)

    YN = (me, 1 - mp)
    SIB = (base + 2 * chip + 1 - core, mp)
    NXT, PRV = at_vp((vp + 1) % RING), at_vp((vp + RING - 1) % RING)
    XN = at_xz(1 - x, z)
    Z1 = at_xz(x, z // 2 * 2 + 1 - z % 2)
    Z2 = at_xz(x, (z + 2) % 4)

    def rc(src, dst, ss, rr, dev):
        return pltpu.make_async_remote_copy(
            src_ref=src, dst_ref=dst, send_sem=ss, recv_sem=rr, device_id=dev, device_id_type=MESH
        )

    peers = (YN, SIB, NXT, PRV, XN, Z1, Z2)
    bar = pltpu.get_barrier_semaphore()
    for d in peers:
        pl.semaphore_signal(bar, inc=1, device_id=d, device_id_type=MESH)

    pairs = [
        (tokens, tok_v), (wq, wq_v), (wk, wk_v), (wv, wv_v), (wo, wo_v), (tcot, v_tcot), (i_qb, v_qb), (i_vb, v_vb),
        (i_ob, v_ob), (i_g1, v_g1), (i_s1, v_s1), (i_ub, v_ub), (i_db, v_db), (i_g2, v_g2), (i_s2, v_s2), (i_tw, v_tw),
        (i_tb, v_tb), (i_seg, seg), (i_pad, pad), (wu, wu_v), (wd, wd_v), (hcot, hc),
    ]
    loads = [pltpu.make_async_copy(a, b, ld_sem.at[i]) for i, (a, b) in enumerate(pairs)]
    L_TOK, L_WQ, L_WK, L_WV, L_WO, *L_VEC, L_WU, L_WD, L_HC = loads
    for c in loads[:-3]:
        c.start()

    r_wor = 4 * SUB
    r_wos = r_wor + L
    r_bias = 8 * SUB
    r_cs = r_bias + T
    r_cr = r_cs + L
    SH = L // 8

    def wor(ax, az, ac):
        return G.at[pl.ds(pl.multiple_of(r_wor + ((az * 2 + ax) * 2 + ac) * SH, 16), SH)]

    zp = z % 2

    def wo_copy(k):
        ax, az = ((x, zp), (x, zp), (x, zp), (1 - x, zp), (x, zp), (1 - x, zp), (x, 1 - zp), (1 - x, 1 - zp))[k]
        place = wor(ax, az, core)
        if k == 0:
            return rc(G.at[pl.ds(r_wos, SH)], place, y_s.at[0], y_r.at[0], YN)
        return rc(place, place, wo_s, wo_r.at[min(k, 4) - 1], (XN, Z1, Z1, SIB, SIB, SIB, SIB)[k - 1])

    for c in L_VEC:
        c.wait()
    vec[V_QV : V_QV + 1, 0:L] = v_qb[...].astype(f32).reshape(1, L)
    vec[V_QV : V_QV + 1, L : 2 * L] = v_vb[...].astype(f32).reshape(1, L)
    vec[V_OB : V_OB + 1, :] = v_ob[...].astype(f32).reshape(1, D)
    vec[V_G1 : V_G1 + 1, :] = v_g1[...].astype(f32).reshape(1, D)
    vec[V_S1 : V_S1 + 1, :] = v_s1[...].astype(f32).reshape(1, D)
    vec[V_DB : V_DB + 1, :] = v_db[...].astype(f32).reshape(1, D)
    vec[V_G2 : V_G2 + 1, :] = v_g2[...].astype(f32).reshape(1, D)
    vec[V_S2 : V_S2 + 1, :] = v_s2[...].astype(f32).reshape(1, D)
    vec[V_TW : V_TW + 1, :] = v_tw[...].astype(f32).reshape(1, D)
    vec[V_TB : V_TB + 1, :] = jnp.broadcast_to(v_tb[...].astype(f32).reshape(1, 1), (1, D))
    ubv[...] = v_ub[...].astype(f32).reshape(1, F)

    L_TOK.wait()
    L_WQ.wait()
    lane = lax.broadcasted_iota(jnp.int32, (T, L), 1)
    odd = (lane // HEAD_DIM) % 2
    qv = (nn(tok_v[...], wq_v[...]) + vec[V_QV : V_QV + 1, 0:L]).astype(bf16).astype(f32) * (HEAD_DIM**-0.5)
    for par in range(2):
        one = jnp.where(odd == par, qv, 0.0).astype(bf16)
        qz[par * T : (par + 1) * T, :] = one
        qTz[par * L : (par + 1) * L, :] = one.T
    L_WK.wait()
    kv = nn(tok_v[...], wk_v[...]).astype(bf16)
    kn[...] = kv
    kT[...] = kv.T
    L_WV.wait()
    vv = (nn(tok_v[...], wv_v[...]) + vec[V_QV : V_QV + 1, L : 2 * L]).astype(bf16)
    vn[...] = vv
    vT[...] = vv.T

    for c in loads[-3:]:
        c.start()
    L_WO.wait()
    G[r_wos : r_wos + SH, :] = wo_v[pl.ds(pl.multiple_of(((zp * 2 + x) * 2 + core) * SH, 16), SH), :].astype(f32)
    pl.semaphore_wait(bar, len(peers))
    wo_copy(0).start()

    segf, padf = seg[...].astype(f32), pad[...].astype(f32)
    rows8 = jnp.concatenate([segf, padf, v_tcot[...].reshape(1, T), jnp.zeros((5, T), f32)], axis=0)
    col[...] = rows8.T
    for qc in range(T // CH):
        ki = lax.broadcasted_iota(jnp.int32, (T, CH), 0)
        qi = lax.broadcasted_iota(jnp.int32, (T, CH), 1) + qc * CH
        same = col[:, 0:1] == segf[:, qc * CH : (qc + 1) * CH]
        allowed = same & ((col[:, 1:2] == 0.0) | (ki == qi))
        G[r_bias : r_bias + T, qc * CH : (qc + 1) * CH] = jnp.where(allowed, 0.0, -1e9)

    Y_CTX, Y_BR, Y_FP, Y_TP, Y_PART = 1, 1 + NPC, 1 + 2 * NPC, 1 + 3 * NPC, 1 + 4 * NPC

    def span(i):
        return pl.ds(pl.multiple_of(i * PC, PC), PC)

    def ctx_copy(i):
        return rc(G.at[pl.ds(r_cs, L), span(i)], G.at[pl.ds(r_cr, L), span(i)], y_s.at[1], y_r.at[Y_CTX + i], YN)

    def ctx_part(hp):
        rows = [pl.ds(pl.multiple_of(r + hp * 128, 128), 128) for r in (r_cs, r_cr)]
        return rc(G.at[rows[0], span(0)], G.at[rows[1], span(0)], y_s.at[1], y_r.at[Y_PART + hp], YN)

    def attend(i):
        def body(hp, _):
            blk = pl.ds(pl.multiple_of(hp * 128, 128), 128)
            for par in range(2):
                qrows = pl.ds(pl.multiple_of(par * L + hp * 128, 128), 128)
                head = pl.multiple_of(hp * 128 + par * HEAD_DIM, HEAD_DIM)
                s = nn(kn[:, blk], qTz[qrows, span(i)]) + G[r_bias : r_bias + T, span(i)]
                e = jnp.exp(s - jnp.max(s, axis=0, keepdims=True))
                p = (e * (1.0 / colsum(e))).astype(bf16)
                pm[hp, :, pl.ds(par * T + i * PC, PC)] = p
                c = nn(vT[pl.ds(head, HEAD_DIM), :], p).astype(bf16)
                ctxT[pl.ds(head, HEAD_DIM), span(i)] = c
                G[pl.ds(pl.multiple_of(r_cs + head, HEAD_DIM), HEAD_DIM), span(i)] = c.astype(f32)
            if i == 0:
                ctx_part(hp).start()
            return 0

        lax.fori_loop(0, NP, body, 0)

    for i in range(NPC):
        attend(i)
        if i > 0:
            ctx_copy(i).start()
        if i == 1:
            wo_copy(0).wait_recv()
            for k in (1, 2, 4):
                wo_copy(k).start()
        if i == 3:
            wo_copy(1).wait_recv()
            for k in (3, 5):
                wo_copy(k).start()
    for k in (2, 3):
        wo_copy(k).wait_recv()
        wo_copy(k + 4).start()

    def piece(buf, i):
        return buf.at[span(i)]

    def y_piece(dst, which, i):
        return rc(piece(bs, i), piece(dst, i), y_s.at[which - 3 + i], y_r.at[which + i], YN)

    def y_sent(dst, which):
        for i in range(NPC):
            y_piece(dst, which, i).wait_send()

    L_WU.wait()
    L_WD.wait()
    some = G.at[pl.ds(r_wor, 4 * SH)]
    rc(some, some, wo_s, wo_r.at[3], SIB).wait_recv()
    woo_v[...] = G[r_wor : r_wor + L, :].astype(bf16)

    def forward(i, _):
        rows = span(i)

        @pl.when(i == 0)
        def _():
            for hp in range(NP):
                ctx_part(hp).wait_recv()

        @pl.when(i > 0)
        def _():
            ctx_copy(i).wait_recv()

        other = G[r_cr : r_cr + L, rows].astype(bf16)
        res = tok_v[rows, :].astype(f32) + (tn(ctxT[:, rows], wo_v[...]) + tn(other, woo_v[...])) + vec[V_OB : V_OB + 1, :]
        cen = res - rowmean(res)
        rstd = lax.rsqrt(rowmean(cen * cen) + EPS)
        xv = cen * rstd
        xh[rows, :] = xv
        rs[rows, :] = jnp.broadcast_to(rstd, (PC, 128))
        first = xv * vec[V_G1 : V_G1 + 1, :] + vec[V_S1 : V_S1 + 1, :]
        first_v[rows, :] = first
        fl[rows, :] = first.astype(bf16)
        bs[rows, :] = jnp.zeros((PC, D), f32)

        def body(fb, _):
            cols = pl.ds(pl.multiple_of(fb * FB, FB), FB)
            u = nn(fl[rows, :], wu_v[:, cols]) + ubv[:, cols]
            ph = 0.5 + 0.5 * lax.erf(u * 0.7071067811865476)
            a = (u * ph).astype(bf16)
            act[rows, cols] = a
            gp[rows, cols] = (ph + u * (jnp.exp(-0.5 * u * u) * 0.3989422804014327)).astype(bf16)
            bs[rows, :] += nn(a, wd_v[cols, :])
            return 0

        lax.fori_loop(0, F // FB, body, 0)
        y_piece(br, Y_BR, i).start()
        return 0

    lax.fori_loop(0, NPC, forward, 0)
    wo_copy(0).wait_send()
    some = G.at[pl.ds(r_wor, 7 * SH)]
    rc(some, some, wo_s, wo_r.at[3], SIB).wait_send()
    rc(G.at[pl.ds(r_cs, L), pl.ds(0, T)], G.at[pl.ds(r_cr, L), pl.ds(0, T)], y_s.at[1], y_r.at[Y_CTX], YN).wait_send()

    sm[0] = jnp.zeros((16, D), f32)
    L_HC.wait()

    def tail(i):
        rows = span(i)
        y_piece(br, Y_BR, i).wait_recv()
        first = first_v[rows, :]
        res = first + (bs[rows, :] + br[rows, :]) + vec[V_DB : V_DB + 1, :]
        cen = res - rowmean(res)
        rstd = lax.rsqrt(rowmean(cen * cen) + EPS)
        xv = cen * rstd
        g2 = vec[V_G2 : V_G2 + 1, :]
        tw = vec[V_TW : V_TW + 1, :]
        second = xv * g2 + vec[V_S2 : V_S2 + 1, :]
        hid[rows, :] = second.astype(bf16)
        v = jnp.sum(second * tw, axis=-1, keepdims=True) + vec[V_TB : V_TB + 1, 0:1]
        keep = 1.0 - col[rows, 1:2]
        soft = jnp.maximum(v, 0.0) + jnp.log1p(jnp.exp(-jnp.abs(v)))
        trm[rows, :] = jnp.broadcast_to(soft * keep, (PC, 8))
        dterm = col[rows, 2:3] * keep * lax.logistic(v)
        dsec = hc[rows, :] + dterm * tw
        sm[0, G_G2 : G_G2 + 1, :] += colsum(dsec * xv)
        sm[0, G_S2 : G_S2 + 1, :] += colsum(dsec)
        sm[0, G_TW : G_TW + 1, :] += colsum(dterm * second)
        sm[0, G_TB : G_TB + 1, :] += jnp.broadcast_to(colsum(dterm), (1, D))
        dx = dsec * g2
        dr = rstd * (dx - rowmean(dx) - xv * rowmean(dx * xv))
        hc[rows, :] = dr
        low = dr.astype(bf16)
        db[rows, :] = low
        sm[0, G_DB : G_DB + 1, :] += colsum(low.astype(f32))

    def ffn_back(i, between):
        rows = span(i)
        y_piece(br, Y_BR, i).wait_send()
        for fb in range(F // FB):
            cols = pl.ds(fb * FB, FB)
            low = (nt(db[rows, :], wd_v[cols, :]) * gp[rows, cols].astype(f32)).astype(bf16)
            du[rows, cols] = low
            part = nt(low, wu_v[:, cols])
            if fb == 0:
                bs[rows, :] = part
            else:
                bs[rows, :] += part
            between()
        y_piece(fr, Y_FP, i).start()

    def tail_back(i, _):
        tail(i)
        ffn_back(i, lambda: None)
        return 0

    early = (NPC - 1) * PC

    def down_grad(b, part):
        return tn(act[part, b * SUB : (b + 1) * SUB], db[part, :])

    def up_grad(b, part):
        rows, cols = b % 2 * SUB, b // 2 * D
        return tn(fl[part, rows : rows + SUB], du[part, cols : cols + D])

    lax.fori_loop(0, NPC - 1, tail_back, 0)
    for b in range(4):
        G[b * SUB : (b + 1) * SUB, :] = down_grad(b, pl.ds(0, early))
    for b in range(4):
        G[(4 + b) * SUB : (5 + b) * SUB, :] = up_grad(b, pl.ds(0, early))
    tail(NPC - 1)

    def chunk(b, j):
        return pl.ds(pl.multiple_of(starts[b] + core * (sizes[b] // 2) + j * (sizes[b] // 2 // RING), 8), sizes[b] // 2 // RING)

    def own(b, j):
        return S.at[pl.ds(pl.multiple_of(starts[b] // 2 + j * (sizes[b] // 2 // RING), 8), sizes[b] // 2 // RING)]

    def slot(b, k):
        size = sizes[b] // 2 // RING
        return R.at[pl.ds(starts[b] // 2 // RING * (RING - 1) + k * size, size)]

    def mine(b, j):
        return G[chunk(b, j), :] + own(b, j)[...]

    def sib_copy(b):
        half = sizes[b] // 2
        src = G.at[pl.ds(pl.multiple_of(starts[b] + (1 - core) * half, 8), half)]
        return rc(src, S.at[pl.ds(starts[b] // 2, half)], sib_s.at[b], sib_r.at[b], SIB)

    def one_copy(b):
        size = sizes[b] // 2 // RING
        begin = starts[b] + (1 - core) * (sizes[b] // 2) + (RING - vp) % RING * size
        return rc(G.at[pl.ds(pl.multiple_of(begin, 8), size)], S1.at[b], one_s.at[b], one_r.at[b], SIB)

    def rs_copy(b, k):
        begin = S1.at[b] if b < len(DOWN) else own(b, vp)
        return rc(begin if k == 0 else slot(b, k - 1), slot(b, k), ring_s, ring_r.at[b, k], NXT)

    def ag_copy(b, k, back):
        rows = G.at[chunk(b, (vp + 1 - back - k + RING) % RING)]
        return rc(rows, rows, ring_s, ring_r.at[b, k - 1 if k else RING - 1], NXT)

    def fw_copy(b, k):
        rows = G.at[chunk(b, (vp + 1 - k + RING) % RING)]
        return rc(rows, rows, fw_s, fw_r, SIB)

    def event(b, e):
        early = b < len(DOWN)
        if e == (2 if early else 1):
            sib_copy(b).wait()
            if early:
                one_copy(b).wait_send()
            pl.semaphore_signal(free_sib.at[b], inc=1, device_id=SIB, device_id_type=MESH)
        if e == 0:
            (one_copy if early else sib_copy)(b).start()
        elif e == 1:
            if early:
                one_copy(b).wait_recv()
                S1[b] += G[chunk(b, vp), :]
            else:
                own(b, vp)[...] += G[chunk(b, vp), :]
            rs_copy(b, 0).start()
        elif e < RING:
            k = e - 1
            rs_copy(b, k - 1).wait_recv()
            slot(b, k - 1)[...] += mine(b, (vp - k + RING) % RING)
            rs_copy(b, k).start()
        elif e == RING:
            rs_copy(b, RING - 2).wait_recv()
            j = (vp + 1) % RING
            G[chunk(b, j), :] = slot(b, RING - 2)[...] + mine(b, j)
            ag_copy(b, 0, 0).start()
            pl.semaphore_wait(free_sib.at[b], 1)
            fw_copy(b, 0).start()
        else:
            k = e - RING
            ag_copy(b, k - 1, 1).wait_recv()
            if k < RING - 1:
                ag_copy(b, k, 0).start()
            fw_copy(b, k).start()

    def finish():
        sent = G.at[pl.ds(0, 3 * F // RING * (RING - 1))]
        rc(sent, sent, ring_s, ring_r.at[0, 0], NXT).wait_send()
        half = G.at[pl.ds(0, 3 * F // 2)]
        rc(half, half, fw_s, fw_r, SIB).wait()

    queue = []

    begun = [0]

    def complete(rows):
        while begun[0] < len(starts) and starts[begun[0]] + sizes[begun[0]] <= rows:
            event(begun[0], 0)
            queue.append((begun[0], 1))
            begun[0] += 1

    def pump(n):
        for _ in range(n):
            if not queue:
                return
            b, e = queue.pop(0)
            event(b, e)
            if e + 1 < 2 * RING:
                place = len(queue)
                while place > 4 and queue[place - 1][1] > e + 1:
                    place -= 1
                queue.insert(place, (b, e + 1))

    last = pl.ds(early, PC)
    for b in range(4):
        G[b * SUB : (b + 1) * SUB, :] += down_grad(b, last)
        complete((b + 1) * SUB)
    for b in range(len(DOWN)):
        sib_copy(b).start()
    ffn_back(NPC - 1, lambda: pump(PUMPS[0]))
    for b in range(4):
        G[(4 + b) * SUB : (5 + b) * SUB, :] += up_grad(b, last)
        complete((5 + b) * SUB)
        pump(PUMPS[1])
    for h in range(F // D):
        sm[0, G_UB0 + h : G_UB0 + h + 1, :] = colsum(du[:, h * D : (h + 1) * D].astype(f32))

    pump(PUMPS[2])

    def norm_back(i, _):
        rows = span(i)
        y_piece(fr, Y_FP, i).wait_recv()
        dfirst = hc[rows, :] + (bs[rows, :] + fr[rows, :])
        xv = xh[rows, :]
        sm[0, G_G1 : G_G1 + 1, :] += colsum(dfirst * xv)
        sm[0, G_S1 : G_S1 + 1, :] += colsum(dfirst)
        dx = dfirst * vec[V_G1 : V_G1 + 1, :]
        dr = rs[rows, 0:1] * (dx - rowmean(dx) - xv * rowmean(dx * xv))
        hc[rows, :] = dr
        low = dr.astype(bf16)
        db[rows, :] = low
        sm[0, G_OB : G_OB + 1, :] += colsum(low.astype(f32))
        return 0

    for i in range(NPC):
        norm_back(i, 0)
        pump(PUMPS[3] if i < NPC - 1 else 1)

    dc = nt(db[...], wo_v[...])
    for par in range(2):
        one = jnp.where(odd == par, dc, 0.0).astype(bf16)
        dcz[par * T : (par + 1) * T, :] = one
        dcTz[par * L : (par + 1) * L, :] = one.T
    pump(1)

    dsb = act.at[:, pl.ds(0, 2 * T)]
    dq, dk, dv = (gp.at[:, pl.ds(k * L, L)] for k in range(3))

    def attend_back(hp, _):
        blk = pl.ds(pl.multiple_of(hp * 128, 128), 128)
        for par in range(2):
            qrows = pl.ds(pl.multiple_of(par * L + hp * 128, 128), 128)
            head = pl.ds(pl.multiple_of(hp * 128 + par * HEAD_DIM, HEAD_DIM), HEAD_DIM)
            for qc in range(2):
                pcols = pl.ds(par * T + qc * CH, CH)
                dp = nn(vn[:, blk], dcTz[qrows, qc * CH : (qc + 1) * CH])
                p = pm[hp, :, pcols].astype(f32)
                t = dp * p
                dsb[:, pcols] = (t - p * colsum(t)).astype(bf16)
            d = nn(kT[head, :], dsb[:, par * T : (par + 1) * T]) * (HEAD_DIM**-0.5)
            dqT[head, :] = d.astype(bf16)
        dk[:, blk] = nn(dsb[...], qz[:, blk]).astype(bf16)
        dv[:, blk] = nn(pm[hp], dcz[:, blk]).astype(bf16)
        return 0

    for hp in range(NP):
        attend_back(hp, 0)
        pump(PUMPS[4])
    dq[...] = dqT[...].T

    y_sent(fr, Y_FP)
    for qc in range(2):
        rows = pl.ds(qc * CH, CH)
        bs[rows, :] = nt(dq[rows, :], wq_v[...]) + nt(dk[rows, :], wk_v[...]) + nt(dv[rows, :], wv_v[...])
        for i in range(2 * qc, 2 * qc + 2):
            y_piece(br, Y_TP, i).start()
    pump(PUMPS[5])
    G[8 * SUB : 9 * SUB, :] = nn(ctxT[...], db[...])
    complete(9 * SUB)
    for b in range(2):
        half = pl.ds(b * SUB, SUB)
        G[(9 + b) * SUB : (10 + b) * SUB, 0:L] = tn(tok_v[:, half], dq[...])
        G[(9 + b) * SUB : (10 + b) * SUB, L : 2 * L] = tn(tok_v[:, half], dk[...])
        complete((10 + b) * SUB)
        pump(PUMPS[5])
    for b in range(2):
        G[11 * SUB : 12 * SUB, b * L : (b + 1) * L] = tn(tok_v[:, b * SUB : (b + 1) * SUB], dv[...])
    complete(12 * SUB)
    pump(PUMPS[5])

    sm[0, G_QV : G_QV + 1, 0:L] = colsum(dq[...].astype(f32))
    sm[0, G_QV : G_QV + 1, L : 2 * L] = colsum(dv[...].astype(f32))

    mine_sm, other_sm = pl.ds(pl.multiple_of(core * 8, 8), 8), pl.ds(pl.multiple_of((1 - core) * 8, 8), 8)

    def sm_copy(k):
        if k == 0:
            return rc(sm.at[0], smr.at[0], sm_s.at[0], sm_r.at[0], SIB)
        if k == 4:
            return rc(sm.at[4, mine_sm], smr.at[4, mine_sm], sm_s.at[4], sm_r.at[4], SIB)
        return rc(sm.at[k, mine_sm], smr.at[k, mine_sm], sm_s.at[k], sm_r.at[k], (XN, Z1, Z2)[k - 1])

    for k in range(4):
        sm_copy(k).start()
        pump(PUMPS[6])
        sm_copy(k).wait()
        if k == 0:
            sm[1] = sm[0] + smr[0]
        else:
            sm[k + 1, mine_sm] = sm[k, mine_sm] + smr[k, mine_sm]
    sm_copy(4).start()
    smt[mine_sm, :] = sm[4, mine_sm]
    pump(2)
    sm_copy(4).wait()
    smt[other_sm, :] = smr[4, other_sm]
    o_term[...] = trm[...].T

    for i in range(NPC):
        pump(PUMPS[7])
        rows = pl.ds(i * PC, PC)
        y_piece(br, Y_TP, i).wait_recv()
        hc[rows, :] += bs[rows, :] + br[rows, :]
    pump(len(starts) * 2 * RING)
    finish()
    y_sent(br, Y_TP)


def spread(
    G, hc, hid, term, smt,
    o_hid, o_term, o_tok, o_wq, o_qb, o_wk, o_wv, o_vb, o_wo, o_ob, o_g1, o_s1, o_wu, o_ub, o_wd, o_db, o_g2, o_s2, o_tw,
    o_tb,
    sem, *small,
):
    D, L = o_wq.shape
    F = o_wu.shape[1]

    def g(r, n, c0=0, c1=D):
        return G.at[pl.ds(r, n), pl.ds(c0, c1 - c0)]

    q = 2 * F + L
    copies = [(g(0, F), o_wd)]
    copies += [(g(F + h * D, D), o_wu.at[:, pl.ds(h * D, D)]) for h in range(F // D)]
    copies += [
        (hc, o_tok), (hid, o_hid), (g(2 * F, L), o_wo), (g(q, D, 0, L), o_wq), (g(q, D, L, 2 * L), o_wk),
        (g(q + D, L, 0, L), o_wv.at[pl.ds(0, L)]), (g(q + D, L, L, 2 * L), o_wv.at[pl.ds(L, L)]),
    ]
    started = [pltpu.make_async_copy(a, b, sem.at[i]) for i, (a, b) in enumerate(copies)]
    for c in started:
        c.start()
    rows = [term[0, :], smt[G_QV, 0:L], smt[G_QV, L : 2 * L]]
    rows += [smt[r, :] for r in (G_OB, G_G1, G_S1, G_DB, G_G2, G_S2, G_TW)]
    rows.append(jnp.concatenate([smt[G_UB0 + h : G_UB0 + h + 1, :] for h in range(F // D)], axis=1).reshape(F))
    rows.append(smt[G_TB : G_TB + 1, 0:1].reshape(1))
    places = (o_term, o_qb, o_vb, o_ob, o_g1, o_s1, o_db, o_g2, o_s2, o_tw, o_ub, o_tb)
    for i, (row, held, place) in enumerate(zip(rows, small, places)):
        held[...] = row
        started.append(pltpu.make_async_copy(held, place, sem.at[len(copies) + i]))
        started[-1].start()
    for c in started:
        c.wait()


def per_device(
    tokens, segment_ids, pad_flags, query_weight, query_bias, key_weight, value_weight, value_bias, output_weight,
    output_bias, first_gain, first_shift, up_weight, up_bias, down_weight, down_bias, second_gain, second_shift,
    term_weight, term_bias, hidden_cot, term_cot, *, groups,
):
    T, D = tokens.shape
    L, F = query_weight.shape[1], up_weight.shape[1]
    anywhere, vmem = pl.BlockSpec(memory_space=pl.ANY), pl.BlockSpec(memory_space=pltpu.VMEM)
    NB = len(sub_batches(F)[0])
    dma = pltpu.SemaphoreType.DMA
    V = pltpu.VMEM
    G, hc, hid, term, smt = pl.pallas_call(
        kernel,
        out_shape=[V((3 * F, D), f32), V((T, D), f32), V((T, D), bf16), V((8, T), f32), V((16, D), f32)],
        in_specs=[anywhere] * 22,
        out_specs=[vmem] * 5,
        scratch_shapes=[
            V((T,), f32), V((L,), bf16), V((L,), bf16), V((D,), bf16), V((D,), bf16), V((D,), bf16), V((F,), bf16),
            V((D,), bf16), V((D,), bf16), V((D,), bf16), V((D,), bf16), V((1,), bf16), V((1, T), jnp.int32), V((1, T), jnp.int32),
            V((16, D), f32), V((1, F), f32),
            V((T, D), bf16), V((D, L), bf16), V((D, L), bf16), V((D, L), bf16), V((L, D), bf16), V((L, D), bf16),
            V((D, F), bf16), V((F, D), bf16),
            V((T, L), bf16), V((T, L), bf16), V((L, T), bf16), V((L, T), bf16),
            V((2 * T, L), bf16), V((2 * L, T), bf16), V((L // 128, T, 2 * T), bf16), V((L, T), bf16),
            V((T, D), f32), V((T, 128), f32), V((T, D), f32), V((T, D), bf16),
            V((T, F), bf16), V((T, F), bf16), V((T, D), f32), V((T, D), f32), V((T, D), f32),
            V((T, D), bf16), V((T, F), bf16),
            V((2 * T, L), bf16), V((2 * L, T), bf16), V((L, T), bf16),
            V((T, 8), f32), V((T, 8), f32),
            V((5, 16, D), f32), V((5, 16, D), f32),
            V((3 * F // 2, D), f32), V((len(DOWN), DOWN[0] * F // 12 // 2 // RING, D), f32), V((3 * F // 2 // RING * (RING - 1), D), f32),
            dma((22,)), dma((14,)), dma((17 + L // 128,)), dma, dma((4,)), dma((5,)), dma((5,)),
            dma((NB,)), dma((NB,)), dma((len(DOWN),)), dma((len(DOWN),)), dma, dma((NB, RING)), dma, dma, pltpu.SemaphoreType.REGULAR((NB,)),
        ],
        compiler_params=pltpu.CompilerParams(
            collective_id=0, has_side_effects=True, vmem_limit_bytes=VMEM_LIMIT
        ),
    )(
        tokens, segment_ids, pad_flags, term_cot, query_bias, value_bias, output_bias, first_gain, first_shift, up_bias,
        down_bias, second_gain, second_shift, term_weight, term_bias, query_weight, key_weight, value_weight,
        output_weight, up_weight, down_weight, hidden_cot,
    )
    vector = [jax.ShapeDtypeStruct((n,), f32) for n in (D, L, F, T, 1)]
    vd, vl, vf, vt, v1 = vector
    dl = jax.ShapeDtypeStruct((D, L), f32)
    outs = pl.pallas_call(
        spread,
        out_shape=[
            jax.ShapeDtypeStruct((T, D), bf16), vt, jax.ShapeDtypeStruct((T, D), f32), dl, vl, dl, dl, vl,
            jax.ShapeDtypeStruct((L, D), f32), vd, vd, vd, jax.ShapeDtypeStruct((D, F), f32), vf,
            jax.ShapeDtypeStruct((F, D), f32), vd, vd, vd, vd, v1,
        ],
        in_specs=[vmem] * 5,
        out_specs=[anywhere] * 20,
        scratch_shapes=[dma((24,)), V((T,), f32), V((L,), f32), V((L,), f32)]
        + [V((D,), f32)] * 7
        + [V((F,), f32), V((1,), f32)],
        compiler_params=pltpu.CompilerParams(vmem_limit_bytes=2**20),
    )(G, hc, hid, term, smt)
    if groups > 1:
        outs = list(outs[:3]) + list(lax.psum(tuple(v * (1.0 / GROUP) for v in outs[3:]), "dp"))
    return tuple(outs)


def solution(mesh):
    rows, cols, vec = P("dp", None), P(None, "mp"), P("mp")
    return jax.shard_map(
        partial(per_device, groups=mesh.shape["dp"] // GROUP),
        mesh=mesh,
        in_specs=(
            rows, rows, rows, cols, vec, cols, cols, vec, P("mp", None), P(), P(), P(), cols, vec, P("mp", None), P(), P(),
            P(), P(), P(), rows, P("dp"),
        ),
        out_specs=(
            rows, P("dp"), rows, cols, vec, cols, cols, vec, P("mp", None), P(), P(), P(), cols, vec, P("mp", None), P(),
            P(), P(), P(), P(),
        ),
        check_vma=False,
    )
```
